32 devices in a mesh: pas: 8 (over z, y), head: 4 (over x, core).
Axes of the slice: x: 2, y: 2, z: 4, core: 2. Of those that a mesh axis runs over, the one named last changes fastest.
Arguments:
- queries: bfloat16 [1024, 4096], P('pas', 'head'), may hold values from -144 to 144
- encoded: bfloat16 [8192, 4096], P('pas'), may hold values from -6 to 6
- key_weight: bfloat16 [4096, 4096], P(None, 'head'), may hold values from -0.09375 to 0.09375
- value_weight: bfloat16 [4096, 4096], P(None, 'head'), may hold values from -0.09375 to 0.09375
- out_weight: bfloat16 [4096, 4096], P('head'), may hold values from -0.75 to 0.75
- out_grad: bfloat16 [1024, 4096], P('pas', 'head'), may hold values from -0.75 to 0.75
- slot_of: int32 [32], replicated, may hold values from 0 to 31, as said below
- passage_lists: int32 [8, 16], replicated, may hold values from 0 to 31, as said below
- list_counts: int32 [8], replicated, may hold values from 12 to 16, as said below
Outputs:
- output: bfloat16 [1024, 4096], P('pas', 'head')
- query_grad: bfloat16 [1024, 4096], P('pas', 'head')
- key_grad: bfloat16 [8192, 4096], P('pas', 'head')
- value_grad: bfloat16 [8192, 4096], P('pas', 'head')
The draws below stay inside these ranges and needn't reach their ends.
Inputs may be any that keep to these rules, and one draw needn't show every extreme that they name: slot_of is a permutation of the pool: passage p is stored at slot slot_of[p], on index slot_of[p] // 4 of pas. `passage_lists`: the entries of one row are distinct passage ids. Among the first list_counts[q] entries of row q, at most 2 are stored on one index of pas, and some row has exactly 2 on some index. Entries past list_counts[q] are not read. `list_counts`: some question reads all 16 entries.
All inputs are finite; a program needn't handle non-finite values.
Results may differ from the reference program's by a relative error of at most 0.0055.
The reference program's roundings to bfloat16 on the way (of `pool_keys`, `pool_values`, `context_grad`, `context`, `value_term`, `dscore` and `key_term`) count: a program that leaves them out, or rounds other values in their place, can miss the bound.
Values may be sent and summed in bfloat16 or wider, within the bound.
No kernel may reach another device: no remote copies, remote signals or barrier semaphores. Data moves between devices by JAX's collectives and lax.ppermute only.
A program may use at most 192 MiB of HBM per device.

```python
import jax
import jax.numpy as jnp
from jax import lax

D = 4096
HEADS = 64
HEAD_DIM = 64
QLEN = 128
PLEN = 256
PAS_DEV = 4
MAXP = 16
CAP = 2
QUESTIONS = 8
POOL = 32
POOL_TOK = 8192
QTOK = 1024
N_PAS = 8


def routing(base_key):
    key_perm, key_owner, key_local, key_order, key_count, key_pick = jax.random.split(base_key, 6)
    slot_table = jax.random.permutation(key_perm, POOL).astype(jnp.int32)
    passage_at = jnp.zeros((POOL,), jnp.int32).at[slot_table].set(jnp.arange(POOL, dtype=jnp.int32))

    def pick_owners(item_key):
        return jax.random.permutation(item_key, N_PAS)[:MAXP // CAP].astype(jnp.int32)

    def pick_locals(item_key):
        return jax.random.permutation(item_key, PAS_DEV)[:CAP].astype(jnp.int32)

    def pick_order(item_key):
        return jax.random.permutation(item_key, MAXP).astype(jnp.int32)
    owner_pick = jax.vmap(pick_owners)(jax.random.split(key_owner, QUESTIONS))
    local_pick = jax.vmap(pick_locals)(jax.random.split(key_local, QUESTIONS * (MAXP // CAP)))
    local_pick = local_pick.reshape(QUESTIONS, MAXP // CAP, CAP)
    slot_rows = (owner_pick[:, :, None] * PAS_DEV + local_pick).reshape(QUESTIONS, MAXP)
    list_order = jax.vmap(pick_order)(jax.random.split(key_order, QUESTIONS))
    slot_rows = jnp.take_along_axis(slot_rows, list_order, axis=1)
    listed = passage_at[slot_rows]
    drawn_counts = jax.random.randint(key_count, (QUESTIONS,), MAXP - MAXP // 4, MAXP + 1)
    full_at = jax.random.randint(key_pick, (), 0, QUESTIONS)
    low_at = (full_at + 1 + jax.random.randint(jax.random.fold_in(key_pick, 1), (), 0, QUESTIONS - 1)) % QUESTIONS
    question_ids = jnp.arange(QUESTIONS, dtype=jnp.int32)
    drawn_counts = jnp.where(question_ids == full_at, MAXP, jnp.where(question_ids == low_at, MAXP - MAXP // 4, drawn_counts))
    return (slot_table, listed.astype(jnp.int32), drawn_counts.astype(jnp.int32))


def draw_slot_of(key, part):
    shared = routing(key)
    return shared[0]


def draw_passage_lists(key, part):
    shared = routing(key)
    return shared[1]


def draw_list_counts(key, part):
    shared = routing(key)
    return shared[2]


def draw_queries(key, part):
    key = jax.random.fold_in(key, 11)
    key_base = jax.random.fold_in(key, 0)
    base_values = jnp.clip(jax.random.normal(key_base, (QTOK, D), jnp.float32), -6.0, 6.0)
    drawn = base_values * 1.5
    return drawn.astype(jnp.bfloat16)


def levels(own_key, dims, cuts, low, largest):
    level = 1.0
    for axis_at, parts in cuts:
        draws = jax.random.uniform(jax.random.fold_in(jax.random.fold_in(own_key, 6), axis_at), (parts,), jnp.float32, low / len(cuts), largest / len(cuts))
        level = level * jnp.repeat(jnp.exp(draws), dims[axis_at] // parts).reshape((-1,) + (1,) * (len(dims) - 1 - axis_at))
    return level


def scatter_about(own_key, shape, deviation, reach, shards=(), kind=jnp.bfloat16):
    result = jax.random.normal(own_key, shape, jnp.float32) * deviation
    if len(shards) > 0:
        result = levels(own_key, shape, shards, -0.22, 0.18) * result
    return jnp.clip(result, min=-reach, max=reach).astype(kind)


def setup_inputs(seed: int = 0) -> dict:
    splits = jax.random.split(jax.random.key(seed), 10)
    queries = draw_queries(jax.random.fold_in(splits[9], 71), 0)
    encoded = scatter_about(splits[1], (POOL_TOK, D), 1.0, 6.0, ((0, 8),))
    key_weight = scatter_about(splits[2], (D, D), D ** -0.5, 0.09375, ((1, 4),))
    value_weight = scatter_about(splits[3], (D, D), D ** -0.5, 0.09375, ((1, 4),))
    out_weight = scatter_about(splits[4], (D, D), HEAD_DIM ** -0.5, 0.75, ((0, 4),))
    out_grad = scatter_about(splits[5], (QTOK, D), 0.125, 0.75, ((0, 8), (1, 4)))
    slot_of = draw_slot_of(jax.random.fold_in(splits[9], 71), 0)
    passage_lists = draw_passage_lists(jax.random.fold_in(splits[9], 71), 0)
    list_counts = draw_list_counts(jax.random.fold_in(splits[9], 71), 0)
    return {"queries": queries, "encoded": encoded, "key_weight": key_weight, "value_weight": value_weight, "out_weight": out_weight, "out_grad": out_grad, "slot_of": slot_of, "passage_lists": passage_lists, "list_counts": list_counts}


def rounded(values):
    return lax.optimization_barrier(values.astype(jnp.bfloat16)).astype(jnp.float32)


def reference(queries, encoded, key_weight, value_weight, out_weight, out_grad, slot_of, passage_lists, list_counts):
    score_scale = HEAD_DIM ** -0.5
    pool_keys = jnp.dot(encoded, key_weight, preferred_element_type=jnp.float32).astype(jnp.bfloat16)
    pool_values = jnp.dot(encoded, value_weight, preferred_element_type=jnp.float32).astype(jnp.bfloat16)
    pool_keys = pool_keys.reshape(POOL, PLEN, HEADS, HEAD_DIM)
    pool_values = pool_values.reshape(POOL, PLEN, HEADS, HEAD_DIM)
    context_grad = lax.dot_general(out_grad, out_weight, (((1,), (1,)), ((), ())), preferred_element_type=jnp.float32).astype(jnp.bfloat16)

    def question_step(loop_state, question):
        key_sum, value_sum = loop_state
        chosen = slot_of[passage_lists[question]].astype(jnp.int32)
        is_live = jnp.arange(MAXP, dtype=jnp.int32) < list_counts[question]
        key_valid = jnp.repeat(is_live, PLEN)
        key_block = pool_keys[chosen].reshape(MAXP * PLEN, HEADS, HEAD_DIM).astype(jnp.float32)
        value_block = pool_values[chosen].reshape(MAXP * PLEN, HEADS, HEAD_DIM).astype(jnp.float32)
        first_row = (question * QLEN).astype(jnp.int32)
        query_block = lax.dynamic_slice_in_dim(queries, first_row, QLEN, 0).reshape(QLEN, HEADS, HEAD_DIM).astype(jnp.float32)
        grad_block = lax.dynamic_slice_in_dim(context_grad, first_row, QLEN, 0).reshape(QLEN, HEADS, HEAD_DIM).astype(jnp.float32)
        scores = jnp.einsum("qhd,khd->hqk", query_block, key_block) * score_scale
        scores = jnp.where(key_valid[None, None, :], scores, -1e30)
        row_top = jnp.max(scores, axis=2, keepdims=True)
        weights = jnp.where(key_valid[None, None, :], jnp.exp(scores - row_top), 0.0)
        row_total = jnp.sum(weights, axis=2, keepdims=True)
        value_mix = jnp.einsum("hqk,khd->qhd", rounded(weights), value_block)
        context = (value_mix / jnp.transpose(row_total, (1, 0, 2))).astype(jnp.bfloat16)
        grad_dot = jnp.sum(grad_block * context.astype(jnp.float32), axis=2)
        softmax_rows = weights / row_total
        value_term = jnp.einsum("hqk,qhd->khd", rounded(softmax_rows), grad_block).astype(jnp.bfloat16)
        dprob = jnp.einsum("qhd,khd->hqk", grad_block, value_block)
        dscore = rounded(softmax_rows * (dprob - jnp.transpose(grad_dot)[:, :, None]))
        query_term = (jnp.einsum("hqk,khd->qhd", dscore, key_block) * score_scale).astype(jnp.bfloat16)
        key_term = (jnp.einsum("hqk,qhd->khd", dscore, query_block) * score_scale).astype(jnp.bfloat16)
        key_sum = key_sum.at[chosen].add(key_term.reshape(MAXP, PLEN, HEADS, HEAD_DIM).astype(jnp.float32))
        value_sum = value_sum.at[chosen].add(value_term.reshape(MAXP, PLEN, HEADS, HEAD_DIM).astype(jnp.float32))
        return (key_sum, value_sum), (context.reshape(QLEN, D), query_term.reshape(QLEN, D))

    start_state = (jnp.zeros((POOL, PLEN, HEADS, HEAD_DIM), jnp.float32), jnp.zeros((POOL, PLEN, HEADS, HEAD_DIM), jnp.float32))
    (key_sum, value_sum), (contexts, query_terms) = lax.scan(question_step, start_state, jnp.arange(QUESTIONS, dtype=jnp.int32))
    output = jnp.dot(contexts.reshape(QTOK, D), out_weight, preferred_element_type=jnp.float32).astype(jnp.bfloat16)
    return (output, query_terms.reshape(QTOK, D), key_sum.astype(jnp.bfloat16).reshape(POOL_TOK, D), value_sum.astype(jnp.bfloat16).reshape(POOL_TOK, D))
```

```python
import functools

import jax
import jax.numpy as jnp
from jax import lax
from jax.experimental import pallas as pl
from jax.experimental.pallas import tpu as pltpu
from jax.sharding import PartitionSpec as P

HEAD_DIM = 64
PLEN = 256
INNER = 4
LANES = 128
NEG_LARGE = -1e30
SCALE = HEAD_DIM ** (-0.5)

BF16 = jnp.bfloat16
F32 = jnp.float32

VMEM_LIMIT = 56 * 1024 * 1024


def params(semantics=None):
    return pltpu.CompilerParams(vmem_limit_bytes=VMEM_LIMIT, dimension_semantics=semantics)


def dot_nt(a, b):
    return lax.dot_general(a, b, (((1,), (1,)), ((), ())), preferred_element_type=F32)


def dot_nn(a, b):
    return lax.dot_general(a, b, (((1,), (0,)), ((), ())), preferred_element_type=F32)


def dot_tn(a, b):
    return lax.dot_general(a, b, (((0,), (0,)), ((), ())), preferred_element_type=F32)


def project_kernel(inner, x_ref, w_ref, o_ref, acc):
    step = pl.program_id(0)
    part = dot_nn(x_ref[...], w_ref[...])

    @pl.when(step == 0)
    def _():
        acc[...] = part

    @pl.when(step > 0)
    def _():
        acc[...] += part

    @pl.when(step == pl.num_programs(0) - 1)
    def _():
        width = o_ref.shape[2]
        for block in range(inner):
            o_ref[block] = acc[:, block * width : (block + 1) * width].astype(BF16)


def project(x, w, inner):
    rows, depth = x.shape
    cols = w.shape[1]
    tile = 512
    return pl.pallas_call(
        functools.partial(project_kernel, inner),
        grid=(depth // tile,),
        in_specs=[
            pl.BlockSpec((rows, tile), lambda k: (0, k)),
            pl.BlockSpec((tile, cols), lambda k: (k, 0)),
        ],
        out_specs=pl.BlockSpec((inner, rows, cols // inner), lambda k: (0, 0, 0)),
        out_shape=jax.ShapeDtypeStruct((inner, rows, cols // inner), BF16),
        scratch_shapes=[pltpu.VMEM((rows, cols), F32)],
        compiler_params=params(("arbitrary",)),
        cost_estimate=pl.CostEstimate(
            flops=2 * rows * depth * cols,
            bytes_accessed=2 * (rows * depth + depth * cols + rows * cols),
            transcendentals=0,
        ),
        name="project",
    )(x, w)


def two_heads(block):
    lane = lax.broadcasted_iota(jnp.int32, block.shape, 1)
    zero = jnp.zeros_like(block)
    return jnp.concatenate(
        [jnp.where(lane < HEAD_DIM, block, zero), jnp.where(lane >= HEAD_DIM, block, zero)], axis=0
    )


def own_blocks(full):
    rows = full.shape[1] // 2
    return jnp.concatenate([full[:HEAD_DIM, :rows], full[HEAD_DIM:, rows:]], axis=0)


def each_question(n_outer, inner, n_local, refs, begin, entry, end):
    outer_ref, slot_ref, list_ref, count_ref = refs
    my_outer = outer_ref[0]
    first_slot = my_outer * n_local
    list_len = list_ref.shape[1]

    def question(rel, carry):
        outer = lax.rem(my_outer + lax.div(rel, inner), n_outer)
        ident = outer * inner + lax.rem(rel, inner)
        begin(rel)

        def one(e, inner_carry):
            slot = slot_ref[list_ref[ident, e]] - first_slot

            @pl.when((slot >= 0) & (slot < n_local))
            def _():
                entry(rel, slot)

            return inner_carry

        lax.fori_loop(0, jnp.minimum(count_ref[ident], list_len), one, 0)
        end(rel)
        return carry

    lax.fori_loop(0, n_outer * inner, question, 0)


def pair_lanes(pair):
    return slice(pair * LANES, (pair + 1) * LANES)


def stats_kernel(n_outer, inner, outer_ref, slot_ref, list_ref, count_ref, k_ref, q_ref, o_ref, qbd):
    n_pair = q_ref.shape[2] // LANES
    n_local = k_ref.shape[0]

    def begin(rel):
        for pair in range(n_pair):
            qbd[pair] = two_heads(q_ref[rel, :, pair_lanes(pair)])
        o_ref[0, rel] = jnp.full(o_ref.shape[2:], NEG_LARGE, F32)
        o_ref[1, rel] = jnp.zeros(o_ref.shape[2:], F32)

    def entry(rel, slot):
        for pair in range(n_pair):
            scores = dot_nt(k_ref[slot, :, pair_lanes(pair)], qbd[pair])
            row = slice(pair, pair + 1)
            old = o_ref[0, rel, row, :]
            new = jnp.maximum(old, jnp.max(scores, axis=0, keepdims=True))
            add = jnp.sum(jnp.exp(scores - new), axis=0, keepdims=True)
            o_ref[0, rel, row, :] = new
            o_ref[1, rel, row, :] = o_ref[1, rel, row, :] * jnp.exp(old - new) + add

    each_question(
        n_outer, inner, n_local, (outer_ref, slot_ref, list_ref, count_ref), begin, entry, lambda rel: None
    )


def value_grad_kernel(
    n_outer, inner, outer_ref, slot_ref, list_ref, count_ref, k_ref, q_ref, g_ref, st_ref, o_ref, qbd, gbd, acc
):
    n_pair = q_ref.shape[2] // LANES
    n_local = k_ref.shape[0]
    acc[...] = jnp.zeros_like(acc)

    def begin(rel):
        for pair in range(n_pair):
            qbd[pair] = two_heads(q_ref[rel, :, pair_lanes(pair)])
            gbd[pair] = two_heads(g_ref[rel, :, pair_lanes(pair)])

    def entry(rel, slot):
        for pair in range(n_pair):
            row = slice(pair, pair + 1)
            scores = dot_nt(k_ref[slot, :, pair_lanes(pair)], qbd[pair])
            probs = jnp.exp(scores - st_ref[0, rel, row, :]) * st_ref[1, rel, row, :]
            term = dot_nn(probs.astype(BF16), gbd[pair]).astype(BF16)
            acc[slot, :, pair_lanes(pair)] += term.astype(F32)

    each_question(
        n_outer, inner, n_local, (outer_ref, slot_ref, list_ref, count_ref), begin, entry, lambda rel: None
    )

    def finish(slot, carry):
        o_ref[slot] = acc[slot].astype(BF16)
        return carry

    lax.fori_loop(0, n_local, finish, 0)


def context_kernel(
    n_outer, inner, outer_ref, slot_ref, list_ref, count_ref, k_ref, v_ref, q_ref, st_ref, o_ref, qbd, acc
):
    n_pair = q_ref.shape[2] // LANES
    n_local = k_ref.shape[0]

    def begin(rel):
        for pair in range(n_pair):
            qbd[pair] = two_heads(q_ref[rel, :, pair_lanes(pair)])
        acc[...] = jnp.zeros_like(acc)

    def entry(rel, slot):
        for pair in range(n_pair):
            row = slice(pair, pair + 1)
            scores = dot_nt(k_ref[slot, :, pair_lanes(pair)], qbd[pair])
            weights = jnp.exp(scores - st_ref[0, rel, row, :]).astype(BF16)
            acc[pair] += dot_tn(v_ref[slot, :, pair_lanes(pair)], weights)

    def end(rel):
        for pair in range(n_pair):
            o_ref[rel, pair_lanes(pair), :] = own_blocks(acc[pair])

    each_question(
        n_outer, inner, n_local, (outer_ref, slot_ref, list_ref, count_ref), begin, entry, end
    )


def score_grad_kernel(
    n_outer,
    inner,
    outer_ref,
    slot_ref,
    list_ref,
    count_ref,
    k_ref,
    v_ref,
    q_ref,
    g_ref,
    st_ref,
    dot_ref,
    dk_ref,
    dq_ref,
    qbd,
    gbd,
    acc_k,
    acc_q,
):
    n_pair = q_ref.shape[2] // LANES
    n_local = k_ref.shape[0]
    acc_k[...] = jnp.zeros_like(acc_k)

    def begin(rel):
        for pair in range(n_pair):
            qbd[pair] = two_heads(q_ref[rel, :, pair_lanes(pair)])
            gbd[pair] = two_heads(g_ref[rel, :, pair_lanes(pair)])
        acc_q[...] = jnp.zeros_like(acc_q)

    def entry(rel, slot):
        for pair in range(n_pair):
            row = slice(pair, pair + 1)
            keys = k_ref[slot, :, pair_lanes(pair)]
            scores = dot_nt(keys, qbd[pair])
            probs = jnp.exp(scores - st_ref[0, rel, row, :]) * st_ref[1, rel, row, :]
            dprob = dot_nt(v_ref[slot, :, pair_lanes(pair)], gbd[pair])
            dscore = (probs * (dprob - dot_ref[rel, row, :])).astype(BF16)
            term = dot_nn(dscore, qbd[pair]).astype(BF16)
            acc_k[slot, :, pair_lanes(pair)] += term.astype(F32)
            acc_q[pair] += dot_tn(keys, dscore)

    def end(rel):
        for pair in range(n_pair):
            dq_ref[rel, pair_lanes(pair), :] = own_blocks(acc_q[pair])

    each_question(
        n_outer, inner, n_local, (outer_ref, slot_ref, list_ref, count_ref), begin, entry, end
    )

    def finish(slot, carry):
        dk_ref[slot] = acc_k[slot].astype(BF16)
        return carry

    lax.fori_loop(0, n_local, finish, 0)


def combine_context_kernel(n_parts, *refs):
    parts, (total_ref, g_ref, o_ref, dot_ref) = refs[:n_parts], refs[n_parts:]
    width = g_ref.shape[2]
    for q in range(g_ref.shape[0]):
        mix = parts[0][q]
        for part in parts[1:]:
            mix = mix + part[q]
        grad = jnp.transpose(g_ref[q].astype(F32))
        rows = mix.shape[1]
        pieces = []
        for head in range(width // HEAD_DIM):
            feats = slice(head * HEAD_DIM, (head + 1) * HEAD_DIM)
            pair, lanes = head // 2, slice((head % 2) * rows, (head % 2 + 1) * rows)
            ctx = (mix[feats] / total_ref[q, pair : pair + 1, lanes]).astype(BF16).astype(F32)
            dot_ref[q, pair : pair + 1, lanes] = jnp.sum(grad[feats] * ctx, axis=0, keepdims=True)
            pieces.append(ctx)
        o_ref[q] = jnp.transpose(jnp.concatenate(pieces, axis=0)).astype(BF16)


def combine_query_kernel(n_parts, *refs):
    parts, o_ref = refs[:n_parts], refs[n_parts]
    for q in range(o_ref.shape[0]):
        mix = parts[0][q]
        for part in parts[1:]:
            mix = mix + part[q]
        o_ref[q] = jnp.transpose(mix * SCALE).astype(BF16)


def vmem_call(kernel, scalars, arrays, out_shape, scratch, flops, name, transcendentals=0):
    smem = pl.BlockSpec(memory_space=pltpu.SMEM)
    vmem = pl.BlockSpec(memory_space=pltpu.VMEM)
    size = sum(a.size * a.dtype.itemsize for a in arrays)
    outs = jax.tree.leaves(out_shape)
    size += sum(o.size * o.dtype.itemsize for o in outs)
    return pl.pallas_call(
        kernel,
        in_specs=[smem] * len(scalars) + [vmem] * len(arrays),
        out_specs=jax.tree.map(lambda _: vmem, out_shape),
        out_shape=out_shape,
        scratch_shapes=scratch,
        compiler_params=params(),
        cost_estimate=pl.CostEstimate(
            flops=int(flops), bytes_accessed=int(size), transcendentals=int(transcendentals)
        ),
        name=name,
    )(*scalars, *arrays)


def body(
    queries,
    encoded,
    key_weight,
    value_weight,
    out_weight,
    out_grad,
    slot_of,
    passage_lists,
    list_counts,
):
    head_width = key_weight.shape[1]
    rows = queries.shape[0]
    tok_local = encoded.shape[0]
    pas_dev = tok_local // PLEN
    n_pas = lax.axis_size("pas")
    inner = INNER
    n_outer = n_pas // inner
    width = head_width // inner
    n_pair = width // LANES
    n_local = inner * pas_dev
    n_q = n_pas
    my_outer = (lax.axis_index("pas") // inner).astype(jnp.int32).reshape(1)
    groups = [[o * inner + i for i in range(inner)] for o in range(n_outer)]

    def swap(x):
        return lax.all_to_all(
            x, "pas", split_axis=0, concat_axis=0, tiled=True, axis_index_groups=groups
        )

    def from_outer(x, r):
        return lax.ppermute(
            x,
            "pas",
            [(((o + r) % n_outer) * inner + i, o * inner + i) for o in range(n_outer) for i in range(inner)],
        )

    def to_outer(x, r):
        return lax.ppermute(
            x,
            "pas",
            [(o * inner + i, ((o + r) % n_outer) * inner + i) for o in range(n_outer) for i in range(inner)],
        )

    def by_block(x):
        return jnp.transpose(x.reshape(x.shape[0], inner, width), (1, 0, 2))

    def from_block(x):
        return jnp.transpose(x, (1, 0, 2)).reshape(x.shape[1], head_width)

    def gather_outer(x):
        return jnp.concatenate([x] + [from_outer(x, r) for r in range(1, n_outer)], axis=0)

    scalars = (my_outer, slot_of, passage_lists, list_counts)
    dims = (n_outer, inner)
    unit = 2.0 * n_q * inner * 2 * PLEN * 2 * rows * LANES * n_pair
    exps = n_q * inner * 2 * PLEN * 2 * rows * n_pair

    q_all = gather_outer(swap(by_block(queries * jnp.asarray(SCALE, BF16))))
    key_part = project(encoded, key_weight, inner)
    keys = swap(key_part).reshape(n_local, PLEN, width)
    value_part = project(encoded, value_weight, inner)
    values = swap(value_part).reshape(n_local, PLEN, width)
    context_grad = lax.dot_general(
        lax.all_gather(out_grad, "head", axis=1, tiled=True),
        out_weight,
        (((1,), (1,)), ((), ())),
        preferred_element_type=F32,
    ).astype(BF16)
    g_own = swap(by_block(context_grad))
    g_all = gather_outer(g_own)

    pair_scratch = pltpu.VMEM((n_pair, 2 * rows, LANES), BF16)
    stat_shape = (n_q, n_pair, 2 * rows)
    stats = vmem_call(
        functools.partial(stats_kernel, *dims),
        scalars,
        (keys, q_all),
        jax.ShapeDtypeStruct((2,) + stat_shape, F32),
        [pair_scratch],
        unit,
        "stats",
        exps,
    )
    tops, sums = [stats[0]], [stats[1]]
    for r in range(1, n_outer):
        other = jnp.roll(from_outer(stats, r), r * inner, axis=1)
        tops.append(other[0])
        sums.append(other[1])
    row_top = functools.reduce(jnp.maximum, tops)
    row_total = sum(s * jnp.exp(t - row_top) for s, t in zip(sums, tops))
    norm = jnp.stack([row_top, 1.0 / row_total])

    acc_scratch = pltpu.VMEM((n_local, PLEN, width), F32)
    value_done = vmem_call(
        functools.partial(value_grad_kernel, *dims),
        scalars,
        (keys, q_all, g_all, norm),
        jax.ShapeDtypeStruct((n_local, PLEN, width), BF16),
        [pair_scratch, pair_scratch, acc_scratch],
        2 * unit,
        "value_grad",
        exps,
    )
    value_grad = from_block(swap(value_done.reshape(inner, tok_local, width)))

    mix_scratch = pltpu.VMEM((n_pair, LANES, 2 * rows), F32)
    mix_shape = jax.ShapeDtypeStruct((n_q, width, rows), F32)
    mixes = vmem_call(
        functools.partial(context_kernel, *dims),
        scalars,
        (keys, values, q_all, norm),
        mix_shape,
        [pair_scratch, mix_scratch],
        2 * unit,
        "context",
        exps,
    )

    def parts_of(x):
        return [x[:inner]] + [
            to_outer(x[r * inner : (r + 1) * inner], r) for r in range(1, n_outer)
        ]

    context, grad_dot = vmem_call(
        functools.partial(combine_context_kernel, n_outer),
        (),
        tuple(parts_of(mixes)) + (row_total[:inner], g_own),
        (
            jax.ShapeDtypeStruct((inner, rows, width), BF16),
            jax.ShapeDtypeStruct((inner, n_pair, 2 * rows), F32),
        ),
        [],
        1e6,
        "combine_context",
    )
    dots = gather_outer(grad_dot)
    key_done, query_mix = vmem_call(
        functools.partial(score_grad_kernel, *dims),
        scalars,
        (keys, values, q_all, g_all, norm, dots),
        (jax.ShapeDtypeStruct((n_local, PLEN, width), BF16), mix_shape),
        [pair_scratch, pair_scratch, acc_scratch, mix_scratch],
        4 * unit,
        "score_grad",
        exps,
    )
    query_done = vmem_call(
        functools.partial(combine_query_kernel, n_outer),
        (),
        tuple(parts_of(query_mix)),
        jax.ShapeDtypeStruct((inner, rows, width), BF16),
        [],
        1e6,
        "combine_query",
    )
    query_grad = from_block(swap(query_done))
    key_grad = from_block(swap(key_done.reshape(inner, tok_local, width)))

    context_rows = from_block(swap(context))
    projected = jnp.dot(context_rows, out_weight, preferred_element_type=F32)
    output = lax.psum_scatter(projected, "head", scatter_dimension=1, tiled=True).astype(BF16)
    return (output, query_grad, key_grad, value_grad)


def solution(mesh):
    in_specs = (
        P("pas", "head"),
        P("pas", None),
        P(None, "head"),
        P(None, "head"),
        P("head", None),
        P("pas", "head"),
        P(),
        P(),
        P(),
    )
    out_specs = (P("pas", "head"), P("pas", "head"), P("pas", "head"), P("pas", "head"))
    return jax.shard_map(body, mesh=mesh, in_specs=in_specs, out_specs=out_specs, check_vma=False)
```

```python
import functools

import jax
import jax.numpy as jnp
from jax import lax
from jax.experimental import pallas as pl
from jax.experimental.pallas import tpu as pltpu
from jax.sharding import PartitionSpec as P

HEAD_DIM = 64
PLEN = 256
INNER = 4
GROUP = 4
LANES = 128
NEG_LARGE = -1e30
SCALE = HEAD_DIM ** (-0.5)

BF16 = jnp.bfloat16
F32 = jnp.float32

VMEM_LIMIT = 56 * 1024 * 1024


def params(semantics=None):
    return pltpu.CompilerParams(vmem_limit_bytes=VMEM_LIMIT, dimension_semantics=semantics)


def dot_nt(a, b):
    return lax.dot_general(a, b, (((1,), (1,)), ((), ())), preferred_element_type=F32)


def dot_nn(a, b):
    return lax.dot_general(a, b, (((1,), (0,)), ((), ())), preferred_element_type=F32)


def dot_tn(a, b):
    return lax.dot_general(a, b, (((0,), (0,)), ((), ())), preferred_element_type=F32)


def cost_us(time):
    return pl.CostEstimate(flops=int(time * 1e9), bytes_accessed=0, transcendentals=0)


def project_kernel(x_ref, w_ref, o_ref):
    width = o_ref.shape[2]
    for block in range(INNER):
        cols = slice(block * width, (block + 1) * width)
        o_ref[block] = dot_nn(x_ref[...], w_ref[:, cols]).astype(BF16)


def project(x, w):
    rows, depth = x.shape
    cols = w.shape[1]
    tile = 256
    return pl.pallas_call(
        project_kernel,
        grid=(rows // tile,),
        in_specs=[
            pl.BlockSpec((tile, depth), lambda m: (m, 0)),
            pl.BlockSpec((depth, cols), lambda m: (0, 0)),
        ],
        out_specs=pl.BlockSpec((INNER, tile, cols // INNER), lambda m: (0, m, 0)),
        out_shape=jax.ShapeDtypeStruct((INNER, rows, cols // INNER), BF16),
        compiler_params=params(("arbitrary",)),
        cost_estimate=cost_us(14),
        name="project",
    )(x, w)


def two_heads(block):
    lane = lax.broadcasted_iota(jnp.int32, block.shape, 1)
    zero = jnp.zeros_like(block)
    return jnp.concatenate(
        [jnp.where(lane < HEAD_DIM, block, zero), jnp.where(lane >= HEAD_DIM, block, zero)], axis=0
    )


def own_blocks(full):
    rows = full.shape[1] // 2
    return jnp.concatenate([full[:HEAD_DIM, :rows], full[HEAD_DIM:, rows:]], axis=0)


def route_kernel(n_local, outer_ref, slot_ref, list_ref, count_ref, pick_ref, live_ref):
    n_q, list_len = list_ref.shape
    first_slot = outer_ref[0] * n_local

    def question(ident, carry):
        found = jnp.int32(0)
        for e in range(list_len):
            slot = slot_ref[list_ref[ident, e]] - first_slot
            here = (slot >= 0) & (slot < n_local) & (e < count_ref[ident])
            pick_ref[ident, found] = jnp.where(here, slot, 0)
            found = found + here.astype(jnp.int32)
        for e in range(GROUP):
            pick_ref[ident, found + e] = 0
        live_ref[ident] = found
        return carry

    lax.fori_loop(0, n_q, question, 0)


def each_group(pick_ref, live_ref, ident, entries):
    live = live_ref[ident]

    def group(step, carry):
        first = step * GROUP
        entries([(pick_ref[ident, first + j], first + j < live) for j in range(GROUP)])
        return carry

    lax.fori_loop(0, lax.div(live + (GROUP - 1), GROUP), group, 0)


def pair_lanes(pair):
    return slice(pair * LANES, (pair + 1) * LANES)


def stats_kernel(pick_ref, live_ref, k_ref, q_ref, o_ref, qbd):
    n_q = q_ref.shape[0]
    n_pair = q_ref.shape[2] // LANES

    def question(ident, carry):
        for pair in range(n_pair):
            qbd[pair] = two_heads(q_ref[ident, :, pair_lanes(pair)])
        o_ref[0, ident] = jnp.full(o_ref.shape[2:], NEG_LARGE, F32)
        o_ref[1, ident] = jnp.zeros(o_ref.shape[2:], F32)

        def entries(items):
            for pair in range(n_pair):
                row = slice(pair, pair + 1)
                scores = [dot_nt(k_ref[slot, :, pair_lanes(pair)], qbd[pair]) for slot, _ in items]
                old = o_ref[0, ident, row, :]
                new = old
                for (_, live), part in zip(items, scores):
                    top = jnp.max(part, axis=0, keepdims=True)
                    new = jnp.maximum(new, jnp.where(live, top, NEG_LARGE))
                add = o_ref[1, ident, row, :] * jnp.exp(old - new)
                for (_, live), part in zip(items, scores):
                    shift = jnp.where(live, new, -NEG_LARGE)
                    add = add + jnp.sum(jnp.exp(part - shift), axis=0, keepdims=True)
                o_ref[0, ident, row, :] = new
                o_ref[1, ident, row, :] = add

        each_group(pick_ref, live_ref, ident, entries)
        return carry

    lax.fori_loop(0, n_q, question, 0)


def value_grad_kernel(pick_ref, live_ref, k_ref, q_ref, g_ref, st_ref, o_ref, qbd, gbd, acc):
    n_q = q_ref.shape[0]
    n_pair = q_ref.shape[2] // LANES
    acc[...] = jnp.zeros_like(acc)

    def question(ident, carry):
        for pair in range(n_pair):
            qbd[pair] = two_heads(q_ref[ident, :, pair_lanes(pair)])
            gbd[pair] = two_heads(g_ref[ident, :, pair_lanes(pair)])

        def entries(items):
            for pair in range(n_pair):
                row = slice(pair, pair + 1)
                for slot, live in items:
                    shift = jnp.where(live, st_ref[0, ident, row, :], -NEG_LARGE)
                    scores = dot_nt(k_ref[slot, :, pair_lanes(pair)], qbd[pair])
                    probs = jnp.exp(scores - shift) * st_ref[1, ident, row, :]
                    term = dot_nn(probs.astype(BF16), gbd[pair]).astype(BF16)
                    acc[slot, :, pair_lanes(pair)] += term.astype(F32)

        each_group(pick_ref, live_ref, ident, entries)
        return carry

    lax.fori_loop(0, n_q, question, 0)

    def finish(slot, carry):
        o_ref[slot] = acc[slot].astype(BF16)
        return carry

    lax.fori_loop(0, k_ref.shape[0], finish, 0)


def turn(src_ref, dst_ref):
    def one(slot, carry):
        dst_ref[slot] = jnp.transpose(src_ref[slot])
        return carry

    lax.fori_loop(0, src_ref.shape[0], one, 0)


def context_kernel(n_outer, pick_ref, live_ref, outer_ref, k_ref, v_ref, q_ref, st_ref, *rest):
    o_refs, (qbd, vt) = rest[:n_outer], rest[n_outer:]
    n_q = q_ref.shape[0]
    inner = n_q // n_outer
    n_pair = q_ref.shape[2] // LANES
    turn(v_ref, vt)

    def question(o_ref, outer, index, carry):
        ident = outer * inner + index
        for pair in range(n_pair):
            qbd[pair] = two_heads(q_ref[ident, :, pair_lanes(pair)])
        zero = jnp.zeros((LANES, 2 * q_ref.shape[1]), F32)

        def group(step, sums):
            out = []
            for pair in range(n_pair):
                total = sums[pair]
                row = slice(pair, pair + 1)
                for j in range(GROUP):
                    at = step * GROUP + j
                    slot = pick_ref[ident, at]
                    shift = jnp.where(at < live_ref[ident], st_ref[0, ident, row, :], -NEG_LARGE)
                    scores = dot_nt(k_ref[slot, :, pair_lanes(pair)], qbd[pair])
                    weights = jnp.exp(scores - shift).astype(BF16)
                    total = total + dot_nn(vt[slot, pair_lanes(pair), :], weights)
                out.append(total)
            return tuple(out)

        steps = lax.div(live_ref[ident] + (GROUP - 1), GROUP)
        sums = lax.fori_loop(0, steps, group, (zero,) * n_pair)
        for pair in range(n_pair):
            o_ref[index, pair_lanes(pair), :] = own_blocks(sums[pair])
        return carry

    for r in reversed(range(n_outer)):
        outer = lax.rem(outer_ref[0] + r, n_outer)
        lax.fori_loop(0, inner, functools.partial(question, o_refs[r], outer), 0)


def score_grad_kernel(n_outer, pick_ref, live_ref, outer_ref, k_ref, v_ref, q_ref, g_ref, st_ref, *rest):
    dot_refs, rest = rest[:n_outer], rest[n_outer:]
    dk_ref, rest = rest[0], rest[1:]
    dq_refs, (qbd, gbd, kt, acc_k) = rest[:n_outer], rest[n_outer:]
    n_q = q_ref.shape[0]
    inner = n_q // n_outer
    n_pair = q_ref.shape[2] // LANES
    turn(k_ref, kt)
    acc_k[...] = jnp.zeros_like(acc_k)

    def question(dot_ref, dq_ref, outer, index, carry):
        ident = outer * inner + index
        for pair in range(n_pair):
            qbd[pair] = two_heads(q_ref[ident, :, pair_lanes(pair)])
            gbd[pair] = two_heads(g_ref[ident, :, pair_lanes(pair)])
        zero = jnp.zeros((LANES, 2 * q_ref.shape[1]), F32)

        def group(step, sums):
            out = []
            for pair in range(n_pair):
                total = sums[pair]
                row = slice(pair, pair + 1)
                for j in range(GROUP):
                    at = step * GROUP + j
                    slot = pick_ref[ident, at]
                    shift = jnp.where(at < live_ref[ident], st_ref[0, ident, row, :], -NEG_LARGE)
                    scores = dot_nt(k_ref[slot, :, pair_lanes(pair)], qbd[pair])
                    probs = jnp.exp(scores - shift) * st_ref[1, ident, row, :]
                    dprob = dot_nt(v_ref[slot, :, pair_lanes(pair)], gbd[pair])
                    dscore = (probs * (dprob - dot_ref[index, row, :])).astype(BF16)
                    term = dot_nn(dscore, qbd[pair]).astype(BF16)
                    acc_k[slot, :, pair_lanes(pair)] += term.astype(F32)
                    total = total + dot_nn(kt[slot, pair_lanes(pair), :], dscore)
                out.append(total)
            return tuple(out)

        steps = lax.div(live_ref[ident] + (GROUP - 1), GROUP)
        sums = lax.fori_loop(0, steps, group, (zero,) * n_pair)
        for pair in range(n_pair):
            dq_ref[index, pair_lanes(pair), :] = own_blocks(sums[pair])
        return carry

    for r in reversed(range(n_outer)):
        outer = lax.rem(outer_ref[0] + r, n_outer)
        lax.fori_loop(0, inner, functools.partial(question, dot_refs[r], dq_refs[r], outer), 0)

    def finish(slot, carry):
        dk_ref[slot] = acc_k[slot].astype(BF16)
        return carry

    lax.fori_loop(0, k_ref.shape[0], finish, 0)


def merge_kernel(n_outer, *refs):
    parts, o_ref = refs[:n_outer], refs[n_outer]
    top = parts[0][0]
    for part in parts[1:]:
        top = jnp.maximum(top, part[0])
    total = parts[0][1] * jnp.exp(parts[0][0] - top)
    for part in parts[1:]:
        total = total + part[1] * jnp.exp(part[0] - top)
    o_ref[0] = top
    o_ref[1] = 1.0 / total
    o_ref[2] = total


def combine_context_kernel(n_parts, outer_ref, *refs):
    parts, (st_ref, g_ref, o_ref, dot_ref) = refs[:n_parts], refs[n_parts:]
    width = g_ref.shape[2]
    inner = o_ref.shape[0]
    first = outer_ref[0] * inner
    for q in range(inner):
        mix = parts[0][q]
        for part in parts[1:]:
            mix = mix + part[q]
        grad = jnp.transpose(g_ref[first + q].astype(F32))
        rows = mix.shape[1]
        pieces = []
        for head in range(width // HEAD_DIM):
            feats = slice(head * HEAD_DIM, (head + 1) * HEAD_DIM)
            pair, lanes = head // 2, slice((head % 2) * rows, (head % 2 + 1) * rows)
            total = st_ref[2, first + q, pair : pair + 1, lanes]
            ctx = (mix[feats] / total).astype(BF16).astype(F32)
            dot_ref[q, pair : pair + 1, lanes] = jnp.sum(grad[feats] * ctx, axis=0, keepdims=True)
            pieces.append(ctx)
        o_ref[q] = jnp.transpose(jnp.concatenate(pieces, axis=0)).astype(BF16)


def combine_query_kernel(n_parts, *refs):
    parts, o_ref = refs[:n_parts], refs[n_parts]
    for q in range(o_ref.shape[0]):
        mix = parts[0][q]
        for part in parts[1:]:
            mix = mix + part[q]
        o_ref[q] = jnp.transpose(mix * SCALE).astype(BF16)


def spread_kernel(x_ref, o_ref):
    width = o_ref.shape[2]
    for block in range(INNER):
        part = x_ref[:, block * width : (block + 1) * width] * jnp.asarray(SCALE, BF16)
        for outer in range(o_ref.shape[0] // INNER):
            o_ref[outer * INNER + block] = part


def context_grad_kernel(x_ref, w_ref, o_ref):
    part = dot_nt(x_ref[...], w_ref[...]).astype(BF16)
    for outer in range(o_ref.shape[0]):
        o_ref[outer, 0] = part


def context_grad_blocks(x, w, n_outer, width):
    rows, depth = x.shape
    return pl.pallas_call(
        context_grad_kernel,
        grid=(INNER,),
        in_specs=[
            pl.BlockSpec((rows, depth), lambda j: (0, 0)),
            pl.BlockSpec((width, depth), lambda j: (j, 0)),
        ],
        out_specs=pl.BlockSpec((n_outer, 1, rows, width), lambda j: (0, j, 0, 0)),
        out_shape=jax.ShapeDtypeStruct((n_outer, INNER, rows, width), BF16),
        compiler_params=params(("arbitrary",)),
        cost_estimate=cost_us(5),
        name="context_grad",
    )(x, w)


def out_project_kernel(x_ref, w_ref, o_ref):
    step = pl.program_id(0)
    part = dot_nn(x_ref[0], w_ref[...])

    @pl.when(step == 0)
    def _():
        o_ref[...] = part

    @pl.when(step > 0)
    def _():
        o_ref[...] += part


def out_project(x, w):
    blocks, rows, width = x.shape
    cols = w.shape[1]
    return pl.pallas_call(
        out_project_kernel,
        grid=(blocks,),
        in_specs=[
            pl.BlockSpec((1, rows, width), lambda j: (j, 0, 0)),
            pl.BlockSpec((width, cols), lambda j: (j, 0)),
        ],
        out_specs=pl.BlockSpec((rows, cols), lambda j: (0, 0)),
        out_shape=jax.ShapeDtypeStruct((rows, cols), F32),
        compiler_params=params(("arbitrary",)),
        cost_estimate=cost_us(5),
        name="out_project",
    )(x, w)


def vmem_call(kernel, scalars, arrays, out_shape, scratch, time, name):
    smem = pl.BlockSpec(memory_space=pltpu.SMEM)
    vmem = pl.BlockSpec(memory_space=pltpu.VMEM)
    return pl.pallas_call(
        kernel,
        in_specs=[smem] * len(scalars) + [vmem] * len(arrays),
        out_specs=jax.tree.map(lambda _: vmem, out_shape),
        out_shape=out_shape,
        scratch_shapes=scratch,
        compiler_params=params(),
        cost_estimate=cost_us(time),
        name=name,
    )(*scalars, *arrays)


def route(outer, slot_of, passage_lists, list_counts, n_local):
    smem = pl.BlockSpec(memory_space=pltpu.SMEM)
    n_q, list_len = passage_lists.shape
    return pl.pallas_call(
        functools.partial(route_kernel, n_local),
        in_specs=[smem] * 4,
        out_specs=(smem, smem),
        out_shape=(
            jax.ShapeDtypeStruct((n_q, list_len + GROUP), jnp.int32),
            jax.ShapeDtypeStruct((n_q,), jnp.int32),
        ),
        cost_estimate=cost_us(3),
        name="route",
    )(outer, slot_of, passage_lists, list_counts)


def after(value, *others):
    return lax.optimization_barrier((value,) + others)[0]


def body(
    queries,
    encoded,
    key_weight,
    value_weight,
    out_weight,
    out_grad,
    slot_of,
    passage_lists,
    list_counts,
):
    head_width = key_weight.shape[1]
    rows = queries.shape[0]
    tok_local = encoded.shape[0]
    n_pas = lax.axis_size("pas")
    inner = INNER
    n_outer = n_pas // inner
    width = head_width // inner
    n_pair = width // LANES
    n_local = inner * (tok_local // PLEN)
    n_q = n_pas
    outer = (lax.axis_index("pas") // inner).astype(jnp.int32).reshape(1)
    groups = [[o * inner + i for i in range(inner)] for o in range(n_outer)]
    sds = jax.ShapeDtypeStruct

    def swap(x):
        return lax.all_to_all(
            x, "pas", split_axis=0, concat_axis=0, tiled=True, axis_index_groups=groups
        )

    def swap_all(x):
        return lax.all_to_all(x, "pas", split_axis=0, concat_axis=0, tiled=True)

    def to_outer(x, r):
        return lax.ppermute(
            x,
            "pas",
            [(o * inner + i, ((o + r) % n_outer) * inner + i) for o in range(n_outer) for i in range(inner)],
        )

    def from_block(x):
        return jnp.transpose(x, (1, 0, 2)).reshape(x.shape[1], head_width)

    def partials(parts):
        return [parts[0]] + [to_outer(parts[r], r) for r in range(1, n_outer)]

    q_spread = vmem_call(spread_kernel, (), (queries,), sds((n_q, rows, width), BF16), [], 1.5, "spread")
    q_all = swap_all(q_spread)
    grad_rows = lax.all_gather(out_grad, "head", axis=1, tiled=True)

    key_part = project(after(encoded, q_spread), key_weight)
    keys = swap(key_part).reshape(n_local, PLEN, width)
    value_part = project(after(encoded, key_part), value_weight)
    values = swap(value_part).reshape(n_local, PLEN, width)
    g_spread = context_grad_blocks(after(grad_rows, value_part), out_weight, n_outer, width)
    g_spread = g_spread.reshape(n_q, rows, width)
    g_all = swap_all(g_spread)

    pick, live = route(outer, slot_of, passage_lists, list_counts, n_local)
    pair_scratch = pltpu.VMEM((n_pair, 2 * rows, LANES), BF16)
    acc_scratch = pltpu.VMEM((n_local, PLEN, width), F32)
    turned = pltpu.VMEM((n_local, width, PLEN), BF16)
    stat_shape = (n_q, n_pair, 2 * rows)
    mix_shape = (sds((inner, width, rows), F32),) * n_outer

    stats = vmem_call(
        stats_kernel,
        (pick, live),
        (keys, after(q_all, g_spread)),
        sds((2,) + stat_shape, F32),
        [pair_scratch],
        14,
        "stats",
    )
    norm = vmem_call(
        functools.partial(merge_kernel, n_outer),
        (),
        [stats] + [to_outer(stats, r) for r in range(1, n_outer)],
        sds((3,) + stat_shape, F32),
        [],
        1,
        "merge",
    )
    mixes = vmem_call(
        functools.partial(context_kernel, n_outer),
        (pick, live, outer),
        (keys, values, q_all, norm),
        mix_shape,
        [pair_scratch, turned],
        22,
        "context",
    )
    value_done = vmem_call(
        value_grad_kernel,
        (pick, live),
        (keys, q_all, g_all, after(norm, mixes[0])),
        sds((n_local, PLEN, width), BF16),
        [pair_scratch, pair_scratch, acc_scratch],
        20,
        "value_grad",
    )
    context, grad_dot = vmem_call(
        functools.partial(combine_context_kernel, n_outer),
        (outer,),
        partials(mixes) + [after(norm, value_done), g_all],
        (sds((inner, rows, width), BF16), sds((inner, n_pair, 2 * rows), F32)),
        [],
        2,
        "combine_context",
    )
    dots = [grad_dot] + [to_outer(grad_dot, n_outer - r) for r in range(1, n_outer)]
    projected = out_project(swap(context), out_weight)
    value_back = swap(value_done.reshape(inner, tok_local, width))
    output = lax.psum_scatter(projected, "head", scatter_dimension=1, tiled=True).astype(BF16)
    done = vmem_call(
        functools.partial(score_grad_kernel, n_outer),
        (pick, live, outer),
        [keys, values, q_all, g_all, after(norm, projected)] + dots,
        (sds((n_local, PLEN, width), BF16),) + mix_shape,
        [pair_scratch, pair_scratch, turned, acc_scratch],
        36,
        "score_grad",
    )
    key_back = swap(after(done[0], value_back).reshape(inner, tok_local, width))
    query_done = vmem_call(
        functools.partial(combine_query_kernel, n_outer),
        (),
        [after(done[1], output)] + partials(done[1:])[1:],
        sds((inner, rows, width), BF16),
        [],
        2,
        "combine_query",
    )
    query_grad = from_block(swap(after(query_done, key_back)))
    key_grad, value_grad = from_block(key_back), from_block(value_back)
    return (output, query_grad, key_grad, value_grad)


def solution(mesh):
    in_specs = (
        P("pas", "head"),
        P("pas", None),
        P(None, "head"),
        P(None, "head"),
        P("head", None),
        P("pas", "head"),
        P(),
        P(),
        P(),
    )
    out_specs = (P("pas", "head"), P("pas", "head"), P("pas", "head"), P("pas", "head"))
    return jax.shard_map(body, mesh=mesh, in_specs=in_specs, out_specs=out_specs, check_vma=False)
```

```python
import functools

import jax
import jax.numpy as jnp
from jax import lax
from jax.experimental import pallas as pl
from jax.experimental.pallas import tpu as pltpu
from jax.sharding import PartitionSpec as P

HEAD_DIM = 64
PLEN = 256
INNER = 4
GROUP = 8
LANES = 128
NEG_LARGE = -1e30
SCALE = HEAD_DIM ** (-0.5)

BF16 = jnp.bfloat16
F32 = jnp.float32

VMEM_LIMIT = 56 * 1024 * 1024


def params(semantics=None):
    return pltpu.CompilerParams(vmem_limit_bytes=VMEM_LIMIT, dimension_semantics=semantics)


def dot_nt(a, b):
    return lax.dot_general(a, b, (((1,), (1,)), ((), ())), preferred_element_type=F32)


def dot_nn(a, b):
    return lax.dot_general(a, b, (((1,), (0,)), ((), ())), preferred_element_type=F32)


def dot_tn(a, b):
    return lax.dot_general(a, b, (((0,), (0,)), ((), ())), preferred_element_type=F32)


def cost_us(time):
    return pl.CostEstimate(flops=int(time * 1e9), bytes_accessed=0, transcendentals=0)


def project_kernel(x_ref, w_ref, o_ref):
    width = o_ref.shape[2]
    for block in range(INNER):
        cols = slice(block * width, (block + 1) * width)
        o_ref[block] = dot_nn(x_ref[...], w_ref[:, cols]).astype(BF16)


def project(x, w):
    rows, depth = x.shape
    cols = w.shape[1]
    tile = 256
    return pl.pallas_call(
        project_kernel,
        grid=(rows // tile,),
        in_specs=[
            pl.BlockSpec((tile, depth), lambda m: (m, 0)),
            pl.BlockSpec((depth, cols), lambda m: (0, 0)),
        ],
        out_specs=pl.BlockSpec((INNER, tile, cols // INNER), lambda m: (0, m, 0)),
        out_shape=jax.ShapeDtypeStruct((INNER, rows, cols // INNER), BF16),
        compiler_params=params(("arbitrary",)),
        cost_estimate=cost_us(14),
        name="project",
    )(x, w)


def two_heads(block):
    lane = lax.broadcasted_iota(jnp.int32, block.shape, 1)
    zero = jnp.zeros_like(block)
    return jnp.concatenate(
        [jnp.where(lane < HEAD_DIM, block, zero), jnp.where(lane >= HEAD_DIM, block, zero)], axis=0
    )


def two_heads_turned(block):
    turned = jnp.transpose(block)
    feat = lax.broadcasted_iota(jnp.int32, turned.shape, 0)
    zero = jnp.zeros_like(turned)
    return jnp.concatenate(
        [jnp.where(feat < HEAD_DIM, turned, zero), jnp.where(feat >= HEAD_DIM, turned, zero)], axis=1
    )


def own_blocks(full):
    rows = full.shape[1] // 2
    return jnp.concatenate([full[:HEAD_DIM, :rows], full[HEAD_DIM:, rows:]], axis=0)


def route_kernel(n_local, outer_ref, slot_ref, list_ref, count_ref, pick_ref, live_ref):
    n_q, list_len = list_ref.shape
    first_slot = outer_ref[0] * n_local

    def question(ident, carry):
        found = jnp.int32(0)
        for e in range(list_len):
            slot = slot_ref[list_ref[ident, e]] - first_slot
            here = (slot >= 0) & (slot < n_local) & (e < count_ref[ident])
            pick_ref[ident, found] = jnp.where(here, slot, 0)
            found = found + here.astype(jnp.int32)
        for e in range(GROUP):
            pick_ref[ident, found + e] = 0
        live_ref[ident] = found
        return carry

    lax.fori_loop(0, n_q, question, 0)


def each_group(pick_ref, live_ref, ident, entries, start):
    live = live_ref[ident]

    def group(step, carry):
        first = step * GROUP
        slots = [pick_ref[ident, first + j] for j in range(GROUP)]
        return entries(carry, slots, [first + j < live for j in range(GROUP)])

    return lax.fori_loop(0, lax.div(live + (GROUP - 1), GROUP), group, start)


def pair_lanes(pair):
    return slice(pair * LANES, (pair + 1) * LANES)


def stacked(ref, slots, pair):
    return jnp.concatenate([ref[slot, :, pair_lanes(pair)] for slot in slots], axis=0)


def beside(ref, slots, pair):
    return jnp.concatenate([ref[slot, pair_lanes(pair), :] for slot in slots], axis=1)


def shifted(scores, lives, top):
    keys = scores.shape[0] // GROUP
    return [
        jnp.exp(scores[j * keys : (j + 1) * keys] - jnp.where(live, top, -NEG_LARGE))
        for j, live in enumerate(lives)
    ]


def stats_kernel(pick_ref, live_ref, k_ref, q_ref, o_ref, qt):
    n_q = q_ref.shape[0]
    n_pair = q_ref.shape[2] // LANES

    def question(ident, carry):
        for pair in range(n_pair):
            qt[pair] = two_heads_turned(q_ref[ident, :, pair_lanes(pair)])
        o_ref[0, ident] = jnp.full(o_ref.shape[2:], NEG_LARGE, F32)
        o_ref[1, ident] = jnp.zeros(o_ref.shape[2:], F32)

        def entries(state, slots, lives):
            for pair in range(n_pair):
                row = slice(pair, pair + 1)
                scores = [dot_nn(k_ref[slot, :, pair_lanes(pair)], qt[pair]) for slot in slots]
                old = o_ref[0, ident, row, :]
                new = old
                for j, live in enumerate(lives):
                    top = jnp.max(scores[j], axis=0, keepdims=True)
                    new = jnp.maximum(new, jnp.where(live, top, NEG_LARGE))
                add = o_ref[1, ident, row, :] * jnp.exp(old - new)
                for part, live in zip(scores, lives):
                    part = jnp.exp(part - jnp.where(live, new, -NEG_LARGE))
                    add = add + jnp.sum(part, axis=0, keepdims=True)
                o_ref[0, ident, row, :] = new
                o_ref[1, ident, row, :] = add
            return state

        each_group(pick_ref, live_ref, ident, entries, 0)
        return carry

    lax.fori_loop(0, n_q, question, 0)


def value_grad_kernel(pick_ref, live_ref, k_ref, q_ref, g_ref, st_ref, o_ref, qt, gbd, acc):
    n_q = q_ref.shape[0]
    n_pair = q_ref.shape[2] // LANES
    acc[...] = jnp.zeros_like(acc)

    def question(ident, carry):
        for pair in range(n_pair):
            qt[pair] = two_heads_turned(q_ref[ident, :, pair_lanes(pair)])
            gbd[pair] = two_heads(g_ref[ident, :, pair_lanes(pair)])

        def entries(state, slots, lives):
            for pair in range(n_pair):
                row = slice(pair, pair + 1)
                scores = dot_nn(stacked(k_ref, slots, pair), qt[pair])
                norm = st_ref[1, ident, row, :]
                probs = [
                    (part * norm).astype(BF16)
                    for part in shifted(scores, lives, st_ref[0, ident, row, :])
                ]
                term = dot_nn(jnp.concatenate(probs, axis=0), gbd[pair]).astype(BF16)
                for j, slot in enumerate(slots):
                    acc[slot, :, pair_lanes(pair)] += term[j * PLEN : (j + 1) * PLEN].astype(F32)
            return state

        each_group(pick_ref, live_ref, ident, entries, 0)
        return carry

    lax.fori_loop(0, n_q, question, 0)

    def finish(slot, carry):
        o_ref[slot] = acc[slot].astype(BF16)
        return carry

    lax.fori_loop(0, k_ref.shape[0], finish, 0)


def turn(src_ref, dst_ref):
    def one(slot, carry):
        dst_ref[slot] = jnp.transpose(src_ref[slot])
        return carry

    lax.fori_loop(0, src_ref.shape[0], one, 0)


def context_kernel(n_outer, pick_ref, live_ref, outer_ref, k_ref, v_ref, q_ref, st_ref, *rest):
    o_refs, (qt, vt) = rest[:n_outer], rest[n_outer:]
    n_q = q_ref.shape[0]
    inner = n_q // n_outer
    n_pair = q_ref.shape[2] // LANES
    turn(v_ref, vt)

    def question(o_ref, outer, index, carry):
        ident = outer * inner + index
        for pair in range(n_pair):
            qt[pair] = two_heads_turned(q_ref[ident, :, pair_lanes(pair)])
        zero = jnp.zeros((LANES, 2 * q_ref.shape[1]), F32)

        def entries(sums, slots, lives):
            out = []
            for pair in range(n_pair):
                scores = dot_nn(stacked(k_ref, slots, pair), qt[pair])
                weights = [
                    part.astype(BF16)
                    for part in shifted(scores, lives, st_ref[0, ident, slice(pair, pair + 1), :])
                ]
                mix = dot_nn(beside(vt, slots, pair), jnp.concatenate(weights, axis=0))
                out.append(sums[pair] + mix)
            return tuple(out)

        sums = each_group(pick_ref, live_ref, ident, entries, (zero,) * n_pair)
        for pair in range(n_pair):
            o_ref[index, pair_lanes(pair), :] = own_blocks(sums[pair])
        return carry

    for r in reversed(range(n_outer)):
        outer = lax.rem(outer_ref[0] + r, n_outer)
        lax.fori_loop(0, inner, functools.partial(question, o_refs[r], outer), 0)


def score_grad_kernel(n_outer, pick_ref, live_ref, outer_ref, k_ref, v_ref, q_ref, g_ref, st_ref, *rest):
    dot_refs, rest = rest[:n_outer], rest[n_outer:]
    dk_ref, rest = rest[0], rest[1:]
    dq_refs, (qt, qbd, gt, kt, acc_k) = rest[:n_outer], rest[n_outer:]
    n_q = q_ref.shape[0]
    inner = n_q // n_outer
    n_pair = q_ref.shape[2] // LANES
    turn(k_ref, kt)
    acc_k[...] = jnp.zeros_like(acc_k)

    def question(dot_ref, dq_ref, outer, index, carry):
        ident = outer * inner + index
        for pair in range(n_pair):
            qbd[pair] = two_heads(q_ref[ident, :, pair_lanes(pair)])
            qt[pair] = two_heads_turned(q_ref[ident, :, pair_lanes(pair)])
            gt[pair] = two_heads_turned(g_ref[ident, :, pair_lanes(pair)])
        zero = jnp.zeros((LANES, 2 * q_ref.shape[1]), F32)

        def entries(sums, slots, lives):
            out = []
            for pair in range(n_pair):
                row = slice(pair, pair + 1)
                scores = dot_nn(stacked(k_ref, slots, pair), qt[pair])
                dprob = dot_nn(stacked(v_ref, slots, pair), gt[pair])
                norm = st_ref[1, ident, row, :]
                dots = dot_ref[index, row, :]
                dscore = [
                    (part * norm * (dprob[j * PLEN : (j + 1) * PLEN] - dots)).astype(BF16)
                    for j, part in enumerate(shifted(scores, lives, st_ref[0, ident, row, :]))
                ]
                dscore = jnp.concatenate(dscore, axis=0)
                term = dot_nn(dscore, qbd[pair]).astype(BF16)
                for j, slot in enumerate(slots):
                    acc_k[slot, :, pair_lanes(pair)] += term[j * PLEN : (j + 1) * PLEN].astype(F32)
                out.append(sums[pair] + dot_nn(beside(kt, slots, pair), dscore))
            return tuple(out)

        sums = each_group(pick_ref, live_ref, ident, entries, (zero,) * n_pair)
        for pair in range(n_pair):
            dq_ref[index, pair_lanes(pair), :] = own_blocks(sums[pair])
        return carry

    for r in reversed(range(n_outer)):
        outer = lax.rem(outer_ref[0] + r, n_outer)
        lax.fori_loop(0, inner, functools.partial(question, dot_refs[r], dq_refs[r], outer), 0)

    def finish(slot, carry):
        dk_ref[slot] = acc_k[slot].astype(BF16)
        return carry

    lax.fori_loop(0, k_ref.shape[0], finish, 0)


def merge_kernel(n_outer, *refs):
    parts, o_ref = refs[:n_outer], refs[n_outer]
    top = parts[0][0]
    for part in parts[1:]:
        top = jnp.maximum(top, part[0])
    total = parts[0][1] * jnp.exp(parts[0][0] - top)
    for part in parts[1:]:
        total = total + part[1] * jnp.exp(part[0] - top)
    o_ref[0] = top
    o_ref[1] = 1.0 / total
    o_ref[2] = total


def combine_context_kernel(n_parts, outer_ref, *refs):
    parts, (st_ref, g_ref, o_ref, dot_ref) = refs[:n_parts], refs[n_parts:]
    width = g_ref.shape[2]
    inner = o_ref.shape[0]
    first = outer_ref[0] * inner
    for q in range(inner):
        mix = parts[0][q]
        for part in parts[1:]:
            mix = mix + part[q]
        grad = jnp.transpose(g_ref[first + q].astype(F32))
        rows = mix.shape[1]
        pieces = []
        for head in range(width // HEAD_DIM):
            feats = slice(head * HEAD_DIM, (head + 1) * HEAD_DIM)
            pair, lanes = head // 2, slice((head % 2) * rows, (head % 2 + 1) * rows)
            total = st_ref[2, first + q, pair : pair + 1, lanes]
            ctx = (mix[feats] / total).astype(BF16).astype(F32)
            dot_ref[q, pair : pair + 1, lanes] = jnp.sum(grad[feats] * ctx, axis=0, keepdims=True)
            pieces.append(ctx)
        o_ref[q] = jnp.transpose(jnp.concatenate(pieces, axis=0)).astype(BF16)


def combine_query_kernel(n_parts, *refs):
    parts, o_ref = refs[:n_parts], refs[n_parts]
    for q in range(o_ref.shape[0]):
        mix = parts[0][q]
        for part in parts[1:]:
            mix = mix + part[q]
        o_ref[q] = jnp.transpose(mix * SCALE).astype(BF16)


def spread_kernel(x_ref, o_ref):
    width = o_ref.shape[2]
    for block in range(INNER):
        part = x_ref[:, block * width : (block + 1) * width] * jnp.asarray(SCALE, BF16)
        for outer in range(o_ref.shape[0] // INNER):
            o_ref[outer * INNER + block] = part


def context_grad_kernel(x_ref, w_ref, o_ref):
    part = dot_nt(x_ref[...], w_ref[...]).astype(BF16)
    for outer in range(o_ref.shape[0]):
        o_ref[outer, 0] = part


def context_grad_blocks(x, w, n_outer, width):
    rows, depth = x.shape
    return pl.pallas_call(
        context_grad_kernel,
        grid=(INNER,),
        in_specs=[
            pl.BlockSpec((rows, depth), lambda j: (0, 0)),
            pl.BlockSpec((width, depth), lambda j: (j, 0)),
        ],
        out_specs=pl.BlockSpec((n_outer, 1, rows, width), lambda j: (0, j, 0, 0)),
        out_shape=jax.ShapeDtypeStruct((n_outer, INNER, rows, width), BF16),
        compiler_params=params(("arbitrary",)),
        cost_estimate=cost_us(5),
        name="context_grad",
    )(x, w)


def out_project_kernel(x_ref, w_ref, o_ref):
    step = pl.program_id(0)
    part = dot_nn(x_ref[0], w_ref[...])

    @pl.when(step == 0)
    def _():
        o_ref[...] = part

    @pl.when(step > 0)
    def _():
        o_ref[...] += part


def out_project(x, w):
    blocks, rows, width = x.shape
    cols = w.shape[1]
    return pl.pallas_call(
        out_project_kernel,
        grid=(blocks,),
        in_specs=[
            pl.BlockSpec((1, rows, width), lambda j: (j, 0, 0)),
            pl.BlockSpec((width, cols), lambda j: (j, 0)),
        ],
        out_specs=pl.BlockSpec((rows, cols), lambda j: (0, 0)),
        out_shape=jax.ShapeDtypeStruct((rows, cols), F32),
        compiler_params=params(("arbitrary",)),
        cost_estimate=cost_us(5),
        name="out_project",
    )(x, w)


def vmem_call(kernel, scalars, arrays, out_shape, scratch, time, name):
    smem = pl.BlockSpec(memory_space=pltpu.SMEM)
    vmem = pl.BlockSpec(memory_space=pltpu.VMEM)
    return pl.pallas_call(
        kernel,
        in_specs=[smem] * len(scalars) + [vmem] * len(arrays),
        out_specs=jax.tree.map(lambda _: vmem, out_shape),
        out_shape=out_shape,
        scratch_shapes=scratch,
        compiler_params=params(),
        cost_estimate=cost_us(time),
        name=name,
    )(*scalars, *arrays)


def route(outer, slot_of, passage_lists, list_counts, n_local):
    smem = pl.BlockSpec(memory_space=pltpu.SMEM)
    n_q, list_len = passage_lists.shape
    return pl.pallas_call(
        functools.partial(route_kernel, n_local),
        in_specs=[smem] * 4,
        out_specs=(smem, smem),
        out_shape=(
            jax.ShapeDtypeStruct((n_q, list_len + GROUP), jnp.int32),
            jax.ShapeDtypeStruct((n_q,), jnp.int32),
        ),
        cost_estimate=cost_us(3),
        name="route",
    )(outer, slot_of, passage_lists, list_counts)


def after(value, *others):
    return lax.optimization_barrier((value,) + others)[0]


def body(
    queries,
    encoded,
    key_weight,
    value_weight,
    out_weight,
    out_grad,
    slot_of,
    passage_lists,
    list_counts,
):
    head_width = key_weight.shape[1]
    rows = queries.shape[0]
    tok_local = encoded.shape[0]
    n_pas = lax.axis_size("pas")
    inner = INNER
    n_outer = n_pas // inner
    width = head_width // inner
    n_pair = width // LANES
    n_local = inner * (tok_local // PLEN)
    n_q = n_pas
    outer = (lax.axis_index("pas") // inner).astype(jnp.int32).reshape(1)
    groups = [[o * inner + i for i in range(inner)] for o in range(n_outer)]
    sds = jax.ShapeDtypeStruct

    def swap(x):
        return lax.all_to_all(
            x, "pas", split_axis=0, concat_axis=0, tiled=True, axis_index_groups=groups
        )

    def swap_all(x):
        return lax.all_to_all(x, "pas", split_axis=0, concat_axis=0, tiled=True)

    def to_outer(x, r):
        return lax.ppermute(
            x,
            "pas",
            [(o * inner + i, ((o + r) % n_outer) * inner + i) for o in range(n_outer) for i in range(inner)],
        )

    def from_block(x):
        return jnp.transpose(x, (1, 0, 2)).reshape(x.shape[1], head_width)

    def partials(parts):
        return [parts[0]] + [to_outer(parts[r], r) for r in range(1, n_outer)]

    q_spread = vmem_call(spread_kernel, (), (queries,), sds((n_q, rows, width), BF16), [], 1.5, "spread")
    q_all = swap_all(q_spread)
    grad_rows = lax.all_gather(out_grad, "head", axis=1, tiled=True)

    key_part = project(after(encoded, q_spread), key_weight)
    keys = swap(key_part).reshape(n_local, PLEN, width)
    value_part = project(after(encoded, key_part, grad_rows), value_weight)
    g_spread = context_grad_blocks(after(grad_rows, value_part), out_weight, n_outer, width)
    g_spread = g_spread.reshape(n_q, rows, width)
    pick, live = route(after(outer, value_part), slot_of, passage_lists, list_counts, n_local)
    values = swap(after(value_part, g_spread, pick)).reshape(n_local, PLEN, width)

    pair_scratch = pltpu.VMEM((n_pair, 2 * rows, LANES), BF16)
    turned_pair = pltpu.VMEM((n_pair, LANES, 2 * rows), BF16)
    acc_scratch = pltpu.VMEM((n_local, PLEN, width), F32)
    turned = pltpu.VMEM((n_local, width, PLEN), BF16)
    stat_shape = (n_q, n_pair, 2 * rows)
    mix_shape = (sds((inner, width, rows), F32),) * n_outer

    stats = vmem_call(
        stats_kernel,
        (pick, live),
        (keys, q_all),
        sds((2,) + stat_shape, F32),
        [turned_pair],
        13,
        "stats",
    )
    norm = vmem_call(
        functools.partial(merge_kernel, n_outer),
        (),
        [stats] + [to_outer(stats, r) for r in range(1, n_outer)],
        sds((3,) + stat_shape, F32),
        [],
        1,
        "merge",
    )
    mixes = vmem_call(
        functools.partial(context_kernel, n_outer),
        (pick, live, outer),
        (keys, values, q_all, norm),
        mix_shape,
        [turned_pair, turned],
        19,
        "context",
    )
    g_all = swap_all(after(g_spread, mixes[0]))
    value_done = vmem_call(
        value_grad_kernel,
        (pick, live),
        (keys, q_all, g_all, after(norm, mixes[0])),
        sds((n_local, PLEN, width), BF16),
        [turned_pair, pair_scratch, acc_scratch],
        15,
        "value_grad",
    )
    context, grad_dot = vmem_call(
        functools.partial(combine_context_kernel, n_outer),
        (outer,),
        partials(mixes) + [after(norm, value_done), g_all],
        (sds((inner, rows, width), BF16), sds((inner, n_pair, 2 * rows), F32)),
        [],
        2,
        "combine_context",
    )
    dots = [grad_dot] + [to_outer(grad_dot, n_outer - r) for r in range(1, n_outer)]
    projected = out_project(swap(context), out_weight)
    value_back = swap(value_done.reshape(inner, tok_local, width))
    output = lax.psum_scatter(projected, "head", scatter_dimension=1, tiled=True).astype(BF16)
    done = vmem_call(
        functools.partial(score_grad_kernel, n_outer),
        (pick, live, outer),
        [keys, values, q_all, g_all, after(norm, projected)] + dots,
        (sds((n_local, PLEN, width), BF16),) + mix_shape,
        [turned_pair, pair_scratch, turned_pair, turned, acc_scratch],
        25,
        "score_grad",
    )
    key_back = swap(after(done[0], value_back).reshape(inner, tok_local, width))
    query_done = vmem_call(
        functools.partial(combine_query_kernel, n_outer),
        (),
        [after(done[1], output)] + partials(done[1:])[1:],
        sds((inner, rows, width), BF16),
        [],
        2,
        "combine_query",
    )
    query_grad = from_block(swap(after(query_done, key_back)))
    key_grad, value_grad = from_block(key_back), from_block(value_back)
    return (output, query_grad, key_grad, value_grad)


def solution(mesh):
    in_specs = (
        P("pas", "head"),
        P("pas", None),
        P(None, "head"),
        P(None, "head"),
        P("head", None),
        P("pas", "head"),
        P(),
        P(),
        P(),
    )
    out_specs = (P("pas", "head"), P("pas", "head"), P("pas", "head"), P("pas", "head"))
    return jax.shard_map(body, mesh=mesh, in_specs=in_specs, out_specs=out_specs, check_vma=False)
```

```python
import functools

import jax
import jax.numpy as jnp
from jax import lax
from jax.experimental import pallas as pl
from jax.experimental.pallas import tpu as pltpu
from jax.sharding import PartitionSpec as P

HEAD_DIM = 64
PLEN = 256
INNER = 4
GROUP = 8
LANES = 128
NEG_LARGE = -1e30
SCALE = HEAD_DIM ** (-0.5)

BF16 = jnp.bfloat16
F32 = jnp.float32

VMEM_LIMIT = 56 * 1024 * 1024


def params(semantics=None):
    return pltpu.CompilerParams(vmem_limit_bytes=VMEM_LIMIT, dimension_semantics=semantics)


def dot_nt(a, b):
    return lax.dot_general(a, b, (((1,), (1,)), ((), ())), preferred_element_type=F32)


def dot_nn(a, b):
    return lax.dot_general(a, b, (((1,), (0,)), ((), ())), preferred_element_type=F32)


def dot_tn(a, b):
    return lax.dot_general(a, b, (((0,), (0,)), ((), ())), preferred_element_type=F32)


def cost_us(time):
    return pl.CostEstimate(flops=int(time * 1e9), bytes_accessed=0, transcendentals=0)


def project_kernel(x_ref, w_ref, o_ref):
    width = o_ref.shape[2]
    for block in range(INNER):
        cols = slice(block * width, (block + 1) * width)
        o_ref[block] = dot_nn(x_ref[...], w_ref[:, cols]).astype(BF16)


def project(x, w):
    rows, depth = x.shape
    cols = w.shape[1]
    tile = 256
    return pl.pallas_call(
        project_kernel,
        grid=(rows // tile,),
        in_specs=[
            pl.BlockSpec((tile, depth), lambda m: (m, 0)),
            pl.BlockSpec((depth, cols), lambda m: (0, 0)),
        ],
        out_specs=pl.BlockSpec((INNER, tile, cols // INNER), lambda m: (0, m, 0)),
        out_shape=jax.ShapeDtypeStruct((INNER, rows, cols // INNER), BF16),
        compiler_params=params(("arbitrary",)),
        cost_estimate=cost_us(14),
        name="project",
    )(x, w)


def two_heads(block):
    lane = lax.broadcasted_iota(jnp.int32, block.shape, 1)
    zero = jnp.zeros_like(block)
    return jnp.concatenate(
        [jnp.where(lane < HEAD_DIM, block, zero), jnp.where(lane >= HEAD_DIM, block, zero)], axis=0
    )


def two_heads_turned(block):
    turned = jnp.transpose(block)
    feat = lax.broadcasted_iota(jnp.int32, turned.shape, 0)
    zero = jnp.zeros_like(turned)
    return jnp.concatenate(
        [jnp.where(feat < HEAD_DIM, turned, zero), jnp.where(feat >= HEAD_DIM, turned, zero)], axis=1
    )


def own_blocks(full):
    rows = full.shape[1] // 2
    return jnp.concatenate([full[:HEAD_DIM, :rows], full[HEAD_DIM:, rows:]], axis=0)


def route_kernel(n_local, outer_ref, slot_ref, list_ref, count_ref, pick_ref, live_ref):
    n_q, list_len = list_ref.shape
    first_slot = outer_ref[0] * n_local

    def question(ident, carry):
        found = jnp.int32(0)
        for e in range(list_len):
            slot = slot_ref[list_ref[ident, e]] - first_slot
            here = (slot >= 0) & (slot < n_local) & (e < count_ref[ident])
            pick_ref[ident, found] = jnp.where(here, slot, 0)
            found = found + here.astype(jnp.int32)
        for e in range(GROUP):
            pick_ref[ident, found + e] = 0
        live_ref[ident] = found
        return carry

    lax.fori_loop(0, n_q, question, 0)


def each_group(pick_ref, live_ref, ident, entries, start):
    live = live_ref[ident]

    def group(step, carry):
        first = step * GROUP
        slots = [pick_ref[ident, first + j] for j in range(GROUP)]
        return entries(carry, slots, [first + j < live for j in range(GROUP)])

    return lax.fori_loop(0, lax.div(live + (GROUP - 1), GROUP), group, start)


def pair_lanes(pair):
    return slice(pair * LANES, (pair + 1) * LANES)


def stacked(ref, slots, pair):
    return jnp.concatenate([ref[slot, :, pair_lanes(pair)] for slot in slots], axis=0)


def beside(ref, slots, pair):
    return jnp.concatenate([ref[slot, pair_lanes(pair), :] for slot in slots], axis=1)


def shifted(scores, lives, top):
    keys = scores.shape[0] // GROUP
    return [
        jnp.exp(scores[j * keys : (j + 1) * keys] - jnp.where(live, top, -NEG_LARGE))
        for j, live in enumerate(lives)
    ]


def stats_kernel(pick_ref, live_ref, k_ref, q_ref, o_ref, qt):
    n_q = q_ref.shape[0]
    n_pair = q_ref.shape[2] // LANES

    def question(ident, carry):
        for pair in range(n_pair):
            qt[pair] = two_heads_turned(q_ref[ident, :, pair_lanes(pair)])
        o_ref[0, ident] = jnp.full(o_ref.shape[2:], NEG_LARGE, F32)
        o_ref[1, ident] = jnp.zeros(o_ref.shape[2:], F32)

        def entries(state, slots, lives):
            for pair in range(n_pair):
                row = slice(pair, pair + 1)
                scores = [dot_nn(k_ref[slot, :, pair_lanes(pair)], qt[pair]) for slot in slots]
                old = o_ref[0, ident, row, :]
                new = old
                for j, live in enumerate(lives):
                    top = jnp.max(scores[j], axis=0, keepdims=True)
                    new = jnp.maximum(new, jnp.where(live, top, NEG_LARGE))
                add = o_ref[1, ident, row, :] * jnp.exp(old - new)
                for part, live in zip(scores, lives):
                    part = jnp.exp(part - jnp.where(live, new, -NEG_LARGE))
                    add = add + jnp.sum(part, axis=0, keepdims=True)
                o_ref[0, ident, row, :] = new
                o_ref[1, ident, row, :] = add
            return state

        each_group(pick_ref, live_ref, ident, entries, 0)
        return carry

    lax.fori_loop(0, n_q, question, 0)


def value_grad_kernel(pick_ref, live_ref, k_ref, q_ref, g_ref, st_ref, o_ref, qt, gbd, acc):
    n_q = q_ref.shape[0]
    n_pair = q_ref.shape[2] // LANES
    acc[...] = jnp.zeros_like(acc)

    def question(ident, carry):
        for pair in range(n_pair):
            qt[pair] = two_heads_turned(q_ref[ident, :, pair_lanes(pair)])
            gbd[pair] = two_heads(g_ref[ident, :, pair_lanes(pair)])

        def entries(state, slots, lives):
            for pair in range(n_pair):
                row = slice(pair, pair + 1)
                scores = dot_nn(stacked(k_ref, slots, pair), qt[pair])
                norm = st_ref[1, ident, row, :]
                probs = [
                    (part * norm).astype(BF16)
                    for part in shifted(scores, lives, st_ref[0, ident, row, :])
                ]
                term = dot_nn(jnp.concatenate(probs, axis=0), gbd[pair]).astype(BF16)
                for j, slot in enumerate(slots):
                    acc[slot, :, pair_lanes(pair)] += term[j * PLEN : (j + 1) * PLEN].astype(F32)
            return state

        each_group(pick_ref, live_ref, ident, entries, 0)
        return carry

    lax.fori_loop(0, n_q, question, 0)

    def finish(slot, carry):
        o_ref[slot] = acc[slot].astype(BF16)
        return carry

    lax.fori_loop(0, k_ref.shape[0], finish, 0)


def turn(src_ref, dst_ref):
    def one(slot, carry):
        dst_ref[slot] = jnp.transpose(src_ref[slot])
        return carry

    lax.fori_loop(0, src_ref.shape[0], one, 0)


def context_kernel(n_outer, r, pick_ref, live_ref, outer_ref, k_ref, v_ref, q_ref, st_ref, o_ref, qt, vt):
    n_pair = q_ref.shape[2] // LANES
    first = lax.rem(outer_ref[0] + r, n_outer) * o_ref.shape[0]
    turn(v_ref, vt)

    def question(index, carry):
        ident = first + index
        for pair in range(n_pair):
            qt[pair] = two_heads_turned(q_ref[ident, :, pair_lanes(pair)])
        zero = jnp.zeros((LANES, 2 * q_ref.shape[1]), F32)

        def entries(sums, slots, lives):
            out = []
            for pair in range(n_pair):
                scores = dot_nn(stacked(k_ref, slots, pair), qt[pair])
                weights = [
                    part.astype(BF16)
                    for part in shifted(scores, lives, st_ref[0, ident, slice(pair, pair + 1), :])
                ]
                mix = dot_nn(beside(vt, slots, pair), jnp.concatenate(weights, axis=0))
                out.append(sums[pair] + mix)
            return tuple(out)

        sums = each_group(pick_ref, live_ref, ident, entries, (zero,) * n_pair)
        for pair in range(n_pair):
            o_ref[index, pair_lanes(pair), :] = own_blocks(sums[pair])
        return carry

    lax.fori_loop(0, o_ref.shape[0], question, 0)


def score_grad_kernel(n_outer, pick_ref, live_ref, outer_ref, k_ref, v_ref, q_ref, g_ref, st_ref, *rest):
    dot_refs, rest = rest[:n_outer], rest[n_outer:]
    dk_ref, rest = rest[0], rest[1:]
    dq_refs, (qt, qbd, gt, kt, acc_k) = rest[:n_outer], rest[n_outer:]
    n_q = q_ref.shape[0]
    inner = n_q // n_outer
    n_pair = q_ref.shape[2] // LANES
    turn(k_ref, kt)
    acc_k[...] = jnp.zeros_like(acc_k)

    def question(dot_ref, dq_ref, outer, index, carry):
        ident = outer * inner + index
        for pair in range(n_pair):
            qbd[pair] = two_heads(q_ref[ident, :, pair_lanes(pair)])
            qt[pair] = two_heads_turned(q_ref[ident, :, pair_lanes(pair)])
            gt[pair] = two_heads_turned(g_ref[ident, :, pair_lanes(pair)])
        zero = jnp.zeros((LANES, 2 * q_ref.shape[1]), F32)

        def entries(sums, slots, lives):
            out = []
            for pair in range(n_pair):
                row = slice(pair, pair + 1)
                scores = dot_nn(stacked(k_ref, slots, pair), qt[pair])
                dprob = dot_nn(stacked(v_ref, slots, pair), gt[pair])
                norm = st_ref[1, ident, row, :]
                dots = dot_ref[index, row, :]
                dscore = [
                    (part * norm * (dprob[j * PLEN : (j + 1) * PLEN] - dots)).astype(BF16)
                    for j, part in enumerate(shifted(scores, lives, st_ref[0, ident, row, :]))
                ]
                dscore = jnp.concatenate(dscore, axis=0)
                term = dot_nn(dscore, qbd[pair]).astype(BF16)
                for j, slot in enumerate(slots):
                    acc_k[slot, :, pair_lanes(pair)] += term[j * PLEN : (j + 1) * PLEN].astype(F32)
                out.append(sums[pair] + dot_nn(beside(kt, slots, pair), dscore))
            return tuple(out)

        sums = each_group(pick_ref, live_ref, ident, entries, (zero,) * n_pair)
        for pair in range(n_pair):
            dq_ref[index, pair_lanes(pair), :] = own_blocks(sums[pair])
        return carry

    for r in reversed(range(n_outer)):
        outer = lax.rem(outer_ref[0] + r, n_outer)
        lax.fori_loop(0, inner, functools.partial(question, dot_refs[r], dq_refs[r], outer), 0)

    def finish(slot, carry):
        dk_ref[slot] = acc_k[slot].astype(BF16)
        return carry

    lax.fori_loop(0, k_ref.shape[0], finish, 0)


def merge_kernel(n_outer, *refs):
    parts, o_ref = refs[:n_outer], refs[n_outer]
    top = parts[0][0]
    for part in parts[1:]:
        top = jnp.maximum(top, part[0])
    total = parts[0][1] * jnp.exp(parts[0][0] - top)
    for part in parts[1:]:
        total = total + part[1] * jnp.exp(part[0] - top)
    o_ref[0] = top
    o_ref[1] = 1.0 / total
    o_ref[2] = total


def combine_context_kernel(n_parts, outer_ref, *refs):
    parts, (st_ref, g_ref, o_ref, dot_ref) = refs[:n_parts], refs[n_parts:]
    width = g_ref.shape[2]
    inner = o_ref.shape[0]
    first = outer_ref[0] * inner
    for q in range(inner):
        mix = parts[0][q]
        for part in parts[1:]:
            mix = mix + part[q]
        grad = jnp.transpose(g_ref[first + q].astype(F32))
        rows = mix.shape[1]
        pieces = []
        for head in range(width // HEAD_DIM):
            feats = slice(head * HEAD_DIM, (head + 1) * HEAD_DIM)
            pair, lanes = head // 2, slice((head % 2) * rows, (head % 2 + 1) * rows)
            total = st_ref[2, first + q, pair : pair + 1, lanes]
            ctx = (mix[feats] / total).astype(BF16).astype(F32)
            dot_ref[q, pair : pair + 1, lanes] = jnp.sum(grad[feats] * ctx, axis=0, keepdims=True)
            pieces.append(ctx)
        o_ref[q] = jnp.transpose(jnp.concatenate(pieces, axis=0)).astype(BF16)


def combine_query_kernel(n_parts, *refs):
    parts, o_ref = refs[:n_parts], refs[n_parts]
    for q in range(o_ref.shape[0]):
        mix = parts[0][q]
        for part in parts[1:]:
            mix = mix + part[q]
        o_ref[q] = jnp.transpose(mix * SCALE).astype(BF16)


def spread_kernel(x_ref, o_ref):
    width = o_ref.shape[2]
    for block in range(INNER):
        part = x_ref[:, block * width : (block + 1) * width] * jnp.asarray(SCALE, BF16)
        for outer in range(o_ref.shape[0] // INNER):
            o_ref[outer * INNER + block] = part


def context_grad_kernel(x_ref, w_ref, o_ref):
    part = dot_nt(x_ref[...], w_ref[...]).astype(BF16)
    for outer in range(o_ref.shape[0]):
        o_ref[outer, 0] = part


def context_grad_blocks(x, w, n_outer, width):
    rows, depth = x.shape
    return pl.pallas_call(
        context_grad_kernel,
        grid=(INNER,),
        in_specs=[
            pl.BlockSpec((rows, depth), lambda j: (0, 0)),
            pl.BlockSpec((width, depth), lambda j: (j, 0)),
        ],
        out_specs=pl.BlockSpec((n_outer, 1, rows, width), lambda j: (0, j, 0, 0)),
        out_shape=jax.ShapeDtypeStruct((n_outer, INNER, rows, width), BF16),
        compiler_params=params(("arbitrary",)),
        cost_estimate=cost_us(5),
        name="context_grad",
    )(x, w)


def out_project_kernel(x_ref, w_ref, o_ref):
    step = pl.program_id(0)
    part = dot_nn(x_ref[0], w_ref[...])

    @pl.when(step == 0)
    def _():
        o_ref[...] = part

    @pl.when(step > 0)
    def _():
        o_ref[...] += part


def out_project(x, w):
    blocks, rows, width = x.shape
    cols = w.shape[1]
    return pl.pallas_call(
        out_project_kernel,
        grid=(blocks,),
        in_specs=[
            pl.BlockSpec((1, rows, width), lambda j: (j, 0, 0)),
            pl.BlockSpec((width, cols), lambda j: (j, 0)),
        ],
        out_specs=pl.BlockSpec((rows, cols), lambda j: (0, 0)),
        out_shape=jax.ShapeDtypeStruct((rows, cols), F32),
        compiler_params=params(("arbitrary",)),
        cost_estimate=cost_us(5),
        name="out_project",
    )(x, w)


def vmem_call(kernel, scalars, arrays, out_shape, scratch, time, name):
    smem = pl.BlockSpec(memory_space=pltpu.SMEM)
    vmem = pl.BlockSpec(memory_space=pltpu.VMEM)
    return pl.pallas_call(
        kernel,
        in_specs=[smem] * len(scalars) + [vmem] * len(arrays),
        out_specs=jax.tree.map(lambda _: vmem, out_shape),
        out_shape=out_shape,
        scratch_shapes=scratch,
        compiler_params=params(),
        cost_estimate=cost_us(time),
        name=name,
    )(*scalars, *arrays)


def route(outer, slot_of, passage_lists, list_counts, n_local):
    smem = pl.BlockSpec(memory_space=pltpu.SMEM)
    n_q, list_len = passage_lists.shape
    return pl.pallas_call(
        functools.partial(route_kernel, n_local),
        in_specs=[smem] * 4,
        out_specs=(smem, smem),
        out_shape=(
            jax.ShapeDtypeStruct((n_q, list_len + GROUP), jnp.int32),
            jax.ShapeDtypeStruct((n_q,), jnp.int32),
        ),
        cost_estimate=cost_us(3),
        name="route",
    )(outer, slot_of, passage_lists, list_counts)


def after(value, *others):
    return lax.optimization_barrier((value,) + others)[0]


def body(
    queries,
    encoded,
    key_weight,
    value_weight,
    out_weight,
    out_grad,
    slot_of,
    passage_lists,
    list_counts,
):
    head_width = key_weight.shape[1]
    rows = queries.shape[0]
    tok_local = encoded.shape[0]
    n_pas = lax.axis_size("pas")
    inner = INNER
    n_outer = n_pas // inner
    width = head_width // inner
    n_pair = width // LANES
    n_local = inner * (tok_local // PLEN)
    n_q = n_pas
    outer = (lax.axis_index("pas") // inner).astype(jnp.int32).reshape(1)
    groups = [[o * inner + i for i in range(inner)] for o in range(n_outer)]
    sds = jax.ShapeDtypeStruct

    def swap(x):
        return lax.all_to_all(
            x, "pas", split_axis=0, concat_axis=0, tiled=True, axis_index_groups=groups
        )

    def swap_all(x):
        return lax.all_to_all(x, "pas", split_axis=0, concat_axis=0, tiled=True)

    def to_outer(x, r):
        return lax.ppermute(
            x,
            "pas",
            [(o * inner + i, ((o + r) % n_outer) * inner + i) for o in range(n_outer) for i in range(inner)],
        )

    def from_block(x):
        return jnp.transpose(x, (1, 0, 2)).reshape(x.shape[1], head_width)

    def partials(parts):
        return [parts[0]] + [to_outer(parts[r], r) for r in range(1, n_outer)]

    q_spread = vmem_call(spread_kernel, (), (queries,), sds((n_q, rows, width), BF16), [], 1.5, "spread")
    q_all = swap_all(q_spread)
    grad_rows = lax.all_gather(out_grad, "head", axis=1, tiled=True)

    key_part = project(after(encoded, q_spread), key_weight)
    keys = swap(key_part).reshape(n_local, PLEN, width)
    value_part = project(after(encoded, key_part, grad_rows), value_weight)
    g_spread = context_grad_blocks(after(grad_rows, value_part), out_weight, n_outer, width)
    g_spread = g_spread.reshape(n_q, rows, width)
    pick, live = route(after(outer, value_part), slot_of, passage_lists, list_counts, n_local)
    values = swap(after(value_part, g_spread, pick)).reshape(n_local, PLEN, width)

    pair_scratch = pltpu.VMEM((n_pair, 2 * rows, LANES), BF16)
    turned_pair = pltpu.VMEM((n_pair, LANES, 2 * rows), BF16)
    acc_scratch = pltpu.VMEM((n_local, PLEN, width), F32)
    turned = pltpu.VMEM((n_local, width, PLEN), BF16)
    stat_shape = (n_q, n_pair, 2 * rows)
    mix_shape = sds((inner, width, rows), F32)

    stats = vmem_call(
        stats_kernel,
        (pick, live),
        (keys, q_all),
        sds((2,) + stat_shape, F32),
        [turned_pair],
        13,
        "stats",
    )
    norm = vmem_call(
        functools.partial(merge_kernel, n_outer),
        (),
        [stats] + [to_outer(stats, r) for r in range(1, n_outer)],
        sds((3,) + stat_shape, F32),
        [],
        1,
        "merge",
    )
    g_all = swap_all(after(g_spread, values))
    mixes, norm_then = [None] * n_outer, norm
    for r in reversed(range(n_outer)):
        mixes[r] = vmem_call(
            functools.partial(context_kernel, n_outer, r),
            (pick, live, outer),
            (keys, values, q_all, norm_then),
            mix_shape,
            [turned_pair, turned],
            10,
            "context",
        )
        norm_then = after(norm, mixes[r], g_all)
    value_done = vmem_call(
        value_grad_kernel,
        (pick, live),
        (keys, q_all, g_all, norm_then),
        sds((n_local, PLEN, width), BF16),
        [turned_pair, pair_scratch, acc_scratch],
        15,
        "value_grad",
    )
    context, grad_dot = vmem_call(
        functools.partial(combine_context_kernel, n_outer),
        (outer,),
        partials([after(mix, g_all) for mix in mixes]) + [after(norm, value_done), g_all],
        (sds((inner, rows, width), BF16), sds((inner, n_pair, 2 * rows), F32)),
        [],
        2,
        "combine_context",
    )
    dots = [grad_dot] + [to_outer(grad_dot, n_outer - r) for r in range(1, n_outer)]
    projected = out_project(swap(after(context, *dots[1:])), out_weight)
    value_back = swap(value_done.reshape(inner, tok_local, width))
    output = lax.psum_scatter(projected, "head", scatter_dimension=1, tiled=True).astype(BF16)
    done = vmem_call(
        functools.partial(score_grad_kernel, n_outer),
        (pick, live, outer),
        [keys, values, q_all, g_all, after(norm, projected)] + dots,
        (sds((n_local, PLEN, width), BF16),) + (mix_shape,) * n_outer,
        [turned_pair, pair_scratch, turned_pair, turned, acc_scratch],
        25,
        "score_grad",
    )
    key_back = swap(after(done[0], value_back).reshape(inner, tok_local, width))
    query_done = vmem_call(
        functools.partial(combine_query_kernel, n_outer),
        (),
        [after(done[1], output)] + partials(done[1:])[1:],
        sds((inner, rows, width), BF16),
        [],
        2,
        "combine_query",
    )
    query_grad = from_block(swap(after(query_done, key_back)))
    key_grad, value_grad = from_block(key_back), from_block(value_back)
    return (output, query_grad, key_grad, value_grad)


def solution(mesh):
    in_specs = (
        P("pas", "head"),
        P("pas", None),
        P(None, "head"),
        P(None, "head"),
        P("head", None),
        P("pas", "head"),
        P(),
        P(),
        P(),
    )
    out_specs = (P("pas", "head"), P("pas", "head"), P("pas", "head"), P("pas", "head"))
    return jax.shard_map(body, mesh=mesh, in_specs=in_specs, out_specs=out_specs, check_vma=False)
```

```python
import functools

import jax
import jax.numpy as jnp
from jax import lax
from jax.experimental import pallas as pl
from jax.experimental.pallas import tpu as pltpu
from jax.sharding import PartitionSpec as P

HEAD_DIM = 64
PLEN = 256
INNER = 4
GROUP = 8
LANES = 128
NEG_LARGE = -1e30
SCALE = HEAD_DIM ** (-0.5)

BF16 = jnp.bfloat16
F32 = jnp.float32

VMEM_LIMIT = 56 * 1024 * 1024


def params(semantics=None):
    return pltpu.CompilerParams(vmem_limit_bytes=VMEM_LIMIT, dimension_semantics=semantics)


def dot_nt(a, b):
    return lax.dot_general(a, b, (((1,), (1,)), ((), ())), preferred_element_type=F32)


def dot_nn(a, b):
    return lax.dot_general(a, b, (((1,), (0,)), ((), ())), preferred_element_type=F32)


def dot_tn(a, b):
    return lax.dot_general(a, b, (((0,), (0,)), ((), ())), preferred_element_type=F32)


def cost_us(time):
    return pl.CostEstimate(flops=int(time * 1e9), bytes_accessed=0, transcendentals=0)


def project_kernel(x_ref, w_ref, o_ref):
    width = o_ref.shape[2]
    for block in range(INNER):
        cols = slice(block * width, (block + 1) * width)
        o_ref[block] = dot_nn(x_ref[...], w_ref[:, cols]).astype(BF16)


def project(x, w):
    rows, depth = x.shape
    cols = w.shape[1]
    tile = 256
    return pl.pallas_call(
        project_kernel,
        grid=(rows // tile,),
        in_specs=[
            pl.BlockSpec((tile, depth), lambda m: (m, 0)),
            pl.BlockSpec((depth, cols), lambda m: (0, 0)),
        ],
        out_specs=pl.BlockSpec((INNER, tile, cols // INNER), lambda m: (0, m, 0)),
        out_shape=jax.ShapeDtypeStruct((INNER, rows, cols // INNER), BF16),
        compiler_params=params(("arbitrary",)),
        cost_estimate=cost_us(14),
        name="project",
    )(x, w)


def two_heads(block):
    lane = lax.broadcasted_iota(jnp.int32, block.shape, 1)
    zero = jnp.zeros_like(block)
    return jnp.concatenate(
        [jnp.where(lane < HEAD_DIM, block, zero), jnp.where(lane >= HEAD_DIM, block, zero)], axis=0
    )


def two_heads_turned(block):
    turned = jnp.transpose(block)
    feat = lax.broadcasted_iota(jnp.int32, turned.shape, 0)
    zero = jnp.zeros_like(turned)
    return jnp.concatenate(
        [jnp.where(feat < HEAD_DIM, turned, zero), jnp.where(feat >= HEAD_DIM, turned, zero)], axis=1
    )


def own_blocks(full):
    rows = full.shape[1] // 2
    return jnp.concatenate([full[:HEAD_DIM, :rows], full[HEAD_DIM:, rows:]], axis=0)


def route_kernel(n_local, outer_ref, slot_ref, list_ref, count_ref, pick_ref, live_ref):
    n_q, list_len = list_ref.shape
    first_slot = outer_ref[0] * n_local

    def question(ident, carry):
        found = jnp.int32(0)
        for e in range(list_len):
            slot = slot_ref[list_ref[ident, e]] - first_slot
            here = (slot >= 0) & (slot < n_local) & (e < count_ref[ident])
            pick_ref[ident, found] = jnp.where(here, slot, 0)
            found = found + here.astype(jnp.int32)
        for e in range(GROUP):
            pick_ref[ident, found + e] = 0
        live_ref[ident] = found
        return carry

    lax.fori_loop(0, n_q, question, 0)


def each_group(pick_ref, live_ref, ident, entries, start):
    live = live_ref[ident]

    def group(step, carry):
        first = step * GROUP
        slots = [pick_ref[ident, first + j] for j in range(GROUP)]
        return entries(carry, slots, [first + j < live for j in range(GROUP)])

    return lax.fori_loop(0, lax.div(live + (GROUP - 1), GROUP), group, start)


def pair_lanes(pair):
    return slice(pair * LANES, (pair + 1) * LANES)


def stacked(ref, slots, pair):
    return jnp.concatenate([ref[slot, :, pair_lanes(pair)] for slot in slots], axis=0)


def beside(ref, slots, pair):
    return jnp.concatenate([ref[slot, pair_lanes(pair), :] for slot in slots], axis=1)


def shifted(scores, lives, top):
    keys = scores.shape[0] // GROUP
    return [
        jnp.exp(scores[j * keys : (j + 1) * keys] - jnp.where(live, top, -NEG_LARGE))
        for j, live in enumerate(lives)
    ]


def stats_kernel(pick_ref, live_ref, k_ref, q_ref, o_ref, qt):
    n_q = q_ref.shape[0]
    n_pair = q_ref.shape[2] // LANES

    def question(ident, carry):
        for pair in range(n_pair):
            qt[pair] = two_heads_turned(q_ref[ident, :, pair_lanes(pair)])
        o_ref[0, ident] = jnp.full(o_ref.shape[2:], NEG_LARGE, F32)
        o_ref[1, ident] = jnp.zeros(o_ref.shape[2:], F32)

        def entries(state, slots, lives):
            for pair in range(n_pair):
                row = slice(pair, pair + 1)
                scores = [dot_nn(k_ref[slot, :, pair_lanes(pair)], qt[pair]) for slot in slots]
                old = o_ref[0, ident, row, :]
                new = old
                for j, live in enumerate(lives):
                    top = jnp.max(scores[j], axis=0, keepdims=True)
                    new = jnp.maximum(new, jnp.where(live, top, NEG_LARGE))
                add = o_ref[1, ident, row, :] * jnp.exp(old - new)
                for part, live in zip(scores, lives):
                    part = jnp.exp(part - jnp.where(live, new, -NEG_LARGE))
                    add = add + jnp.sum(part, axis=0, keepdims=True)
                o_ref[0, ident, row, :] = new
                o_ref[1, ident, row, :] = add
            return state

        each_group(pick_ref, live_ref, ident, entries, 0)
        return carry

    lax.fori_loop(0, n_q, question, 0)


def value_grad_kernel(pick_ref, live_ref, k_ref, q_ref, g_ref, st_ref, o_ref, qt, gbd, acc):
    n_q = q_ref.shape[0]
    n_pair = q_ref.shape[2] // LANES
    acc[...] = jnp.zeros_like(acc)

    def question(ident, carry):
        for pair in range(n_pair):
            qt[pair] = two_heads_turned(q_ref[ident, :, pair_lanes(pair)])
            gbd[pair] = two_heads(g_ref[ident, :, pair_lanes(pair)])

        def entries(state, slots, lives):
            for pair in range(n_pair):
                row = slice(pair, pair + 1)
                scores = dot_nn(stacked(k_ref, slots, pair), qt[pair])
                norm = st_ref[1, ident, row, :]
                probs = [
                    (part * norm).astype(BF16)
                    for part in shifted(scores, lives, st_ref[0, ident, row, :])
                ]
                term = dot_nn(jnp.concatenate(probs, axis=0), gbd[pair]).astype(BF16)
                for j, slot in enumerate(slots):
                    acc[slot, :, pair_lanes(pair)] += term[j * PLEN : (j + 1) * PLEN].astype(F32)
            return state

        each_group(pick_ref, live_ref, ident, entries, 0)
        return carry

    lax.fori_loop(0, n_q, question, 0)

    per = k_ref.shape[0] // o_ref.shape[0]

    def finish(owner, carry):
        for place in range(per):
            o_ref[owner, place * PLEN : (place + 1) * PLEN] = acc[owner * per + place].astype(BF16)
        return carry

    lax.fori_loop(0, o_ref.shape[0], finish, 0)


def turn(src_ref, dst_ref):
    def one(slot, carry):
        dst_ref[slot] = jnp.transpose(src_ref[slot])
        return carry

    lax.fori_loop(0, src_ref.shape[0], one, 0)


def context_kernel(n_outer, r, pick_ref, live_ref, outer_ref, k_ref, v_ref, q_ref, st_ref, o_ref, qt, vt):
    n_pair = q_ref.shape[2] // LANES
    first = lax.rem(outer_ref[0] + r, n_outer) * o_ref.shape[0]
    turn(v_ref, vt)

    def question(index, carry):
        ident = first + index
        for pair in range(n_pair):
            qt[pair] = two_heads_turned(q_ref[ident, :, pair_lanes(pair)])
        zero = jnp.zeros((LANES, 2 * q_ref.shape[1]), F32)

        def entries(sums, slots, lives):
            out = []
            for pair in range(n_pair):
                scores = dot_nn(stacked(k_ref, slots, pair), qt[pair])
                weights = [
                    part.astype(BF16)
                    for part in shifted(scores, lives, st_ref[0, ident, slice(pair, pair + 1), :])
                ]
                mix = dot_nn(beside(vt, slots, pair), jnp.concatenate(weights, axis=0))
                out.append(sums[pair] + mix)
            return tuple(out)

        sums = each_group(pick_ref, live_ref, ident, entries, (zero,) * n_pair)
        for pair in range(n_pair):
            o_ref[index, pair_lanes(pair), :] = own_blocks(sums[pair])
        return carry

    lax.fori_loop(0, o_ref.shape[0], question, 0)


def score_grad_kernel(n_outer, pick_ref, live_ref, outer_ref, k_ref, v_ref, q_ref, g_ref, st_ref, *rest):
    dot_refs, rest = rest[:n_outer], rest[n_outer:]
    dk_ref, rest = rest[0], rest[1:]
    dq_refs, (qt, qbd, gt, kt, acc_k) = rest[:n_outer], rest[n_outer:]
    n_q = q_ref.shape[0]
    inner = n_q // n_outer
    n_pair = q_ref.shape[2] // LANES
    turn(k_ref, kt)
    acc_k[...] = jnp.zeros_like(acc_k)

    def question(dot_ref, dq_ref, outer, index, carry):
        ident = outer * inner + index
        for pair in range(n_pair):
            qbd[pair] = two_heads(q_ref[ident, :, pair_lanes(pair)])
            qt[pair] = two_heads_turned(q_ref[ident, :, pair_lanes(pair)])
            gt[pair] = two_heads_turned(g_ref[ident, :, pair_lanes(pair)])
        zero = jnp.zeros((LANES, 2 * q_ref.shape[1]), F32)

        def entries(sums, slots, lives):
            out = []
            for pair in range(n_pair):
                row = slice(pair, pair + 1)
                scores = dot_nn(stacked(k_ref, slots, pair), qt[pair])
                dprob = dot_nn(stacked(v_ref, slots, pair), gt[pair])
                norm = st_ref[1, ident, row, :]
                dots = dot_ref[index, row, :]
                dscore = [
                    (part * norm * (dprob[j * PLEN : (j + 1) * PLEN] - dots)).astype(BF16)
                    for j, part in enumerate(shifted(scores, lives, st_ref[0, ident, row, :]))
                ]
                dscore = jnp.concatenate(dscore, axis=0)
                term = dot_nn(dscore, qbd[pair]).astype(BF16)
                for j, slot in enumerate(slots):
                    acc_k[slot, :, pair_lanes(pair)] += term[j * PLEN : (j + 1) * PLEN].astype(F32)
                out.append(sums[pair] + dot_nn(beside(kt, slots, pair), dscore))
            return tuple(out)

        sums = each_group(pick_ref, live_ref, ident, entries, (zero,) * n_pair)
        for pair in range(n_pair):
            dq_ref[index, pair_lanes(pair), :] = own_blocks(sums[pair])
        return carry

    for r in reversed(range(n_outer)):
        outer = lax.rem(outer_ref[0] + r, n_outer)
        lax.fori_loop(0, inner, functools.partial(question, dot_refs[r], dq_refs[r], outer), 0)

    def finish(slot, carry):
        dk_ref[slot] = acc_k[slot].astype(BF16)
        return carry

    lax.fori_loop(0, k_ref.shape[0], finish, 0)


def merge_kernel(n_outer, *refs):
    parts, o_ref = refs[:n_outer], refs[n_outer]
    top = parts[0][0]
    for part in parts[1:]:
        top = jnp.maximum(top, part[0])
    total = parts[0][1] * jnp.exp(parts[0][0] - top)
    for part in parts[1:]:
        total = total + part[1] * jnp.exp(part[0] - top)
    o_ref[0] = top
    o_ref[1] = 1.0 / total
    o_ref[2] = total


def combine_context_kernel(n_parts, outer_ref, *refs):
    parts, (st_ref, g_ref, _, o_ref, dot_ref, ctx_ref, sem) = refs[:n_parts], refs[n_parts:]
    width = g_ref.shape[2]
    inner, rows = ctx_ref.shape[0], ctx_ref.shape[1]
    first = outer_ref[0] * inner
    for q in range(inner):
        mix = parts[0][q]
        for part in parts[1:]:
            mix = mix + part[q]
        grad = jnp.transpose(g_ref[first + q].astype(F32))
        pieces = []
        for head in range(width // HEAD_DIM):
            feats = slice(head * HEAD_DIM, (head + 1) * HEAD_DIM)
            pair, lanes = head // 2, slice((head % 2) * rows, (head % 2 + 1) * rows)
            total = st_ref[2, first + q, pair : pair + 1, lanes]
            ctx = (mix[feats] / total).astype(BF16).astype(F32)
            dot_ref[q, pair : pair + 1, lanes] = jnp.sum(grad[feats] * ctx, axis=0, keepdims=True)
            pieces.append(ctx)
        ctx_ref[q] = jnp.transpose(jnp.concatenate(pieces, axis=0)).astype(BF16)
    copy = pltpu.make_async_copy(ctx_ref, o_ref.at[:, pl.ds(o_ref.shape[1] - rows, rows), :], sem)
    copy.start()
    copy.wait()


def combine_query_kernel(n_parts, *refs):
    parts, o_ref = refs[:n_parts], refs[n_parts]
    for q in range(o_ref.shape[0]):
        mix = parts[0][q]
        for part in parts[1:]:
            mix = mix + part[q]
        o_ref[q] = jnp.transpose(mix * SCALE).astype(BF16)


def spread_kernel(x_ref, o_ref):
    width = o_ref.shape[2]
    for block in range(INNER):
        part = x_ref[:, block * width : (block + 1) * width] * jnp.asarray(SCALE, BF16)
        for outer in range(o_ref.shape[0] // INNER):
            o_ref[outer * INNER + block] = part


def context_grad_kernel(x_ref, w_ref, o_ref):
    part = dot_nt(x_ref[...], w_ref[...]).astype(BF16)
    for outer in range(o_ref.shape[0]):
        o_ref[outer, 0] = part


def context_grad_blocks(x, w, n_outer, width):
    rows, depth = x.shape
    return pl.pallas_call(
        context_grad_kernel,
        grid=(INNER,),
        in_specs=[
            pl.BlockSpec((rows, depth), lambda j: (0, 0)),
            pl.BlockSpec((width, depth), lambda j: (j, 0)),
        ],
        out_specs=pl.BlockSpec((n_outer, 1, rows, width), lambda j: (0, j, 0, 0)),
        out_shape=jax.ShapeDtypeStruct((n_outer, INNER, rows, width), BF16),
        compiler_params=params(("arbitrary",)),
        cost_estimate=cost_us(5),
        name="context_grad",
    )(x, w)


def out_project_kernel(x_ref, w_ref, o_ref):
    step = pl.program_id(0)
    part = dot_nn(x_ref[0], w_ref[...])

    @pl.when(step == 0)
    def _():
        o_ref[...] = part

    @pl.when(step > 0)
    def _():
        o_ref[...] += part


def out_project(x, rows, w):
    blocks, length, width = x.shape
    cols = w.shape[1]
    return pl.pallas_call(
        out_project_kernel,
        grid=(blocks,),
        in_specs=[
            pl.BlockSpec((1, rows, width), lambda j: (j, length // rows - 1, 0)),
            pl.BlockSpec((width, cols), lambda j: (j, 0)),
        ],
        out_specs=pl.BlockSpec((rows, cols), lambda j: (0, 0)),
        out_shape=jax.ShapeDtypeStruct((rows, cols), F32),
        compiler_params=params(("arbitrary",)),
        cost_estimate=cost_us(1),
        name="out_project",
    )(x, w)


def collect_kernel(x_ref, o_ref):
    width = x_ref.shape[2]
    for block in range(x_ref.shape[0]):
        o_ref[:, block * width : (block + 1) * width] = x_ref[block]


def collect(x, rows):
    blocks, _, width = x.shape
    tile = min(rows, 512)
    return pl.pallas_call(
        collect_kernel,
        grid=(rows // tile,),
        in_specs=[pl.BlockSpec((blocks, tile, width), lambda m: (0, m, 0))],
        out_specs=pl.BlockSpec((tile, blocks * width), lambda m: (m, 0)),
        out_shape=jax.ShapeDtypeStruct((rows, blocks * width), x.dtype),
        compiler_params=params(("arbitrary",)),
        cost_estimate=cost_us(1),
        name="collect",
    )(x)


def vmem_call(kernel, scalars, arrays, out_shape, scratch, time, name):
    smem = pl.BlockSpec(memory_space=pltpu.SMEM)
    vmem = pl.BlockSpec(memory_space=pltpu.VMEM)
    return pl.pallas_call(
        kernel,
        in_specs=[smem] * len(scalars) + [vmem] * len(arrays),
        out_specs=jax.tree.map(lambda _: vmem, out_shape),
        out_shape=out_shape,
        scratch_shapes=scratch,
        compiler_params=params(),
        cost_estimate=cost_us(time),
        name=name,
    )(*scalars, *arrays)


def route(outer, slot_of, passage_lists, list_counts, n_local):
    smem = pl.BlockSpec(memory_space=pltpu.SMEM)
    n_q, list_len = passage_lists.shape
    return pl.pallas_call(
        functools.partial(route_kernel, n_local),
        in_specs=[smem] * 4,
        out_specs=(smem, smem),
        out_shape=(
            jax.ShapeDtypeStruct((n_q, list_len + GROUP), jnp.int32),
            jax.ShapeDtypeStruct((n_q,), jnp.int32),
        ),
        cost_estimate=cost_us(3),
        name="route",
    )(outer, slot_of, passage_lists, list_counts)


def after(value, *others):
    return lax.optimization_barrier((value,) + others)[0]


def body(
    queries,
    encoded,
    key_weight,
    value_weight,
    out_weight,
    out_grad,
    slot_of,
    passage_lists,
    list_counts,
):
    head_width = key_weight.shape[1]
    rows = queries.shape[0]
    tok_local = encoded.shape[0]
    n_pas = lax.axis_size("pas")
    inner = INNER
    n_outer = n_pas // inner
    width = head_width // inner
    n_pair = width // LANES
    n_local = inner * (tok_local // PLEN)
    n_q = n_pas
    outer = (lax.axis_index("pas") // inner).astype(jnp.int32).reshape(1)
    groups = [[o * inner + i for i in range(inner)] for o in range(n_outer)]
    sds = jax.ShapeDtypeStruct

    def swap(x):
        return lax.all_to_all(
            x, "pas", split_axis=0, concat_axis=0, tiled=True, axis_index_groups=groups
        )

    def swap_all(x):
        return lax.all_to_all(x, "pas", split_axis=0, concat_axis=0, tiled=True)

    def to_outer(x, r):
        return lax.ppermute(
            x,
            "pas",
            [(o * inner + i, ((o + r) % n_outer) * inner + i) for o in range(n_outer) for i in range(inner)],
        )

    def partials(parts):
        return [parts[0]] + [to_outer(parts[r], r) for r in range(1, n_outer)]

    q_spread = vmem_call(spread_kernel, (), (queries,), sds((n_q, rows, width), BF16), [], 1.5, "spread")
    q_all = swap_all(q_spread)
    grad_rows = lax.all_gather(out_grad, "head", axis=1, tiled=True)

    key_part = project(after(encoded, q_spread), key_weight)
    keys = swap(key_part).reshape(n_local, PLEN, width)
    value_part = project(after(encoded, key_part, grad_rows), value_weight)
    g_spread = context_grad_blocks(after(grad_rows, value_part), out_weight, n_outer, width)
    g_spread = g_spread.reshape(n_q, rows, width)
    pick, live = route(after(outer, value_part), slot_of, passage_lists, list_counts, n_local)
    values = swap(after(value_part, g_spread, pick)).reshape(n_local, PLEN, width)

    pair_scratch = pltpu.VMEM((n_pair, 2 * rows, LANES), BF16)
    turned_pair = pltpu.VMEM((n_pair, LANES, 2 * rows), BF16)
    acc_scratch = pltpu.VMEM((n_local, PLEN, width), F32)
    turned = pltpu.VMEM((n_local, width, PLEN), BF16)
    stat_shape = (n_q, n_pair, 2 * rows)
    mix_shape = sds((inner, width, rows), F32)

    stats = vmem_call(
        stats_kernel,
        (pick, live),
        (keys, q_all),
        sds((2,) + stat_shape, F32),
        [turned_pair],
        13,
        "stats",
    )
    norm = vmem_call(
        functools.partial(merge_kernel, n_outer),
        (),
        [stats] + [to_outer(stats, r) for r in range(1, n_outer)],
        sds((3,) + stat_shape, F32),
        [],
        1,
        "merge",
    )
    g_all = swap_all(after(g_spread, values))
    mixes, norm_then = [None] * n_outer, norm
    for r in reversed(range(n_outer)):
        mixes[r] = vmem_call(
            functools.partial(context_kernel, n_outer, r),
            (pick, live, outer),
            (keys, values, q_all, norm_then),
            mix_shape,
            [turned_pair, turned],
            5 if r == 0 else 14,
            "context",
        )
        norm_then = after(norm, mixes[r], g_all)
    value_done = vmem_call(
        value_grad_kernel,
        (pick, live),
        (keys, q_all, g_all, norm_then),
        sds((inner, tok_local + rows, width), BF16),
        [turned_pair, pair_scratch, acc_scratch],
        5,
        "value_grad",
    )
    smem, vmem = pl.BlockSpec(memory_space=pltpu.SMEM), pl.BlockSpec(memory_space=pltpu.VMEM)
    anywhere = pl.BlockSpec(memory_space=pl.ANY)
    packed, grad_dot = pl.pallas_call(
        functools.partial(combine_context_kernel, n_outer),
        in_specs=[smem] + [vmem] * (n_outer + 2) + [anywhere],
        out_specs=(anywhere, vmem),
        out_shape=(
            sds((inner, tok_local + rows, width), BF16),
            sds((inner, n_pair, 2 * rows), F32),
        ),
        scratch_shapes=[pltpu.VMEM((inner, rows, width), BF16), pltpu.SemaphoreType.DMA],
        input_output_aliases={n_outer + 3: 0},
        compiler_params=params(),
        cost_estimate=cost_us(3),
        name="combine_context",
    )(outer, *partials([after(mix, g_all) for mix in mixes]), norm, g_all, value_done)
    dots = [grad_dot] + [to_outer(grad_dot, n_outer - r) for r in range(1, n_outer)]
    packed_back = swap(after(packed, *dots[1:]))
    value_grad = collect(packed_back, tok_local)
    done = vmem_call(
        functools.partial(score_grad_kernel, n_outer),
        (pick, live, outer),
        [keys, values, q_all, g_all, norm] + dots,
        (sds((n_local, PLEN, width), BF16),) + (mix_shape,) * n_outer,
        [turned_pair, pair_scratch, turned_pair, turned, acc_scratch],
        25,
        "score_grad",
    )
    projected = out_project(after(packed_back, done[0]), rows, out_weight)
    output = lax.psum_scatter(projected, "head", scatter_dimension=1, tiled=True).astype(BF16)
    key_back = swap(after(done[0], projected).reshape(inner, tok_local, width))
    query_done = vmem_call(
        functools.partial(combine_query_kernel, n_outer),
        (),
        [after(done[1], value_grad)] + partials(done[1:])[1:],
        sds((inner, rows, width), BF16),
        [],
        40,
        "combine_query",
    )
    query_grad = collect(swap(after(query_done, key_back)), rows)
    key_grad = collect(key_back, tok_local)
    return (output, query_grad, key_grad, value_grad)


def solution(mesh):
    in_specs = (
        P("pas", "head"),
        P("pas", None),
        P(None, "head"),
        P(None, "head"),
        P("head", None),
        P("pas", "head"),
        P(),
        P(),
        P(),
    )
    out_specs = (P("pas", "head"), P("pas", "head"), P("pas", "head"), P("pas", "head"))
    return jax.shard_map(body, mesh=mesh, in_specs=in_specs, out_specs=out_specs, check_vma=False)
```

```python
import functools

import jax
import jax.numpy as jnp
from jax import lax
from jax.experimental import pallas as pl
from jax.experimental.pallas import tpu as pltpu
from jax.sharding import PartitionSpec as P

HEAD_DIM = 64
PLEN = 256
INNER = 4
GROUP = 8
LANES = 128
NEG_LARGE = -1e30
SCALE = HEAD_DIM ** (-0.5)

BF16 = jnp.bfloat16
F32 = jnp.float32

VMEM_LIMIT = 56 * 1024 * 1024


def params(semantics=None):
    return pltpu.CompilerParams(vmem_limit_bytes=VMEM_LIMIT, dimension_semantics=semantics)


def dot_nt(a, b):
    return lax.dot_general(a, b, (((1,), (1,)), ((), ())), preferred_element_type=F32)


def dot_nn(a, b):
    return lax.dot_general(a, b, (((1,), (0,)), ((), ())), preferred_element_type=F32)


def dot_tn(a, b):
    return lax.dot_general(a, b, (((0,), (0,)), ((), ())), preferred_element_type=F32)


def cost_us(time):
    return pl.CostEstimate(flops=int(time * 1e9), bytes_accessed=0, transcendentals=0)


def project_kernel(x_ref, w_ref, o_ref):
    width = o_ref.shape[2]
    for block in range(INNER):
        cols = slice(block * width, (block + 1) * width)
        o_ref[block] = dot_nn(x_ref[...], w_ref[:, cols]).astype(BF16)


def project(x, w):
    rows, depth = x.shape
    cols = w.shape[1]
    tile = 256
    return pl.pallas_call(
        project_kernel,
        grid=(rows // tile,),
        in_specs=[
            pl.BlockSpec((tile, depth), lambda m: (m, 0)),
            pl.BlockSpec((depth, cols), lambda m: (0, 0)),
        ],
        out_specs=pl.BlockSpec((INNER, tile, cols // INNER), lambda m: (0, m, 0)),
        out_shape=jax.ShapeDtypeStruct((INNER, rows, cols // INNER), BF16),
        compiler_params=params(("arbitrary",)),
        cost_estimate=cost_us(14),
        name="project",
    )(x, w)


def two_heads(block):
    lane = lax.broadcasted_iota(jnp.int32, block.shape, 1)
    zero = jnp.zeros_like(block)
    return jnp.concatenate(
        [jnp.where(lane < HEAD_DIM, block, zero), jnp.where(lane >= HEAD_DIM, block, zero)], axis=0
    )


def two_heads_turned(block):
    turned = jnp.transpose(block)
    feat = lax.broadcasted_iota(jnp.int32, turned.shape, 0)
    zero = jnp.zeros_like(turned)
    return jnp.concatenate(
        [jnp.where(feat < HEAD_DIM, turned, zero), jnp.where(feat >= HEAD_DIM, turned, zero)], axis=1
    )


def own_blocks(full):
    rows = full.shape[1] // 2
    return jnp.concatenate([full[:HEAD_DIM, :rows], full[HEAD_DIM:, rows:]], axis=0)


def route_kernel(n_local, outer_ref, slot_ref, list_ref, count_ref, pick_ref, live_ref):
    n_q, list_len = list_ref.shape
    first_slot = outer_ref[0] * n_local

    def question(ident, carry):
        found = jnp.int32(0)
        for e in range(list_len):
            slot = slot_ref[list_ref[ident, e]] - first_slot
            here = (slot >= 0) & (slot < n_local) & (e < count_ref[ident])
            pick_ref[ident, found] = jnp.where(here, slot, 0)
            found = found + here.astype(jnp.int32)
        for e in range(GROUP):
            pick_ref[ident, found + e] = 0
        live_ref[ident] = found
        return carry

    lax.fori_loop(0, n_q, question, 0)


def each_group(pick_ref, live_ref, ident, entries, start):
    live = live_ref[ident]

    def group(step, carry):
        first = step * GROUP
        slots = [pick_ref[ident, first + j] for j in range(GROUP)]
        return entries(carry, slots, [first + j < live for j in range(GROUP)])

    return lax.fori_loop(0, lax.div(live + (GROUP - 1), GROUP), group, start)


def pair_lanes(pair):
    return slice(pair * LANES, (pair + 1) * LANES)


def stacked(ref, slots, pair):
    return jnp.concatenate([ref[slot, :, pair_lanes(pair)] for slot in slots], axis=0)


def beside(ref, slots, pair):
    return jnp.concatenate([ref[slot, pair_lanes(pair), :] for slot in slots], axis=1)


def shifted(scores, lives, top):
    keys = scores.shape[0] // GROUP
    return [
        jnp.exp(scores[j * keys : (j + 1) * keys] - jnp.where(live, top, -NEG_LARGE))
        for j, live in enumerate(lives)
    ]


def stats_kernel(pick_ref, live_ref, k_ref, q_ref, o_ref, qt):
    n_q = q_ref.shape[0]
    n_pair = q_ref.shape[2] // LANES

    def question(ident, carry):
        for pair in range(n_pair):
            qt[pair] = two_heads_turned(q_ref[ident, :, pair_lanes(pair)])
        o_ref[0, ident] = jnp.full(o_ref.shape[2:], NEG_LARGE, F32)
        o_ref[1, ident] = jnp.zeros(o_ref.shape[2:], F32)

        def entries(state, slots, lives):
            for pair in range(n_pair):
                row = slice(pair, pair + 1)
                scores = [dot_nn(k_ref[slot, :, pair_lanes(pair)], qt[pair]) for slot in slots]
                old = o_ref[0, ident, row, :]
                new = old
                for j, live in enumerate(lives):
                    top = jnp.max(scores[j], axis=0, keepdims=True)
                    new = jnp.maximum(new, jnp.where(live, top, NEG_LARGE))
                add = o_ref[1, ident, row, :] * jnp.exp(old - new)
                for part, live in zip(scores, lives):
                    part = jnp.exp(part - jnp.where(live, new, -NEG_LARGE))
                    add = add + jnp.sum(part, axis=0, keepdims=True)
                o_ref[0, ident, row, :] = new
                o_ref[1, ident, row, :] = add
            return state

        each_group(pick_ref, live_ref, ident, entries, 0)
        return carry

    lax.fori_loop(0, n_q, question, 0)


def value_grad_kernel(pick_ref, live_ref, k_ref, q_ref, g_ref, st_ref, o_ref, qt, gbd, acc):
    n_q = q_ref.shape[0]
    n_pair = q_ref.shape[2] // LANES
    acc[...] = jnp.zeros_like(acc)

    def question(ident, carry):
        for pair in range(n_pair):
            qt[pair] = two_heads_turned(q_ref[ident, :, pair_lanes(pair)])
            gbd[pair] = two_heads(g_ref[ident, :, pair_lanes(pair)])

        def entries(state, slots, lives):
            for pair in range(n_pair):
                row = slice(pair, pair + 1)
                scores = dot_nn(stacked(k_ref, slots, pair), qt[pair])
                norm = st_ref[1, ident, row, :]
                probs = [
                    (part * norm).astype(BF16)
                    for part in shifted(scores, lives, st_ref[0, ident, row, :])
                ]
                term = dot_nn(jnp.concatenate(probs, axis=0), gbd[pair]).astype(BF16)
                for j, slot in enumerate(slots):
                    acc[slot, :, pair_lanes(pair)] += term[j * PLEN : (j + 1) * PLEN].astype(F32)
            return state

        each_group(pick_ref, live_ref, ident, entries, 0)
        return carry

    lax.fori_loop(0, n_q, question, 0)

    per = k_ref.shape[0] // o_ref.shape[0]

    def finish(owner, carry):
        for place in range(per):
            o_ref[owner, place * PLEN : (place + 1) * PLEN] = acc[owner * per + place].astype(BF16)
        return carry

    lax.fori_loop(0, o_ref.shape[0], finish, 0)


def turn(src_ref, dst_ref):
    def one(slot, carry):
        dst_ref[slot] = jnp.transpose(src_ref[slot])
        return carry

    lax.fori_loop(0, src_ref.shape[0], one, 0)


def context_kernel(n_outer, r, pick_ref, live_ref, outer_ref, k_ref, v_ref, q_ref, st_ref, o_ref, qt, vt):
    n_pair = q_ref.shape[2] // LANES
    first = lax.rem(outer_ref[0] + r, n_outer) * o_ref.shape[0]
    turn(v_ref, vt)

    def question(index, carry):
        ident = first + index
        for pair in range(n_pair):
            qt[pair] = two_heads_turned(q_ref[ident, :, pair_lanes(pair)])
        zero = jnp.zeros((LANES, 2 * q_ref.shape[1]), F32)

        def entries(sums, slots, lives):
            out = []
            for pair in range(n_pair):
                scores = dot_nn(stacked(k_ref, slots, pair), qt[pair])
                weights = [
                    part.astype(BF16)
                    for part in shifted(scores, lives, st_ref[0, ident, slice(pair, pair + 1), :])
                ]
                mix = dot_nn(beside(vt, slots, pair), jnp.concatenate(weights, axis=0))
                out.append(sums[pair] + mix)
            return tuple(out)

        sums = each_group(pick_ref, live_ref, ident, entries, (zero,) * n_pair)
        for pair in range(n_pair):
            o_ref[index, pair_lanes(pair), :] = own_blocks(sums[pair])
        return carry

    lax.fori_loop(0, o_ref.shape[0], question, 0)


def score_grad_kernel(n_outer, pick_ref, live_ref, outer_ref, k_ref, v_ref, q_ref, g_ref, st_ref, *rest):
    dot_refs, rest = rest[:n_outer], rest[n_outer:]
    dk_ref, rest = rest[0], rest[1:]
    dq_refs, (qt, qbd, gt, kt, acc_k) = rest[:n_outer], rest[n_outer:]
    n_q = q_ref.shape[0]
    inner = n_q // n_outer
    n_pair = q_ref.shape[2] // LANES
    turn(k_ref, kt)
    acc_k[...] = jnp.zeros_like(acc_k)

    def question(dot_ref, dq_ref, outer, index, carry):
        ident = outer * inner + index
        for pair in range(n_pair):
            qbd[pair] = two_heads(q_ref[ident, :, pair_lanes(pair)])
            qt[pair] = two_heads_turned(q_ref[ident, :, pair_lanes(pair)])
            gt[pair] = two_heads_turned(g_ref[ident, :, pair_lanes(pair)])
        zero = jnp.zeros((LANES, 2 * q_ref.shape[1]), F32)

        def entries(sums, slots, lives):
            out = []
            for pair in range(n_pair):
                row = slice(pair, pair + 1)
                scores = dot_nn(stacked(k_ref, slots, pair), qt[pair])
                dprob = dot_nn(stacked(v_ref, slots, pair), gt[pair])
                norm = st_ref[1, ident, row, :]
                dots = dot_ref[index, row, :]
                dscore = [
                    (part * norm * (dprob[j * PLEN : (j + 1) * PLEN] - dots)).astype(BF16)
                    for j, part in enumerate(shifted(scores, lives, st_ref[0, ident, row, :]))
                ]
                dscore = jnp.concatenate(dscore, axis=0)
                term = dot_nn(dscore, qbd[pair]).astype(BF16)
                for j, slot in enumerate(slots):
                    acc_k[slot, :, pair_lanes(pair)] += term[j * PLEN : (j + 1) * PLEN].astype(F32)
                out.append(sums[pair] + dot_nn(beside(kt, slots, pair), dscore))
            return tuple(out)

        sums = each_group(pick_ref, live_ref, ident, entries, (zero,) * n_pair)
        for pair in range(n_pair):
            dq_ref[index, pair_lanes(pair), :] = own_blocks(sums[pair])
        return carry

    for r in reversed(range(n_outer)):
        outer = lax.rem(outer_ref[0] + r, n_outer)
        lax.fori_loop(0, inner, functools.partial(question, dot_refs[r], dq_refs[r], outer), 0)

    def finish(slot, carry):
        dk_ref[slot] = acc_k[slot].astype(BF16)
        return carry

    lax.fori_loop(0, k_ref.shape[0], finish, 0)


def merge_kernel(n_outer, *refs):
    parts, o_ref = refs[:n_outer], refs[n_outer]
    top = parts[0][0]
    for part in parts[1:]:
        top = jnp.maximum(top, part[0])
    total = parts[0][1] * jnp.exp(parts[0][0] - top)
    for part in parts[1:]:
        total = total + part[1] * jnp.exp(part[0] - top)
    o_ref[0] = top
    o_ref[1] = 1.0 / total
    o_ref[2] = total


def combine_context_kernel(n_parts, outer_ref, *refs):
    parts, (st_ref, g_ref, _, o_ref, dot_ref, ctx_ref, sem) = refs[:n_parts], refs[n_parts:]
    width = g_ref.shape[2]
    inner, rows = ctx_ref.shape[0], ctx_ref.shape[1]
    first = outer_ref[0] * inner
    for q in range(inner):
        mix = parts[0][q]
        for part in parts[1:]:
            mix = mix + part[q]
        grad = jnp.transpose(g_ref[first + q].astype(F32))
        pieces = []
        for head in range(width // HEAD_DIM):
            feats = slice(head * HEAD_DIM, (head + 1) * HEAD_DIM)
            pair, lanes = head // 2, slice((head % 2) * rows, (head % 2 + 1) * rows)
            total = st_ref[2, first + q, pair : pair + 1, lanes]
            ctx = (mix[feats] / total).astype(BF16).astype(F32)
            dot_ref[q, pair : pair + 1, lanes] = jnp.sum(grad[feats] * ctx, axis=0, keepdims=True)
            pieces.append(ctx)
        ctx_ref[q] = jnp.transpose(jnp.concatenate(pieces, axis=0)).astype(BF16)
    copy = pltpu.make_async_copy(ctx_ref, o_ref.at[:, pl.ds(o_ref.shape[1] - rows, rows), :], sem)
    copy.start()
    copy.wait()


def combine_query_kernel(n_parts, *refs):
    parts, o_ref = refs[:n_parts], refs[n_parts]
    for q in range(o_ref.shape[0]):
        mix = parts[0][q]
        for part in parts[1:]:
            mix = mix + part[q]
        o_ref[q] = jnp.transpose(mix * SCALE).astype(BF16)


def spread_kernel(x_ref, o_ref):
    width = o_ref.shape[2]
    for block in range(INNER):
        part = x_ref[:, block * width : (block + 1) * width] * jnp.asarray(SCALE, BF16)
        for outer in range(o_ref.shape[0] // INNER):
            o_ref[outer * INNER + block] = part


def context_grad_kernel(x_ref, w_ref, o_ref):
    part = dot_nt(x_ref[...], w_ref[...]).astype(BF16)
    for outer in range(o_ref.shape[0]):
        o_ref[outer, 0] = part


def context_grad_blocks(x, w, n_outer, width):
    rows, depth = x.shape
    return pl.pallas_call(
        context_grad_kernel,
        grid=(INNER,),
        in_specs=[
            pl.BlockSpec((rows, depth), lambda j: (0, 0)),
            pl.BlockSpec((width, depth), lambda j: (j, 0)),
        ],
        out_specs=pl.BlockSpec((n_outer, 1, rows, width), lambda j: (0, j, 0, 0)),
        out_shape=jax.ShapeDtypeStruct((n_outer, INNER, rows, width), BF16),
        compiler_params=params(("arbitrary",)),
        cost_estimate=cost_us(5),
        name="context_grad",
    )(x, w)


def out_project_kernel(x_ref, w_ref, o_ref):
    step = pl.program_id(0)
    part = dot_nn(x_ref[0], w_ref[...])

    @pl.when(step == 0)
    def _():
        o_ref[...] = part

    @pl.when(step > 0)
    def _():
        o_ref[...] += part


def out_project(x, rows, w):
    blocks, length, width = x.shape
    cols = w.shape[1]
    return pl.pallas_call(
        out_project_kernel,
        grid=(blocks,),
        in_specs=[
            pl.BlockSpec((1, rows, width), lambda j: (j, length // rows - 1, 0)),
            pl.BlockSpec((width, cols), lambda j: (j, 0)),
        ],
        out_specs=pl.BlockSpec((rows, cols), lambda j: (0, 0)),
        out_shape=jax.ShapeDtypeStruct((rows, cols), F32),
        compiler_params=params(("arbitrary",)),
        cost_estimate=cost_us(1),
        name="out_project",
    )(x, w)


def collect_kernel(x_ref, o_ref):
    width = x_ref.shape[2]
    for block in range(x_ref.shape[0]):
        o_ref[:, block * width : (block + 1) * width] = x_ref[block]


def collect(x, rows):
    blocks, _, width = x.shape
    tile = min(rows, 512)
    return pl.pallas_call(
        collect_kernel,
        grid=(rows // tile,),
        in_specs=[pl.BlockSpec((blocks, tile, width), lambda m: (0, m, 0))],
        out_specs=pl.BlockSpec((tile, blocks * width), lambda m: (m, 0)),
        out_shape=jax.ShapeDtypeStruct((rows, blocks * width), x.dtype),
        compiler_params=params(("arbitrary",)),
        cost_estimate=cost_us(1),
        name="collect",
    )(x)


def vmem_call(kernel, scalars, arrays, out_shape, scratch, time, name):
    smem = pl.BlockSpec(memory_space=pltpu.SMEM)
    vmem = pl.BlockSpec(memory_space=pltpu.VMEM)
    return pl.pallas_call(
        kernel,
        in_specs=[smem] * len(scalars) + [vmem] * len(arrays),
        out_specs=jax.tree.map(lambda _: vmem, out_shape),
        out_shape=out_shape,
        scratch_shapes=scratch,
        compiler_params=params(),
        cost_estimate=cost_us(time),
        name=name,
    )(*scalars, *arrays)


def route(outer, slot_of, passage_lists, list_counts, n_local):
    smem = pl.BlockSpec(memory_space=pltpu.SMEM)
    n_q, list_len = passage_lists.shape
    return pl.pallas_call(
        functools.partial(route_kernel, n_local),
        in_specs=[smem] * 4,
        out_specs=(smem, smem),
        out_shape=(
            jax.ShapeDtypeStruct((n_q, list_len + GROUP), jnp.int32),
            jax.ShapeDtypeStruct((n_q,), jnp.int32),
        ),
        cost_estimate=cost_us(3),
        name="route",
    )(outer, slot_of, passage_lists, list_counts)


def after(value, *others):
    return lax.optimization_barrier((value,) + others)[0]


def body(
    queries,
    encoded,
    key_weight,
    value_weight,
    out_weight,
    out_grad,
    slot_of,
    passage_lists,
    list_counts,
):
    head_width = key_weight.shape[1]
    rows = queries.shape[0]
    tok_local = encoded.shape[0]
    n_pas = lax.axis_size("pas")
    inner = INNER
    n_outer = n_pas // inner
    width = head_width // inner
    n_pair = width // LANES
    n_local = inner * (tok_local // PLEN)
    n_q = n_pas
    outer = (lax.axis_index("pas") // inner).astype(jnp.int32).reshape(1)
    groups = [[o * inner + i for i in range(inner)] for o in range(n_outer)]
    sds = jax.ShapeDtypeStruct

    def swap(x):
        return lax.all_to_all(
            x, "pas", split_axis=0, concat_axis=0, tiled=True, axis_index_groups=groups
        )

    def swap_all(x):
        return lax.all_to_all(x, "pas", split_axis=0, concat_axis=0, tiled=True)

    def to_outer(x, r):
        return lax.ppermute(
            x,
            "pas",
            [(o * inner + i, ((o + r) % n_outer) * inner + i) for o in range(n_outer) for i in range(inner)],
        )

    def partials(parts):
        return [parts[0]] + [to_outer(parts[r], r) for r in range(1, n_outer)]

    q_spread = vmem_call(spread_kernel, (), (queries,), sds((n_q, rows, width), BF16), [], 1.5, "spread")
    q_all = swap_all(q_spread)
    grad_rows = lax.all_gather(out_grad, "head", axis=1, tiled=True)

    key_part = project(after(encoded, q_spread), key_weight)
    keys = swap(key_part).reshape(n_local, PLEN, width)
    value_part = project(after(encoded, key_part, grad_rows), value_weight)
    g_spread = context_grad_blocks(after(grad_rows, value_part), out_weight, n_outer, width)
    g_spread = g_spread.reshape(n_q, rows, width)
    pick, live = route(after(outer, value_part), slot_of, passage_lists, list_counts, n_local)
    values = swap(after(value_part, g_spread, pick)).reshape(n_local, PLEN, width)

    pair_scratch = pltpu.VMEM((n_pair, 2 * rows, LANES), BF16)
    turned_pair = pltpu.VMEM((n_pair, LANES, 2 * rows), BF16)
    acc_scratch = pltpu.VMEM((n_local, PLEN, width), F32)
    turned = pltpu.VMEM((n_local, width, PLEN), BF16)
    stat_shape = (n_q, n_pair, 2 * rows)
    mix_shape = sds((inner, width, rows), F32)

    stats = vmem_call(
        stats_kernel,
        (pick, live),
        (keys, q_all),
        sds((2,) + stat_shape, F32),
        [turned_pair],
        13,
        "stats",
    )
    norm = vmem_call(
        functools.partial(merge_kernel, n_outer),
        (),
        [stats] + [to_outer(stats, r) for r in range(1, n_outer)],
        sds((3,) + stat_shape, F32),
        [],
        1,
        "merge",
    )
    g_all = swap_all(after(g_spread, values))
    mixes, norm_then = [None] * n_outer, norm
    for r in reversed(range(n_outer)):
        mixes[r] = vmem_call(
            functools.partial(context_kernel, n_outer, r),
            (pick, live, outer),
            (keys, values, q_all, norm_then),
            mix_shape,
            [turned_pair, turned],
            5 if r == 0 else 14,
            "context",
        )
        norm_then = after(norm, mixes[r], g_all)
    value_done = vmem_call(
        value_grad_kernel,
        (pick, live),
        (keys, q_all, g_all, norm_then),
        sds((inner, tok_local + rows, width), BF16),
        [turned_pair, pair_scratch, acc_scratch],
        5,
        "value_grad",
    )
    smem, vmem = pl.BlockSpec(memory_space=pltpu.SMEM), pl.BlockSpec(memory_space=pltpu.VMEM)
    anywhere = pl.BlockSpec(memory_space=pl.ANY)
    packed, grad_dot = pl.pallas_call(
        functools.partial(combine_context_kernel, n_outer),
        in_specs=[smem] + [vmem] * (n_outer + 2) + [anywhere],
        out_specs=(anywhere, vmem),
        out_shape=(
            sds((inner, tok_local + rows, width), BF16),
            sds((inner, n_pair, 2 * rows), F32),
        ),
        scratch_shapes=[pltpu.VMEM((inner, rows, width), BF16), pltpu.SemaphoreType.DMA],
        input_output_aliases={n_outer + 3: 0},
        compiler_params=params(),
        cost_estimate=cost_us(3),
        name="combine_context",
    )(outer, *partials([after(mix, g_all) for mix in mixes]), norm, g_all, value_done)
    dots = [grad_dot] + [to_outer(grad_dot, n_outer - r) for r in range(1, n_outer)]
    packed_back = swap(after(packed, *dots[1:]))
    done = vmem_call(
        functools.partial(score_grad_kernel, n_outer),
        (pick, live, outer),
        [keys, values, q_all, g_all, norm] + dots,
        (sds((n_local, PLEN, width), BF16),) + (mix_shape,) * n_outer,
        [turned_pair, pair_scratch, turned_pair, turned, acc_scratch],
        25,
        "score_grad",
    )
    projected = out_project(after(packed_back, done[0]), rows, out_weight)
    value_grad = collect(after(packed_back, projected), tok_local)
    output = lax.psum_scatter(projected, "head", scatter_dimension=1, tiled=True).astype(BF16)
    key_back = swap(after(done[0], packed_back).reshape(inner, tok_local, width))
    query_done = vmem_call(
        functools.partial(combine_query_kernel, n_outer),
        (),
        [after(done[1], value_grad)] + partials(done[1:])[1:],
        sds((inner, rows, width), BF16),
        [],
        40,
        "combine_query",
    )
    query_grad = collect(swap(after(query_done, key_back)), rows)
    key_grad = collect(key_back, tok_local)
    return (output, query_grad, key_grad, value_grad)


def solution(mesh):
    in_specs = (
        P("pas", "head"),
        P("pas", None),
        P(None, "head"),
        P(None, "head"),
        P("head", None),
        P("pas", "head"),
        P(),
        P(),
        P(),
    )
    out_specs = (P("pas", "head"), P("pas", "head"), P("pas", "head"), P("pas", "head"))
    return jax.shard_map(body, mesh=mesh, in_specs=in_specs, out_specs=out_specs, check_vma=False)
```

```python
import functools

import jax
import jax.numpy as jnp
from jax import lax
from jax.experimental import pallas as pl
from jax.experimental.pallas import tpu as pltpu
from jax.sharding import PartitionSpec as P

HEAD_DIM = 64
PLEN = 256
INNER = 4
GROUP = 8
LANES = 128
NEG_LARGE = -1e30
SCALE = HEAD_DIM ** (-0.5)

BF16 = jnp.bfloat16
F32 = jnp.float32

VMEM_LIMIT = 56 * 1024 * 1024


def params(semantics=None):
    return pltpu.CompilerParams(vmem_limit_bytes=VMEM_LIMIT, dimension_semantics=semantics)


def dot_nt(a, b):
    return lax.dot_general(a, b, (((1,), (1,)), ((), ())), preferred_element_type=F32)


def dot_nn(a, b):
    return lax.dot_general(a, b, (((1,), (0,)), ((), ())), preferred_element_type=F32)


def dot_tn(a, b):
    return lax.dot_general(a, b, (((0,), (0,)), ((), ())), preferred_element_type=F32)


def cost_us(time):
    return pl.CostEstimate(flops=int(time * 1e9), bytes_accessed=0, transcendentals=0)


def project_kernel(x_ref, w_ref, o_ref):
    width = o_ref.shape[2]
    for block in range(INNER):
        cols = slice(block * width, (block + 1) * width)
        o_ref[block] = dot_nn(x_ref[...], w_ref[:, cols]).astype(BF16)


def project(x, w):
    rows, depth = x.shape
    cols = w.shape[1]
    tile = 256
    return pl.pallas_call(
        project_kernel,
        grid=(rows // tile,),
        in_specs=[
            pl.BlockSpec((tile, depth), lambda m: (m, 0)),
            pl.BlockSpec((depth, cols), lambda m: (0, 0)),
        ],
        out_specs=pl.BlockSpec((INNER, tile, cols // INNER), lambda m: (0, m, 0)),
        out_shape=jax.ShapeDtypeStruct((INNER, rows, cols // INNER), BF16),
        compiler_params=params(("arbitrary",)),
        cost_estimate=cost_us(14),
        name="project",
    )(x, w)


def two_heads(block):
    lane = lax.broadcasted_iota(jnp.int32, block.shape, 1)
    zero = jnp.zeros_like(block)
    return jnp.concatenate(
        [jnp.where(lane < HEAD_DIM, block, zero), jnp.where(lane >= HEAD_DIM, block, zero)], axis=0
    )


def two_heads_turned(block):
    turned = jnp.transpose(block)
    feat = lax.broadcasted_iota(jnp.int32, turned.shape, 0)
    zero = jnp.zeros_like(turned)
    return jnp.concatenate(
        [jnp.where(feat < HEAD_DIM, turned, zero), jnp.where(feat >= HEAD_DIM, turned, zero)], axis=1
    )


def own_blocks(full):
    rows = full.shape[1] // 2
    return jnp.concatenate([full[:HEAD_DIM, :rows], full[HEAD_DIM:, rows:]], axis=0)


def route_kernel(n_local, outer_ref, slot_ref, list_ref, count_ref, pick_ref, live_ref):
    n_q, list_len = list_ref.shape
    first_slot = outer_ref[0] * n_local

    def question(ident, carry):
        found = jnp.int32(0)
        for e in range(list_len):
            slot = slot_ref[list_ref[ident, e]] - first_slot
            here = (slot >= 0) & (slot < n_local) & (e < count_ref[ident])
            pick_ref[ident, found] = jnp.where(here, slot, 0)
            found = found + here.astype(jnp.int32)
        for e in range(GROUP):
            pick_ref[ident, found + e] = 0
        live_ref[ident] = found
        return carry

    lax.fori_loop(0, n_q, question, 0)


def each_group(pick_ref, live_ref, ident, entries, start):
    live = live_ref[ident]

    def group(step, carry):
        first = step * GROUP
        slots = [pick_ref[ident, first + j] for j in range(GROUP)]
        return entries(carry, slots, [first + j < live for j in range(GROUP)])

    return lax.fori_loop(0, lax.div(live + (GROUP - 1), GROUP), group, start)


def pair_lanes(pair):
    return slice(pair * LANES, (pair + 1) * LANES)


def stacked(ref, slots, pair):
    return jnp.concatenate([ref[slot, :, pair_lanes(pair)] for slot in slots], axis=0)


def beside(ref, slots, pair):
    return jnp.concatenate([ref[slot, pair_lanes(pair), :] for slot in slots], axis=1)


def shifted(scores, lives, top):
    keys = scores.shape[0] // GROUP
    return [
        jnp.exp(scores[j * keys : (j + 1) * keys] - jnp.where(live, top, -NEG_LARGE))
        for j, live in enumerate(lives)
    ]


def stats_kernel(pick_ref, live_ref, k_ref, q_ref, o_ref, qt):
    n_q = q_ref.shape[0]
    n_pair = q_ref.shape[2] // LANES

    def question(ident, carry):
        for pair in range(n_pair):
            qt[pair] = two_heads_turned(q_ref[ident, :, pair_lanes(pair)])
        o_ref[0, ident] = jnp.full(o_ref.shape[2:], NEG_LARGE, F32)
        o_ref[1, ident] = jnp.zeros(o_ref.shape[2:], F32)

        def entries(state, slots, lives):
            for pair in range(n_pair):
                row = slice(pair, pair + 1)
                scores = [dot_nn(k_ref[slot, :, pair_lanes(pair)], qt[pair]) for slot in slots]
                old = o_ref[0, ident, row, :]
                new = old
                for j, live in enumerate(lives):
                    top = jnp.max(scores[j], axis=0, keepdims=True)
                    new = jnp.maximum(new, jnp.where(live, top, NEG_LARGE))
                add = o_ref[1, ident, row, :] * jnp.exp(old - new)
                for part, live in zip(scores, lives):
                    part = jnp.exp(part - jnp.where(live, new, -NEG_LARGE))
                    add = add + jnp.sum(part, axis=0, keepdims=True)
                o_ref[0, ident, row, :] = new
                o_ref[1, ident, row, :] = add
            return state

        each_group(pick_ref, live_ref, ident, entries, 0)
        return carry

    lax.fori_loop(0, n_q, question, 0)


def value_grad_kernel(pick_ref, live_ref, k_ref, q_ref, g_ref, st_ref, o_ref, qt, gbd, acc):
    n_q = q_ref.shape[0]
    n_pair = q_ref.shape[2] // LANES
    acc[...] = jnp.zeros_like(acc)

    def question(ident, carry):
        for pair in range(n_pair):
            qt[pair] = two_heads_turned(q_ref[ident, :, pair_lanes(pair)])
            gbd[pair] = two_heads(g_ref[ident, :, pair_lanes(pair)])

        def entries(state, slots, lives):
            for pair in range(n_pair):
                row = slice(pair, pair + 1)
                scores = dot_nn(stacked(k_ref, slots, pair), qt[pair])
                norm = st_ref[1, ident, row, :]
                probs = [
                    (part * norm).astype(BF16)
                    for part in shifted(scores, lives, st_ref[0, ident, row, :])
                ]
                term = dot_nn(jnp.concatenate(probs, axis=0), gbd[pair]).astype(BF16)
                for j, slot in enumerate(slots):
                    acc[slot, :, pair_lanes(pair)] += term[j * PLEN : (j + 1) * PLEN].astype(F32)
            return state

        each_group(pick_ref, live_ref, ident, entries, 0)
        return carry

    lax.fori_loop(0, n_q, question, 0)

    per = k_ref.shape[0] // o_ref.shape[0]

    def finish(owner, carry):
        for place in range(per):
            o_ref[owner, place * PLEN : (place + 1) * PLEN] = acc[owner * per + place].astype(BF16)
        return carry

    lax.fori_loop(0, o_ref.shape[0], finish, 0)


def turn(src_ref, dst_ref):
    def one(slot, carry):
        dst_ref[slot] = jnp.transpose(src_ref[slot])
        return carry

    lax.fori_loop(0, src_ref.shape[0], one, 0)


def context_kernel(n_outer, r, pick_ref, live_ref, outer_ref, k_ref, v_ref, q_ref, st_ref, o_ref, qt, vt):
    n_pair = q_ref.shape[2] // LANES
    first = lax.rem(outer_ref[0] + r, n_outer) * o_ref.shape[0]
    turn(v_ref, vt)

    def question(index, carry):
        ident = first + index
        for pair in range(n_pair):
            qt[pair] = two_heads_turned(q_ref[ident, :, pair_lanes(pair)])
        zero = jnp.zeros((LANES, 2 * q_ref.shape[1]), F32)

        def entries(sums, slots, lives):
            out = []
            for pair in range(n_pair):
                scores = dot_nn(stacked(k_ref, slots, pair), qt[pair])
                weights = [
                    part.astype(BF16)
                    for part in shifted(scores, lives, st_ref[0, ident, slice(pair, pair + 1), :])
                ]
                mix = dot_nn(beside(vt, slots, pair), jnp.concatenate(weights, axis=0))
                out.append(sums[pair] + mix)
            return tuple(out)

        sums = each_group(pick_ref, live_ref, ident, entries, (zero,) * n_pair)
        for pair in range(n_pair):
            o_ref[index, pair_lanes(pair), :] = own_blocks(sums[pair])
        return carry

    lax.fori_loop(0, o_ref.shape[0], question, 0)


def score_grad_kernel(n_outer, pick_ref, live_ref, outer_ref, k_ref, v_ref, q_ref, g_ref, st_ref, *rest):
    dot_refs, rest = rest[:n_outer], rest[n_outer:]
    dk_ref, rest = rest[0], rest[1:]
    dq_refs, (qt, qbd, gt, kt, acc_k) = rest[:n_outer], rest[n_outer:]
    n_q = q_ref.shape[0]
    inner = n_q // n_outer
    n_pair = q_ref.shape[2] // LANES
    turn(k_ref, kt)
    acc_k[...] = jnp.zeros_like(acc_k)

    def question(dot_ref, dq_ref, outer, index, carry):
        ident = outer * inner + index
        for pair in range(n_pair):
            qbd[pair] = two_heads(q_ref[ident, :, pair_lanes(pair)])
            qt[pair] = two_heads_turned(q_ref[ident, :, pair_lanes(pair)])
            gt[pair] = two_heads_turned(g_ref[ident, :, pair_lanes(pair)])
        zero = jnp.zeros((LANES, 2 * q_ref.shape[1]), F32)

        def entries(sums, slots, lives):
            out = []
            for pair in range(n_pair):
                row = slice(pair, pair + 1)
                scores = dot_nn(stacked(k_ref, slots, pair), qt[pair])
                dprob = dot_nn(stacked(v_ref, slots, pair), gt[pair])
                norm = st_ref[1, ident, row, :]
                dots = dot_ref[index, row, :]
                dscore = [
                    (part * norm * (dprob[j * PLEN : (j + 1) * PLEN] - dots)).astype(BF16)
                    for j, part in enumerate(shifted(scores, lives, st_ref[0, ident, row, :]))
                ]
                dscore = jnp.concatenate(dscore, axis=0)
                term = dot_nn(dscore, qbd[pair]).astype(BF16)
                for j, slot in enumerate(slots):
                    acc_k[slot, :, pair_lanes(pair)] += term[j * PLEN : (j + 1) * PLEN].astype(F32)
                out.append(sums[pair] + dot_nn(beside(kt, slots, pair), dscore))
            return tuple(out)

        sums = each_group(pick_ref, live_ref, ident, entries, (zero,) * n_pair)
        for pair in range(n_pair):
            dq_ref[index, pair_lanes(pair), :] = own_blocks(sums[pair])
        return carry

    for r in reversed(range(n_outer)):
        outer = lax.rem(outer_ref[0] + r, n_outer)
        lax.fori_loop(0, inner, functools.partial(question, dot_refs[r], dq_refs[r], outer), 0)

    def finish(slot, carry):
        dk_ref[slot] = acc_k[slot].astype(BF16)
        return carry

    lax.fori_loop(0, k_ref.shape[0], finish, 0)


def merge_kernel(n_outer, *refs):
    parts, o_ref = refs[:n_outer], refs[n_outer]
    top = parts[0][0]
    for part in parts[1:]:
        top = jnp.maximum(top, part[0])
    total = parts[0][1] * jnp.exp(parts[0][0] - top)
    for part in parts[1:]:
        total = total + part[1] * jnp.exp(part[0] - top)
    o_ref[0] = top
    o_ref[1] = 1.0 / total
    o_ref[2] = total


def combine_context_kernel(n_parts, outer_ref, *refs):
    parts, (st_ref, g_ref, _, o_ref, dot_ref, ctx_ref, sem) = refs[:n_parts], refs[n_parts:]
    width = g_ref.shape[2]
    inner, rows = ctx_ref.shape[0], ctx_ref.shape[1]
    first = outer_ref[0] * inner
    for q in range(inner):
        mix = parts[0][q]
        for part in parts[1:]:
            mix = mix + part[q]
        grad = jnp.transpose(g_ref[first + q].astype(F32))
        pieces = []
        for head in range(width // HEAD_DIM):
            feats = slice(head * HEAD_DIM, (head + 1) * HEAD_DIM)
            pair, lanes = head // 2, slice((head % 2) * rows, (head % 2 + 1) * rows)
            total = st_ref[2, first + q, pair : pair + 1, lanes]
            ctx = (mix[feats] / total).astype(BF16).astype(F32)
            dot_ref[q, pair : pair + 1, lanes] = jnp.sum(grad[feats] * ctx, axis=0, keepdims=True)
            pieces.append(ctx)
        ctx_ref[q] = jnp.transpose(jnp.concatenate(pieces, axis=0)).astype(BF16)
    copy = pltpu.make_async_copy(ctx_ref, o_ref.at[:, pl.ds(o_ref.shape[1] - rows, rows), :], sem)
    copy.start()
    copy.wait()


def combine_query_kernel(n_parts, place_ref, *refs):
    parts, o_refs = refs[:n_parts], refs[n_parts:]
    for r, o_ref in enumerate(o_refs):
        q = lax.rem(place_ref[0] + r, len(o_refs))
        mix = parts[0][q]
        for part in parts[1:]:
            mix = mix + part[q]
        o_ref[...] = jnp.transpose(mix * SCALE).astype(BF16)


def gather_query_kernel(place_ref, *refs):
    blocks, o_ref = refs[:-1], refs[-1]
    width = blocks[0].shape[1]
    for r, block in enumerate(blocks):
        source = lax.rem(place_ref[0] + len(blocks) - r, len(blocks))
        o_ref[:, pl.ds(pl.multiple_of(source * width, LANES), width)] = block[...]


def spread_kernel(x_ref, o_ref):
    width = o_ref.shape[2]
    for block in range(INNER):
        part = x_ref[:, block * width : (block + 1) * width] * jnp.asarray(SCALE, BF16)
        for outer in range(o_ref.shape[0] // INNER):
            o_ref[outer * INNER + block] = part


def context_grad_kernel(x_ref, w_ref, o_ref):
    part = dot_nt(x_ref[...], w_ref[...]).astype(BF16)
    for outer in range(o_ref.shape[0]):
        o_ref[outer, 0] = part


def context_grad_blocks(x, w, n_outer, width):
    rows, depth = x.shape
    return pl.pallas_call(
        context_grad_kernel,
        grid=(INNER,),
        in_specs=[
            pl.BlockSpec((rows, depth), lambda j: (0, 0)),
            pl.BlockSpec((width, depth), lambda j: (j, 0)),
        ],
        out_specs=pl.BlockSpec((n_outer, 1, rows, width), lambda j: (0, j, 0, 0)),
        out_shape=jax.ShapeDtypeStruct((n_outer, INNER, rows, width), BF16),
        compiler_params=params(("arbitrary",)),
        cost_estimate=cost_us(5),
        name="context_grad",
    )(x, w)


def out_project_kernel(x_ref, w_ref, o_ref):
    step = pl.program_id(0)
    part = dot_nn(x_ref[0], w_ref[...])

    @pl.when(step == 0)
    def _():
        o_ref[...] = part

    @pl.when(step > 0)
    def _():
        o_ref[...] += part


def out_project(x, rows, w):
    blocks, length, width = x.shape
    cols = w.shape[1]
    return pl.pallas_call(
        out_project_kernel,
        grid=(blocks,),
        in_specs=[
            pl.BlockSpec((1, rows, width), lambda j: (j, length // rows - 1, 0)),
            pl.BlockSpec((width, cols), lambda j: (j, 0)),
        ],
        out_specs=pl.BlockSpec((rows, cols), lambda j: (0, 0)),
        out_shape=jax.ShapeDtypeStruct((rows, cols), F32),
        compiler_params=params(("arbitrary",)),
        cost_estimate=cost_us(1),
        name="out_project",
    )(x, w)


def collect_kernel(x_ref, o_ref):
    width = x_ref.shape[2]
    for block in range(x_ref.shape[0]):
        o_ref[:, block * width : (block + 1) * width] = x_ref[block]


def collect(x, rows):
    blocks, _, width = x.shape
    tile = min(rows, 512)
    return pl.pallas_call(
        collect_kernel,
        grid=(rows // tile,),
        in_specs=[pl.BlockSpec((blocks, tile, width), lambda m: (0, m, 0))],
        out_specs=pl.BlockSpec((tile, blocks * width), lambda m: (m, 0)),
        out_shape=jax.ShapeDtypeStruct((rows, blocks * width), x.dtype),
        compiler_params=params(("arbitrary",)),
        cost_estimate=cost_us(1),
        name="collect",
    )(x)


def vmem_call(kernel, scalars, arrays, out_shape, scratch, time, name):
    smem = pl.BlockSpec(memory_space=pltpu.SMEM)
    vmem = pl.BlockSpec(memory_space=pltpu.VMEM)
    return pl.pallas_call(
        kernel,
        in_specs=[smem] * len(scalars) + [vmem] * len(arrays),
        out_specs=jax.tree.map(lambda _: vmem, out_shape),
        out_shape=out_shape,
        scratch_shapes=scratch,
        compiler_params=params(),
        cost_estimate=cost_us(time),
        name=name,
    )(*scalars, *arrays)


def route(outer, slot_of, passage_lists, list_counts, n_local):
    smem = pl.BlockSpec(memory_space=pltpu.SMEM)
    n_q, list_len = passage_lists.shape
    return pl.pallas_call(
        functools.partial(route_kernel, n_local),
        in_specs=[smem] * 4,
        out_specs=(smem, smem),
        out_shape=(
            jax.ShapeDtypeStruct((n_q, list_len + GROUP), jnp.int32),
            jax.ShapeDtypeStruct((n_q,), jnp.int32),
        ),
        cost_estimate=cost_us(3),
        name="route",
    )(outer, slot_of, passage_lists, list_counts)


def after(value, *others):
    return lax.optimization_barrier((value,) + others)[0]


def body(
    queries,
    encoded,
    key_weight,
    value_weight,
    out_weight,
    out_grad,
    slot_of,
    passage_lists,
    list_counts,
):
    head_width = key_weight.shape[1]
    rows = queries.shape[0]
    tok_local = encoded.shape[0]
    n_pas = lax.axis_size("pas")
    inner = INNER
    n_outer = n_pas // inner
    width = head_width // inner
    n_pair = width // LANES
    n_local = inner * (tok_local // PLEN)
    n_q = n_pas
    outer = (lax.axis_index("pas") // inner).astype(jnp.int32).reshape(1)
    groups = [[o * inner + i for i in range(inner)] for o in range(n_outer)]
    sds = jax.ShapeDtypeStruct

    def swap(x):
        return lax.all_to_all(
            x, "pas", split_axis=0, concat_axis=0, tiled=True, axis_index_groups=groups
        )

    def swap_all(x):
        return lax.all_to_all(x, "pas", split_axis=0, concat_axis=0, tiled=True)

    def to_outer(x, r):
        return lax.ppermute(
            x,
            "pas",
            [(o * inner + i, ((o + r) % n_outer) * inner + i) for o in range(n_outer) for i in range(inner)],
        )

    def partials(parts):
        return [parts[0]] + [to_outer(parts[r], r) for r in range(1, n_outer)]

    q_spread = vmem_call(spread_kernel, (), (queries,), sds((n_q, rows, width), BF16), [], 1.5, "spread")
    q_all = swap_all(q_spread)
    grad_rows = lax.all_gather(out_grad, "head", axis=1, tiled=True)

    key_part = project(after(encoded, q_spread), key_weight)
    keys = swap(key_part).reshape(n_local, PLEN, width)
    value_part = project(after(encoded, key_part, grad_rows), value_weight)
    g_spread = context_grad_blocks(after(grad_rows, value_part), out_weight, n_outer, width)
    g_spread = g_spread.reshape(n_q, rows, width)
    pick, live = route(after(outer, value_part), slot_of, passage_lists, list_counts, n_local)
    values = swap(after(value_part, g_spread, pick)).reshape(n_local, PLEN, width)

    pair_scratch = pltpu.VMEM((n_pair, 2 * rows, LANES), BF16)
    turned_pair = pltpu.VMEM((n_pair, LANES, 2 * rows), BF16)
    acc_scratch = pltpu.VMEM((n_local, PLEN, width), F32)
    turned = pltpu.VMEM((n_local, width, PLEN), BF16)
    stat_shape = (n_q, n_pair, 2 * rows)
    mix_shape = sds((inner, width, rows), F32)

    stats = vmem_call(
        stats_kernel,
        (pick, live),
        (keys, q_all),
        sds((2,) + stat_shape, F32),
        [turned_pair],
        13,
        "stats",
    )
    norm = vmem_call(
        functools.partial(merge_kernel, n_outer),
        (),
        [stats] + [to_outer(stats, r) for r in range(1, n_outer)],
        sds((3,) + stat_shape, F32),
        [],
        1,
        "merge",
    )
    g_all = swap_all(after(g_spread, values))
    mixes, norm_then = [None] * n_outer, norm
    for r in reversed(range(n_outer)):
        mixes[r] = vmem_call(
            functools.partial(context_kernel, n_outer, r),
            (pick, live, outer),
            (keys, values, q_all, norm_then),
            mix_shape,
            [turned_pair, turned],
            5 if r == 0 else 14,
            "context",
        )
        norm_then = after(norm, mixes[r], g_all)
    value_done = vmem_call(
        value_grad_kernel,
        (pick, live),
        (keys, q_all, g_all, norm_then),
        sds((inner, tok_local + rows, width), BF16),
        [turned_pair, pair_scratch, acc_scratch],
        5,
        "value_grad",
    )
    smem, vmem = pl.BlockSpec(memory_space=pltpu.SMEM), pl.BlockSpec(memory_space=pltpu.VMEM)
    anywhere = pl.BlockSpec(memory_space=pl.ANY)
    packed, grad_dot = pl.pallas_call(
        functools.partial(combine_context_kernel, n_outer),
        in_specs=[smem] + [vmem] * (n_outer + 2) + [anywhere],
        out_specs=(anywhere, vmem),
        out_shape=(
            sds((inner, tok_local + rows, width), BF16),
            sds((inner, n_pair, 2 * rows), F32),
        ),
        scratch_shapes=[pltpu.VMEM((inner, rows, width), BF16), pltpu.SemaphoreType.DMA],
        input_output_aliases={n_outer + 3: 0},
        compiler_params=params(),
        cost_estimate=cost_us(3),
        name="combine_context",
    )(outer, *partials([after(mix, g_all) for mix in mixes]), norm, g_all, value_done)
    dots = [grad_dot] + [to_outer(grad_dot, n_outer - r) for r in range(1, n_outer)]
    packed_back = swap(after(packed, *dots[1:]))
    done = vmem_call(
        functools.partial(score_grad_kernel, n_outer),
        (pick, live, outer),
        [keys, values, q_all, g_all, norm] + dots,
        (sds((n_local, PLEN, width), BF16),) + (mix_shape,) * n_outer,
        [turned_pair, pair_scratch, turned_pair, turned, acc_scratch],
        25,
        "score_grad",
    )
    projected = out_project(after(packed_back, done[0]), rows, out_weight)
    value_grad = collect(after(packed_back, projected), tok_local)
    output = lax.psum_scatter(projected, "head", scatter_dimension=1, tiled=True).astype(BF16)
    key_back = swap(after(done[0], packed_back).reshape(inner, tok_local, width))
    place = (lax.axis_index("pas") % inner).astype(jnp.int32).reshape(1)
    query_blocks = vmem_call(
        functools.partial(combine_query_kernel, n_outer),
        (place,),
        [after(done[1], value_grad)] + partials(done[1:])[1:],
        (sds((rows, width), BF16),) * inner,
        [],
        40,
        "combine_query",
    )
    arrived = [query_blocks[0]] + [
        lax.ppermute(
            query_blocks[r],
            "pas",
            [(o * inner + i, o * inner + (i + r) % inner) for o in range(n_outer) for i in range(inner)],
        )
        for r in range(1, inner)
    ]
    query_grad = vmem_call(
        gather_query_kernel, (place,), arrived, sds((rows, head_width), BF16), [], 30, "gather_query"
    )
    key_grad = collect(key_back, tok_local)
    return (output, query_grad, key_grad, value_grad)


def solution(mesh):
    in_specs = (
        P("pas", "head"),
        P("pas", None),
        P(None, "head"),
        P(None, "head"),
        P("head", None),
        P("pas", "head"),
        P(),
        P(),
        P(),
    )
    out_specs = (P("pas", "head"), P("pas", "head"), P("pas", "head"), P("pas", "head"))
    return jax.shard_map(body, mesh=mesh, in_specs=in_specs, out_specs=out_specs, check_vma=False)
```

```python
import functools

import jax
import jax.numpy as jnp
from jax import lax
from jax.experimental import pallas as pl
from jax.experimental.pallas import tpu as pltpu
from jax.sharding import PartitionSpec as P

HEAD_DIM = 64
PLEN = 256
INNER = 4
GROUP = 8
SIZES = (6, 7)
LANES = 128
NEG_LARGE = -1e30
SCALE = HEAD_DIM ** (-0.5)

BF16 = jnp.bfloat16
F32 = jnp.float32

VMEM_LIMIT = 56 * 1024 * 1024


def params(semantics=None):
    return pltpu.CompilerParams(vmem_limit_bytes=VMEM_LIMIT, dimension_semantics=semantics)


def dot_nt(a, b):
    return lax.dot_general(a, b, (((1,), (1,)), ((), ())), preferred_element_type=F32)


def dot_nn(a, b):
    return lax.dot_general(a, b, (((1,), (0,)), ((), ())), preferred_element_type=F32)


def dot_tn(a, b):
    return lax.dot_general(a, b, (((0,), (0,)), ((), ())), preferred_element_type=F32)


def cost_us(time):
    return pl.CostEstimate(flops=int(time * 1e9), bytes_accessed=0, transcendentals=0)


def project_kernel(x_ref, w_ref, o_ref):
    width = o_ref.shape[2]
    for block in range(INNER):
        cols = slice(block * width, (block + 1) * width)
        o_ref[block] = dot_nn(x_ref[...], w_ref[:, cols]).astype(BF16)


def project(x, w):
    rows, depth = x.shape
    cols = w.shape[1]
    tile = 256
    return pl.pallas_call(
        project_kernel,
        grid=(rows // tile,),
        in_specs=[
            pl.BlockSpec((tile, depth), lambda m: (m, 0)),
            pl.BlockSpec((depth, cols), lambda m: (0, 0)),
        ],
        out_specs=pl.BlockSpec((INNER, tile, cols // INNER), lambda m: (0, m, 0)),
        out_shape=jax.ShapeDtypeStruct((INNER, rows, cols // INNER), BF16),
        compiler_params=params(("arbitrary",)),
        cost_estimate=cost_us(14),
        name="project",
    )(x, w)


def two_heads(block):
    lane = lax.broadcasted_iota(jnp.int32, block.shape, 1)
    zero = jnp.zeros_like(block)
    return jnp.concatenate(
        [jnp.where(lane < HEAD_DIM, block, zero), jnp.where(lane >= HEAD_DIM, block, zero)], axis=0
    )


def two_heads_turned(block):
    turned = jnp.transpose(block)
    feat = lax.broadcasted_iota(jnp.int32, turned.shape, 0)
    zero = jnp.zeros_like(turned)
    return jnp.concatenate(
        [jnp.where(feat < HEAD_DIM, turned, zero), jnp.where(feat >= HEAD_DIM, turned, zero)], axis=1
    )


def own_blocks(full):
    rows = full.shape[1] // 2
    return jnp.concatenate([full[:HEAD_DIM, :rows], full[HEAD_DIM:, rows:]], axis=0)


def route_kernel(n_local, outer_ref, slot_ref, list_ref, count_ref, pick_ref, live_ref):
    n_q, list_len = list_ref.shape
    first_slot = outer_ref[0] * n_local

    def question(ident, carry):
        found = jnp.int32(0)
        for e in range(list_len):
            slot = slot_ref[list_ref[ident, e]] - first_slot
            here = (slot >= 0) & (slot < n_local) & (e < count_ref[ident])
            pick_ref[ident, found] = jnp.where(here, slot, 0)
            found = found + here.astype(jnp.int32)
        for e in range(GROUP):
            pick_ref[ident, found + e] = 0
        live_ref[ident] = found
        return carry

    lax.fori_loop(0, n_q, question, 0)


def each_group(pick_ref, live_ref, ident, entries, start):
    live = live_ref[ident]

    def group(first, size, carry):
        slots = [pick_ref[ident, first + j] for j in range(size)]
        return entries(carry, slots, [first + j < live for j in range(size)])

    def in_groups():
        steps = lax.div(live + (GROUP - 1), GROUP)
        return lax.fori_loop(0, steps, lambda step, carry: group(step * GROUP, GROUP, carry), start)

    def by_size(sizes):
        if not sizes:
            return in_groups()
        return lax.cond(live <= sizes[0], lambda: group(0, sizes[0], start), lambda: by_size(sizes[1:]))

    return by_size(SIZES)


def pair_lanes(pair):
    return slice(pair * LANES, (pair + 1) * LANES)


def stacked(ref, slots, pair):
    return jnp.concatenate([ref[slot, :, pair_lanes(pair)] for slot in slots], axis=0)


def beside(ref, slots, pair):
    return jnp.concatenate([ref[slot, pair_lanes(pair), :] for slot in slots], axis=1)


def shifted(scores, lives, top):
    keys = scores.shape[0] // len(lives)
    return [
        jnp.exp(scores[j * keys : (j + 1) * keys] - jnp.where(live, top, -NEG_LARGE))
        for j, live in enumerate(lives)
    ]


def stats_kernel(pick_ref, live_ref, k_ref, q_ref, o_ref, qt):
    n_q = q_ref.shape[0]
    n_pair = q_ref.shape[2] // LANES

    def question(ident, carry):
        for pair in range(n_pair):
            qt[pair] = two_heads_turned(q_ref[ident, :, pair_lanes(pair)])
        o_ref[0, ident] = jnp.full(o_ref.shape[2:], NEG_LARGE, F32)
        o_ref[1, ident] = jnp.zeros(o_ref.shape[2:], F32)

        def entries(state, slots, lives):
            for pair in range(n_pair):
                row = slice(pair, pair + 1)
                scores = [dot_nn(k_ref[slot, :, pair_lanes(pair)], qt[pair]) for slot in slots]
                old = o_ref[0, ident, row, :]
                new = old
                for j, live in enumerate(lives):
                    top = jnp.max(scores[j], axis=0, keepdims=True)
                    new = jnp.maximum(new, jnp.where(live, top, NEG_LARGE))
                add = o_ref[1, ident, row, :] * jnp.exp(old - new)
                for part, live in zip(scores, lives):
                    part = jnp.exp(part - jnp.where(live, new, -NEG_LARGE))
                    add = add + jnp.sum(part, axis=0, keepdims=True)
                o_ref[0, ident, row, :] = new
                o_ref[1, ident, row, :] = add
            return state

        each_group(pick_ref, live_ref, ident, entries, 0)
        return carry

    lax.fori_loop(0, n_q, question, 0)


def value_grad_kernel(pick_ref, live_ref, k_ref, q_ref, g_ref, st_ref, o_ref, qt, gbd, acc):
    n_q = q_ref.shape[0]
    n_pair = q_ref.shape[2] // LANES
    acc[...] = jnp.zeros_like(acc)

    def question(ident, carry):
        for pair in range(n_pair):
            qt[pair] = two_heads_turned(q_ref[ident, :, pair_lanes(pair)])
            gbd[pair] = two_heads(g_ref[ident, :, pair_lanes(pair)])

        def entries(state, slots, lives):
            for pair in range(n_pair):
                row = slice(pair, pair + 1)
                scores = dot_nn(stacked(k_ref, slots, pair), qt[pair])
                norm = st_ref[1, ident, row, :]
                probs = [
                    (part * norm).astype(BF16)
                    for part in shifted(scores, lives, st_ref[0, ident, row, :])
                ]
                term = dot_nn(jnp.concatenate(probs, axis=0), gbd[pair]).astype(BF16)
                for j, slot in enumerate(slots):
                    acc[slot, :, pair_lanes(pair)] += term[j * PLEN : (j + 1) * PLEN].astype(F32)
            return state

        each_group(pick_ref, live_ref, ident, entries, 0)
        return carry

    lax.fori_loop(0, n_q, question, 0)

    per = k_ref.shape[0] // o_ref.shape[0]

    def finish(owner, carry):
        for place in range(per):
            o_ref[owner, place * PLEN : (place + 1) * PLEN] = acc[owner * per + place].astype(BF16)
        return carry

    lax.fori_loop(0, o_ref.shape[0], finish, 0)


def turn(src_ref, dst_ref):
    def one(slot, carry):
        dst_ref[slot] = jnp.transpose(src_ref[slot])
        return carry

    lax.fori_loop(0, src_ref.shape[0], one, 0)


def context_kernel(n_outer, r, pick_ref, live_ref, outer_ref, k_ref, v_ref, q_ref, st_ref, o_ref, qt, vt):
    n_pair = q_ref.shape[2] // LANES
    first = lax.rem(outer_ref[0] + r, n_outer) * o_ref.shape[0]
    turn(v_ref, vt)

    def question(index, carry):
        ident = first + index
        for pair in range(n_pair):
            qt[pair] = two_heads_turned(q_ref[ident, :, pair_lanes(pair)])
        zero = jnp.zeros((LANES, 2 * q_ref.shape[1]), F32)

        def entries(sums, slots, lives):
            out = []
            for pair in range(n_pair):
                scores = dot_nn(stacked(k_ref, slots, pair), qt[pair])
                weights = [
                    part.astype(BF16)
                    for part in shifted(scores, lives, st_ref[0, ident, slice(pair, pair + 1), :])
                ]
                mix = dot_nn(beside(vt, slots, pair), jnp.concatenate(weights, axis=0))
                out.append(sums[pair] + mix)
            return tuple(out)

        sums = each_group(pick_ref, live_ref, ident, entries, (zero,) * n_pair)
        for pair in range(n_pair):
            o_ref[index, pair_lanes(pair), :] = own_blocks(sums[pair])
        return carry

    lax.fori_loop(0, o_ref.shape[0], question, 0)


def score_grad_kernel(n_outer, pick_ref, live_ref, outer_ref, k_ref, v_ref, q_ref, g_ref, st_ref, *rest):
    dot_refs, rest = rest[:n_outer], rest[n_outer:]
    dk_ref, rest = rest[0], rest[1:]
    dq_refs, (qt, qbd, gt, kt, acc_k) = rest[:n_outer], rest[n_outer:]
    n_q = q_ref.shape[0]
    inner = n_q // n_outer
    n_pair = q_ref.shape[2] // LANES
    turn(k_ref, kt)
    acc_k[...] = jnp.zeros_like(acc_k)

    def question(dot_ref, dq_ref, outer, index, carry):
        ident = outer * inner + index
        for pair in range(n_pair):
            qbd[pair] = two_heads(q_ref[ident, :, pair_lanes(pair)])
            qt[pair] = two_heads_turned(q_ref[ident, :, pair_lanes(pair)])
            gt[pair] = two_heads_turned(g_ref[ident, :, pair_lanes(pair)])
        zero = jnp.zeros((LANES, 2 * q_ref.shape[1]), F32)

        def entries(sums, slots, lives):
            out = []
            for pair in range(n_pair):
                row = slice(pair, pair + 1)
                scores = dot_nn(stacked(k_ref, slots, pair), qt[pair])
                dprob = dot_nn(stacked(v_ref, slots, pair), gt[pair])
                norm = st_ref[1, ident, row, :]
                dots = dot_ref[index, row, :]
                dscore = [
                    (part * norm * (dprob[j * PLEN : (j + 1) * PLEN] - dots)).astype(BF16)
                    for j, part in enumerate(shifted(scores, lives, st_ref[0, ident, row, :]))
                ]
                dscore = jnp.concatenate(dscore, axis=0)
                term = dot_nn(dscore, qbd[pair]).astype(BF16)
                for j, slot in enumerate(slots):
                    acc_k[slot, :, pair_lanes(pair)] += term[j * PLEN : (j + 1) * PLEN].astype(F32)
                out.append(sums[pair] + dot_nn(beside(kt, slots, pair), dscore))
            return tuple(out)

        sums = each_group(pick_ref, live_ref, ident, entries, (zero,) * n_pair)
        for pair in range(n_pair):
            dq_ref[index, pair_lanes(pair), :] = own_blocks(sums[pair])
        return carry

    for r in reversed(range(n_outer)):
        outer = lax.rem(outer_ref[0] + r, n_outer)
        lax.fori_loop(0, inner, functools.partial(question, dot_refs[r], dq_refs[r], outer), 0)

    def finish(slot, carry):
        dk_ref[slot] = acc_k[slot].astype(BF16)
        return carry

    lax.fori_loop(0, k_ref.shape[0], finish, 0)


def merge_kernel(n_outer, *refs):
    parts, o_ref = refs[:n_outer], refs[n_outer]
    top = parts[0][0]
    for part in parts[1:]:
        top = jnp.maximum(top, part[0])
    total = parts[0][1] * jnp.exp(parts[0][0] - top)
    for part in parts[1:]:
        total = total + part[1] * jnp.exp(part[0] - top)
    o_ref[0] = top
    o_ref[1] = 1.0 / total
    o_ref[2] = total


def combine_context_kernel(n_parts, outer_ref, *refs):
    parts, (st_ref, g_ref, _, o_ref, dot_ref, ctx_ref, sem) = refs[:n_parts], refs[n_parts:]
    width = g_ref.shape[2]
    inner, rows = ctx_ref.shape[0], ctx_ref.shape[1]
    first = outer_ref[0] * inner
    for q in range(inner):
        mix = parts[0][q]
        for part in parts[1:]:
            mix = mix + part[q]
        grad = jnp.transpose(g_ref[first + q].astype(F32))
        pieces = []
        for head in range(width // HEAD_DIM):
            feats = slice(head * HEAD_DIM, (head + 1) * HEAD_DIM)
            pair, lanes = head // 2, slice((head % 2) * rows, (head % 2 + 1) * rows)
            total = st_ref[2, first + q, pair : pair + 1, lanes]
            ctx = (mix[feats] / total).astype(BF16).astype(F32)
            dot_ref[q, pair : pair + 1, lanes] = jnp.sum(grad[feats] * ctx, axis=0, keepdims=True)
            pieces.append(ctx)
        ctx_ref[q] = jnp.transpose(jnp.concatenate(pieces, axis=0)).astype(BF16)
    copy = pltpu.make_async_copy(ctx_ref, o_ref.at[:, pl.ds(o_ref.shape[1] - rows, rows), :], sem)
    copy.start()
    copy.wait()


def combine_query_kernel(n_parts, place_ref, *refs):
    parts, o_refs = refs[:n_parts], refs[n_parts:]
    for r, o_ref in enumerate(o_refs):
        q = lax.rem(place_ref[0] + r, len(o_refs))
        mix = parts[0][q]
        for part in parts[1:]:
            mix = mix + part[q]
        o_ref[...] = jnp.transpose(mix * SCALE).astype(BF16)


def gather_query_kernel(place_ref, *refs):
    blocks, o_ref = refs[:-1], refs[-1]
    width = blocks[0].shape[1]
    for r, block in enumerate(blocks):
        source = lax.rem(place_ref[0] + len(blocks) - r, len(blocks))
        o_ref[:, pl.ds(pl.multiple_of(source * width, LANES), width)] = block[...]


def spread_kernel(x_ref, o_ref):
    width = o_ref.shape[2]
    for block in range(INNER):
        part = x_ref[:, block * width : (block + 1) * width] * jnp.asarray(SCALE, BF16)
        for outer in range(o_ref.shape[0] // INNER):
            o_ref[outer * INNER + block] = part


def context_grad_kernel(x_ref, w_ref, o_ref):
    part = dot_nt(x_ref[...], w_ref[...]).astype(BF16)
    for outer in range(o_ref.shape[0]):
        o_ref[outer, 0] = part


def context_grad_blocks(x, w, n_outer, width):
    rows, depth = x.shape
    return pl.pallas_call(
        context_grad_kernel,
        grid=(INNER,),
        in_specs=[
            pl.BlockSpec((rows, depth), lambda j: (0, 0)),
            pl.BlockSpec((width, depth), lambda j: (j, 0)),
        ],
        out_specs=pl.BlockSpec((n_outer, 1, rows, width), lambda j: (0, j, 0, 0)),
        out_shape=jax.ShapeDtypeStruct((n_outer, INNER, rows, width), BF16),
        compiler_params=params(("arbitrary",)),
        cost_estimate=cost_us(5),
        name="context_grad",
    )(x, w)


def out_project_kernel(x_ref, w_ref, o_ref):
    step = pl.program_id(0)
    part = dot_nn(x_ref[0], w_ref[...])

    @pl.when(step == 0)
    def _():
        o_ref[...] = part

    @pl.when(step > 0)
    def _():
        o_ref[...] += part


def out_project(x, rows, w):
    blocks, length, width = x.shape
    cols = w.shape[1]
    return pl.pallas_call(
        out_project_kernel,
        grid=(blocks,),
        in_specs=[
            pl.BlockSpec((1, rows, width), lambda j: (j, length // rows - 1, 0)),
            pl.BlockSpec((width, cols), lambda j: (j, 0)),
        ],
        out_specs=pl.BlockSpec((rows, cols), lambda j: (0, 0)),
        out_shape=jax.ShapeDtypeStruct((rows, cols), F32),
        compiler_params=params(("arbitrary",)),
        cost_estimate=cost_us(1),
        name="out_project",
    )(x, w)


def collect_kernel(x_ref, o_ref):
    width = x_ref.shape[2]
    for block in range(x_ref.shape[0]):
        o_ref[:, block * width : (block + 1) * width] = x_ref[block]


def collect(x, rows):
    blocks, _, width = x.shape
    tile = min(rows, 512)
    return pl.pallas_call(
        collect_kernel,
        grid=(rows // tile,),
        in_specs=[pl.BlockSpec((blocks, tile, width), lambda m: (0, m, 0))],
        out_specs=pl.BlockSpec((tile, blocks * width), lambda m: (m, 0)),
        out_shape=jax.ShapeDtypeStruct((rows, blocks * width), x.dtype),
        compiler_params=params(("arbitrary",)),
        cost_estimate=cost_us(1),
        name="collect",
    )(x)


def vmem_call(kernel, scalars, arrays, out_shape, scratch, time, name):
    smem = pl.BlockSpec(memory_space=pltpu.SMEM)
    vmem = pl.BlockSpec(memory_space=pltpu.VMEM)
    return pl.pallas_call(
        kernel,
        in_specs=[smem] * len(scalars) + [vmem] * len(arrays),
        out_specs=jax.tree.map(lambda _: vmem, out_shape),
        out_shape=out_shape,
        scratch_shapes=scratch,
        compiler_params=params(),
        cost_estimate=cost_us(time),
        name=name,
    )(*scalars, *arrays)


def route(outer, slot_of, passage_lists, list_counts, n_local):
    smem = pl.BlockSpec(memory_space=pltpu.SMEM)
    n_q, list_len = passage_lists.shape
    return pl.pallas_call(
        functools.partial(route_kernel, n_local),
        in_specs=[smem] * 4,
        out_specs=(smem, smem),
        out_shape=(
            jax.ShapeDtypeStruct((n_q, list_len + GROUP), jnp.int32),
            jax.ShapeDtypeStruct((n_q,), jnp.int32),
        ),
        cost_estimate=cost_us(3),
        name="route",
    )(outer, slot_of, passage_lists, list_counts)


def after(value, *others):
    return lax.optimization_barrier((value,) + others)[0]


def body(
    queries,
    encoded,
    key_weight,
    value_weight,
    out_weight,
    out_grad,
    slot_of,
    passage_lists,
    list_counts,
):
    head_width = key_weight.shape[1]
    rows = queries.shape[0]
    tok_local = encoded.shape[0]
    n_pas = lax.axis_size("pas")
    inner = INNER
    n_outer = n_pas // inner
    width = head_width // inner
    n_pair = width // LANES
    n_local = inner * (tok_local // PLEN)
    n_q = n_pas
    outer = (lax.axis_index("pas") // inner).astype(jnp.int32).reshape(1)
    groups = [[o * inner + i for i in range(inner)] for o in range(n_outer)]
    sds = jax.ShapeDtypeStruct

    def swap(x):
        return lax.all_to_all(
            x, "pas", split_axis=0, concat_axis=0, tiled=True, axis_index_groups=groups
        )

    def swap_all(x):
        return lax.all_to_all(x, "pas", split_axis=0, concat_axis=0, tiled=True)

    def to_outer(x, r):
        return lax.ppermute(
            x,
            "pas",
            [(o * inner + i, ((o + r) % n_outer) * inner + i) for o in range(n_outer) for i in range(inner)],
        )

    def partials(parts):
        return [parts[0]] + [to_outer(parts[r], r) for r in range(1, n_outer)]

    q_spread = vmem_call(spread_kernel, (), (queries,), sds((n_q, rows, width), BF16), [], 1.5, "spread")
    q_all = swap_all(q_spread)
    grad_rows = lax.all_gather(out_grad, "head", axis=1, tiled=True)

    key_part = project(after(encoded, q_spread), key_weight)
    keys = swap(key_part).reshape(n_local, PLEN, width)
    value_part = project(after(encoded, key_part, grad_rows), value_weight)
    g_spread = context_grad_blocks(after(grad_rows, value_part), out_weight, n_outer, width)
    g_spread = g_spread.reshape(n_q, rows, width)
    pick, live = route(after(outer, value_part), slot_of, passage_lists, list_counts, n_local)
    values = swap(after(value_part, g_spread, pick)).reshape(n_local, PLEN, width)

    pair_scratch = pltpu.VMEM((n_pair, 2 * rows, LANES), BF16)
    turned_pair = pltpu.VMEM((n_pair, LANES, 2 * rows), BF16)
    acc_scratch = pltpu.VMEM((n_local, PLEN, width), F32)
    turned = pltpu.VMEM((n_local, width, PLEN), BF16)
    stat_shape = (n_q, n_pair, 2 * rows)
    mix_shape = sds((inner, width, rows), F32)

    stats = vmem_call(
        stats_kernel,
        (pick, live),
        (keys, q_all),
        sds((2,) + stat_shape, F32),
        [turned_pair],
        13,
        "stats",
    )
    norm = vmem_call(
        functools.partial(merge_kernel, n_outer),
        (),
        [stats] + [to_outer(stats, r) for r in range(1, n_outer)],
        sds((3,) + stat_shape, F32),
        [],
        1,
        "merge",
    )
    g_all = swap_all(after(g_spread, values))
    mixes, norm_then = [None] * n_outer, norm
    for r in reversed(range(n_outer)):
        mixes[r] = vmem_call(
            functools.partial(context_kernel, n_outer, r),
            (pick, live, outer),
            (keys, values, q_all, norm_then),
            mix_shape,
            [turned_pair, turned],
            5 if r == 0 else 14,
            "context",
        )
        norm_then = after(norm, mixes[r], g_all)
    value_done = vmem_call(
        value_grad_kernel,
        (pick, live),
        (keys, q_all, g_all, norm_then),
        sds((inner, tok_local + rows, width), BF16),
        [turned_pair, pair_scratch, acc_scratch],
        5,
        "value_grad",
    )
    smem, vmem = pl.BlockSpec(memory_space=pltpu.SMEM), pl.BlockSpec(memory_space=pltpu.VMEM)
    anywhere = pl.BlockSpec(memory_space=pl.ANY)
    packed, grad_dot = pl.pallas_call(
        functools.partial(combine_context_kernel, n_outer),
        in_specs=[smem] + [vmem] * (n_outer + 2) + [anywhere],
        out_specs=(anywhere, vmem),
        out_shape=(
            sds((inner, tok_local + rows, width), BF16),
            sds((inner, n_pair, 2 * rows), F32),
        ),
        scratch_shapes=[pltpu.VMEM((inner, rows, width), BF16), pltpu.SemaphoreType.DMA],
        input_output_aliases={n_outer + 3: 0},
        compiler_params=params(),
        cost_estimate=cost_us(3),
        name="combine_context",
    )(outer, *partials([after(mix, g_all) for mix in mixes]), norm, g_all, value_done)
    dots = [grad_dot] + [to_outer(grad_dot, n_outer - r) for r in range(1, n_outer)]
    packed_back = swap(after(packed, *dots[1:]))
    done = vmem_call(
        functools.partial(score_grad_kernel, n_outer),
        (pick, live, outer),
        [keys, values, q_all, g_all, norm] + dots,
        (sds((n_local, PLEN, width), BF16),) + (mix_shape,) * n_outer,
        [turned_pair, pair_scratch, turned_pair, turned, acc_scratch],
        25,
        "score_grad",
    )
    projected = out_project(after(packed_back, done[0]), rows, out_weight)
    value_grad = collect(after(packed_back, projected), tok_local)
    output = lax.psum_scatter(projected, "head", scatter_dimension=1, tiled=True).astype(BF16)
    key_back = swap(after(done[0], packed_back).reshape(inner, tok_local, width))
    place = (lax.axis_index("pas") % inner).astype(jnp.int32).reshape(1)
    query_blocks = vmem_call(
        functools.partial(combine_query_kernel, n_outer),
        (place,),
        [after(done[1], value_grad)] + partials(done[1:])[1:],
        (sds((rows, width), BF16),) * inner,
        [],
        40,
        "combine_query",
    )
    arrived = [query_blocks[0]] + [
        lax.ppermute(
            query_blocks[r],
            "pas",
            [(o * inner + i, o * inner + (i + r) % inner) for o in range(n_outer) for i in range(inner)],
        )
        for r in range(1, inner)
    ]
    query_grad = vmem_call(
        gather_query_kernel, (place,), arrived, sds((rows, head_width), BF16), [], 30, "gather_query"
    )
    key_grad = collect(key_back, tok_local)
    return (output, query_grad, key_grad, value_grad)


def solution(mesh):
    in_specs = (
        P("pas", "head"),
        P("pas", None),
        P(None, "head"),
        P(None, "head"),
        P("head", None),
        P("pas", "head"),
        P(),
        P(),
        P(),
    )
    out_specs = (P("pas", "head"), P("pas", "head"), P("pas", "head"), P("pas", "head"))
    return jax.shard_map(body, mesh=mesh, in_specs=in_specs, out_specs=out_specs, check_vma=False)
```

```python
import functools

import jax
import jax.numpy as jnp
from jax import lax
from jax.experimental import pallas as pl
from jax.experimental.pallas import tpu as pltpu
from jax.sharding import PartitionSpec as P

HEAD_DIM = 64
PLEN = 256
INNER = 4
GROUP = 8
PIECES = 8
SIZES = (6, 7)
LANES = 128
NEG_LARGE = -1e30
SCALE = HEAD_DIM ** (-0.5)

BF16 = jnp.bfloat16
F32 = jnp.float32

VMEM_LIMIT = 56 * 1024 * 1024


def params(semantics=None):
    return pltpu.CompilerParams(vmem_limit_bytes=VMEM_LIMIT, dimension_semantics=semantics)


def dot_nt(a, b):
    return lax.dot_general(a, b, (((1,), (1,)), ((), ())), preferred_element_type=F32)


def dot_nn(a, b):
    return lax.dot_general(a, b, (((1,), (0,)), ((), ())), preferred_element_type=F32)


def dot_tn(a, b):
    return lax.dot_general(a, b, (((0,), (0,)), ((), ())), preferred_element_type=F32)


def cost_us(time):
    return pl.CostEstimate(flops=int(time * 1e9), bytes_accessed=0, transcendentals=0)


def project_kernel(x_ref, w_hbm, o_ref, w_ref, acc, sems):
    width = o_ref.shape[2]
    pieces = sems.shape[0]
    depth = w_ref.shape[0] // pieces

    def piece(at):
        part = pl.ds(at * depth, depth)
        return pltpu.make_async_copy(w_hbm.at[part], w_ref.at[part], sems.at[at])

    @pl.when(pl.program_id(0) == 0)
    def _():
        for at in range(pieces):
            piece(at).start()
        for at in range(pieces):
            piece(at).wait()
            part = slice(at * depth, (at + 1) * depth)
            for block in range(INNER):
                cols = slice(block * width, (block + 1) * width)
                product = dot_nn(x_ref[:, part], w_ref[part, cols])
                if at == 0:
                    acc[:, cols] = product
                elif at < pieces - 1:
                    acc[:, cols] += product
                else:
                    o_ref[block] = (acc[:, cols] + product).astype(BF16)

    @pl.when(pl.program_id(0) > 0)
    def _():
        for block in range(INNER):
            cols = slice(block * width, (block + 1) * width)
            o_ref[block] = dot_nn(x_ref[...], w_ref[:, cols]).astype(BF16)


def project(x, w):
    rows, depth = x.shape
    cols = w.shape[1]
    tile = 256
    return pl.pallas_call(
        project_kernel,
        grid=(rows // tile,),
        in_specs=[
            pl.BlockSpec((tile, depth), lambda m: (m, 0)),
            pl.BlockSpec(memory_space=pl.ANY),
        ],
        out_specs=pl.BlockSpec((INNER, tile, cols // INNER), lambda m: (0, m, 0)),
        out_shape=jax.ShapeDtypeStruct((INNER, rows, cols // INNER), BF16),
        scratch_shapes=[
            pltpu.VMEM((depth, cols), BF16),
            pltpu.VMEM((tile, cols), F32),
            pltpu.SemaphoreType.DMA((PIECES,)),
        ],
        compiler_params=params(("arbitrary",)),
        cost_estimate=cost_us(14),
        name="project",
    )(x, w)


def two_heads(block):
    lane = lax.broadcasted_iota(jnp.int32, block.shape, 1)
    zero = jnp.zeros_like(block)
    return jnp.concatenate(
        [jnp.where(lane < HEAD_DIM, block, zero), jnp.where(lane >= HEAD_DIM, block, zero)], axis=0
    )


def two_heads_turned(block):
    turned = jnp.transpose(block)
    feat = lax.broadcasted_iota(jnp.int32, turned.shape, 0)
    zero = jnp.zeros_like(turned)
    return jnp.concatenate(
        [jnp.where(feat < HEAD_DIM, turned, zero), jnp.where(feat >= HEAD_DIM, turned, zero)], axis=1
    )


def own_blocks(full):
    rows = full.shape[1] // 2
    return jnp.concatenate([full[:HEAD_DIM, :rows], full[HEAD_DIM:, rows:]], axis=0)


def route_kernel(n_local, outer_ref, slot_ref, list_ref, count_ref, pick_ref, live_ref):
    n_q, list_len = list_ref.shape
    first_slot = outer_ref[0] * n_local

    def question(ident, carry):
        found = jnp.int32(0)
        for e in range(list_len):
            slot = slot_ref[list_ref[ident, e]] - first_slot
            here = (slot >= 0) & (slot < n_local) & (e < count_ref[ident])
            pick_ref[ident, found] = jnp.where(here, slot, 0)
            found = found + here.astype(jnp.int32)
        for e in range(GROUP):
            pick_ref[ident, found + e] = 0
        live_ref[ident] = found
        return carry

    lax.fori_loop(0, n_q, question, 0)


def each_group(pick_ref, live_ref, ident, entries, start):
    live = live_ref[ident]

    def group(first, size, carry):
        slots = [pick_ref[ident, first + j] for j in range(size)]
        return entries(carry, slots, [first + j < live for j in range(size)])

    def in_groups():
        steps = lax.div(live + (GROUP - 1), GROUP)
        return lax.fori_loop(0, steps, lambda step, carry: group(step * GROUP, GROUP, carry), start)

    def by_size(sizes):
        if not sizes:
            return in_groups()
        return lax.cond(live <= sizes[0], lambda: group(0, sizes[0], start), lambda: by_size(sizes[1:]))

    return by_size(SIZES)


def pair_lanes(pair):
    return slice(pair * LANES, (pair + 1) * LANES)


def stacked(ref, slots, pair):
    return jnp.concatenate([ref[slot, :, pair_lanes(pair)] for slot in slots], axis=0)


def beside(ref, slots, pair):
    return jnp.concatenate([ref[slot, pair_lanes(pair), :] for slot in slots], axis=1)


def shifted(scores, lives, top):
    keys = scores.shape[0] // len(lives)
    return [
        jnp.exp(scores[j * keys : (j + 1) * keys] - jnp.where(live, top, -NEG_LARGE))
        for j, live in enumerate(lives)
    ]


def stats_kernel(pick_ref, live_ref, k_ref, q_ref, o_ref, qt):
    n_q = q_ref.shape[0]
    n_pair = q_ref.shape[2] // LANES

    def question(ident, carry):
        for pair in range(n_pair):
            qt[pair] = two_heads_turned(q_ref[ident, :, pair_lanes(pair)])
        o_ref[0, ident] = jnp.full(o_ref.shape[2:], NEG_LARGE, F32)
        o_ref[1, ident] = jnp.zeros(o_ref.shape[2:], F32)

        def entries(state, slots, lives):
            for pair in range(n_pair):
                row = slice(pair, pair + 1)
                scores = [dot_nn(k_ref[slot, :, pair_lanes(pair)], qt[pair]) for slot in slots]
                old = o_ref[0, ident, row, :]
                new = old
                for j, live in enumerate(lives):
                    top = jnp.max(scores[j], axis=0, keepdims=True)
                    new = jnp.maximum(new, jnp.where(live, top, NEG_LARGE))
                add = o_ref[1, ident, row, :] * jnp.exp(old - new)
                for part, live in zip(scores, lives):
                    part = jnp.exp(part - jnp.where(live, new, -NEG_LARGE))
                    add = add + jnp.sum(part, axis=0, keepdims=True)
                o_ref[0, ident, row, :] = new
                o_ref[1, ident, row, :] = add
            return state

        each_group(pick_ref, live_ref, ident, entries, 0)
        return carry

    lax.fori_loop(0, n_q, question, 0)


def value_grad_kernel(pick_ref, live_ref, k_ref, q_ref, g_ref, st_ref, o_ref, qt, gbd, acc):
    n_q = q_ref.shape[0]
    n_pair = q_ref.shape[2] // LANES
    acc[...] = jnp.zeros_like(acc)

    def question(ident, carry):
        for pair in range(n_pair):
            qt[pair] = two_heads_turned(q_ref[ident, :, pair_lanes(pair)])
            gbd[pair] = two_heads(g_ref[ident, :, pair_lanes(pair)])

        def entries(state, slots, lives):
            for pair in range(n_pair):
                row = slice(pair, pair + 1)
                scores = dot_nn(stacked(k_ref, slots, pair), qt[pair])
                norm = st_ref[1, ident, row, :]
                probs = [
                    (part * norm).astype(BF16)
                    for part in shifted(scores, lives, st_ref[0, ident, row, :])
                ]
                term = dot_nn(jnp.concatenate(probs, axis=0), gbd[pair]).astype(BF16)
                for j, slot in enumerate(slots):
                    acc[slot, :, pair_lanes(pair)] += term[j * PLEN : (j + 1) * PLEN].astype(F32)
            return state

        each_group(pick_ref, live_ref, ident, entries, 0)
        return carry

    lax.fori_loop(0, n_q, question, 0)

    per = k_ref.shape[0] // o_ref.shape[0]

    def finish(owner, carry):
        for place in range(per):
            o_ref[owner, place * PLEN : (place + 1) * PLEN] = acc[owner * per + place].astype(BF16)
        return carry

    lax.fori_loop(0, o_ref.shape[0], finish, 0)


def turn(src_ref, dst_ref):
    def one(slot, carry):
        dst_ref[slot] = jnp.transpose(src_ref[slot])
        return carry

    lax.fori_loop(0, src_ref.shape[0], one, 0)


def context_kernel(n_outer, r, pick_ref, live_ref, outer_ref, k_ref, v_ref, q_ref, st_ref, o_ref, qt, vt):
    n_pair = q_ref.shape[2] // LANES
    first = lax.rem(outer_ref[0] + r, n_outer) * o_ref.shape[0]
    turn(v_ref, vt)

    def question(index, carry):
        ident = first + index
        for pair in range(n_pair):
            qt[pair] = two_heads_turned(q_ref[ident, :, pair_lanes(pair)])
        zero = jnp.zeros((LANES, 2 * q_ref.shape[1]), F32)

        def entries(sums, slots, lives):
            out = []
            for pair in range(n_pair):
                scores = dot_nn(stacked(k_ref, slots, pair), qt[pair])
                weights = [
                    part.astype(BF16)
                    for part in shifted(scores, lives, st_ref[0, ident, slice(pair, pair + 1), :])
                ]
                mix = dot_nn(beside(vt, slots, pair), jnp.concatenate(weights, axis=0))
                out.append(sums[pair] + mix)
            return tuple(out)

        sums = each_group(pick_ref, live_ref, ident, entries, (zero,) * n_pair)
        for pair in range(n_pair):
            o_ref[index, pair_lanes(pair), :] = own_blocks(sums[pair])
        return carry

    lax.fori_loop(0, o_ref.shape[0], question, 0)


def score_grad_kernel(n_outer, pick_ref, live_ref, outer_ref, k_ref, v_ref, q_ref, g_ref, st_ref, *rest):
    dot_refs, rest = rest[:n_outer], rest[n_outer:]
    dk_ref, rest = rest[0], rest[1:]
    dq_refs, (qt, qbd, gt, kt, acc_k) = rest[:n_outer], rest[n_outer:]
    n_q = q_ref.shape[0]
    inner = n_q // n_outer
    n_pair = q_ref.shape[2] // LANES
    turn(k_ref, kt)
    acc_k[...] = jnp.zeros_like(acc_k)

    def question(dot_ref, dq_ref, outer, index, carry):
        ident = outer * inner + index
        for pair in range(n_pair):
            qbd[pair] = two_heads(q_ref[ident, :, pair_lanes(pair)])
            qt[pair] = two_heads_turned(q_ref[ident, :, pair_lanes(pair)])
            gt[pair] = two_heads_turned(g_ref[ident, :, pair_lanes(pair)])
        zero = jnp.zeros((LANES, 2 * q_ref.shape[1]), F32)

        def entries(sums, slots, lives):
            out = []
            for pair in range(n_pair):
                row = slice(pair, pair + 1)
                scores = dot_nn(stacked(k_ref, slots, pair), qt[pair])
                dprob = dot_nn(stacked(v_ref, slots, pair), gt[pair])
                norm = st_ref[1, ident, row, :]
                dots = dot_ref[index, row, :]
                dscore = [
                    (part * norm * (dprob[j * PLEN : (j + 1) * PLEN] - dots)).astype(BF16)
                    for j, part in enumerate(shifted(scores, lives, st_ref[0, ident, row, :]))
                ]
                dscore = jnp.concatenate(dscore, axis=0)
                term = dot_nn(dscore, qbd[pair]).astype(BF16)
                for j, slot in enumerate(slots):
                    acc_k[slot, :, pair_lanes(pair)] += term[j * PLEN : (j + 1) * PLEN].astype(F32)
                out.append(sums[pair] + dot_nn(beside(kt, slots, pair), dscore))
            return tuple(out)

        sums = each_group(pick_ref, live_ref, ident, entries, (zero,) * n_pair)
        for pair in range(n_pair):
            dq_ref[index, pair_lanes(pair), :] = own_blocks(sums[pair])
        return carry

    for r in reversed(range(n_outer)):
        outer = lax.rem(outer_ref[0] + r, n_outer)
        lax.fori_loop(0, inner, functools.partial(question, dot_refs[r], dq_refs[r], outer), 0)

    def finish(slot, carry):
        dk_ref[slot] = acc_k[slot].astype(BF16)
        return carry

    lax.fori_loop(0, k_ref.shape[0], finish, 0)


def merge_kernel(n_outer, *refs):
    parts, o_ref = refs[:n_outer], refs[n_outer]
    top = parts[0][0]
    for part in parts[1:]:
        top = jnp.maximum(top, part[0])
    total = parts[0][1] * jnp.exp(parts[0][0] - top)
    for part in parts[1:]:
        total = total + part[1] * jnp.exp(part[0] - top)
    o_ref[0] = top
    o_ref[1] = 1.0 / total
    o_ref[2] = total


def combine_context_kernel(n_parts, outer_ref, *refs):
    parts, (st_ref, g_ref, _, o_ref, dot_ref, ctx_ref, sem) = refs[:n_parts], refs[n_parts:]
    width = g_ref.shape[2]
    inner, rows = ctx_ref.shape[0], ctx_ref.shape[1]
    first = outer_ref[0] * inner
    for q in range(inner):
        mix = parts[0][q]
        for part in parts[1:]:
            mix = mix + part[q]
        grad = jnp.transpose(g_ref[first + q].astype(F32))
        pieces = []
        for head in range(width // HEAD_DIM):
            feats = slice(head * HEAD_DIM, (head + 1) * HEAD_DIM)
            pair, lanes = head // 2, slice((head % 2) * rows, (head % 2 + 1) * rows)
            total = st_ref[2, first + q, pair : pair + 1, lanes]
            ctx = (mix[feats] / total).astype(BF16).astype(F32)
            dot_ref[q, pair : pair + 1, lanes] = jnp.sum(grad[feats] * ctx, axis=0, keepdims=True)
            pieces.append(ctx)
        ctx_ref[q] = jnp.transpose(jnp.concatenate(pieces, axis=0)).astype(BF16)
    copy = pltpu.make_async_copy(ctx_ref, o_ref.at[:, pl.ds(o_ref.shape[1] - rows, rows), :], sem)
    copy.start()
    copy.wait()


def combine_query_kernel(n_parts, place_ref, *refs):
    parts, o_refs = refs[:n_parts], refs[n_parts:]
    for r, o_ref in enumerate(o_refs):
        q = lax.rem(place_ref[0] + r, len(o_refs))
        mix = parts[0][q]
        for part in parts[1:]:
            mix = mix + part[q]
        o_ref[...] = jnp.transpose(mix * SCALE).astype(BF16)


def gather_query_kernel(place_ref, *refs):
    blocks, o_ref = refs[:-1], refs[-1]
    width = blocks[0].shape[1]
    for r, block in enumerate(blocks):
        source = lax.rem(place_ref[0] + len(blocks) - r, len(blocks))
        o_ref[:, pl.ds(pl.multiple_of(source * width, LANES), width)] = block[...]


def spread_kernel(x_ref, o_ref):
    width = o_ref.shape[2]
    for block in range(INNER):
        part = x_ref[:, block * width : (block + 1) * width] * jnp.asarray(SCALE, BF16)
        for outer in range(o_ref.shape[0] // INNER):
            o_ref[outer * INNER + block] = part


def context_grad_kernel(x_ref, w_ref, o_ref):
    part = dot_nt(x_ref[...], w_ref[...]).astype(BF16)
    for outer in range(o_ref.shape[0]):
        o_ref[outer, 0] = part


def context_grad_blocks(x, w, n_outer, width):
    rows, depth = x.shape
    return pl.pallas_call(
        context_grad_kernel,
        grid=(INNER,),
        in_specs=[
            pl.BlockSpec((rows, depth), lambda j: (0, 0)),
            pl.BlockSpec((width, depth), lambda j: (j, 0)),
        ],
        out_specs=pl.BlockSpec((n_outer, 1, rows, width), lambda j: (0, j, 0, 0)),
        out_shape=jax.ShapeDtypeStruct((n_outer, INNER, rows, width), BF16),
        compiler_params=params(("arbitrary",)),
        cost_estimate=cost_us(5),
        name="context_grad",
    )(x, w)


def out_project_kernel(x_ref, w_ref, o_ref):
    step = pl.program_id(0)
    part = dot_nn(x_ref[0], w_ref[...])

    @pl.when(step == 0)
    def _():
        o_ref[...] = part

    @pl.when(step > 0)
    def _():
        o_ref[...] += part


def out_project(x, rows, w):
    blocks, length, width = x.shape
    cols = w.shape[1]
    return pl.pallas_call(
        out_project_kernel,
        grid=(blocks,),
        in_specs=[
            pl.BlockSpec((1, rows, width), lambda j: (j, length // rows - 1, 0)),
            pl.BlockSpec((width, cols), lambda j: (j, 0)),
        ],
        out_specs=pl.BlockSpec((rows, cols), lambda j: (0, 0)),
        out_shape=jax.ShapeDtypeStruct((rows, cols), F32),
        compiler_params=params(("arbitrary",)),
        cost_estimate=cost_us(1),
        name="out_project",
    )(x, w)


def collect_kernel(x_ref, o_ref):
    width = x_ref.shape[2]
    for block in range(x_ref.shape[0]):
        o_ref[:, block * width : (block + 1) * width] = x_ref[block]


def collect(x, rows):
    blocks, _, width = x.shape
    tile = min(rows, 512)
    return pl.pallas_call(
        collect_kernel,
        grid=(rows // tile,),
        in_specs=[pl.BlockSpec((blocks, tile, width), lambda m: (0, m, 0))],
        out_specs=pl.BlockSpec((tile, blocks * width), lambda m: (m, 0)),
        out_shape=jax.ShapeDtypeStruct((rows, blocks * width), x.dtype),
        compiler_params=params(("arbitrary",)),
        cost_estimate=cost_us(1),
        name="collect",
    )(x)


def vmem_call(kernel, scalars, arrays, out_shape, scratch, time, name):
    smem = pl.BlockSpec(memory_space=pltpu.SMEM)
    vmem = pl.BlockSpec(memory_space=pltpu.VMEM)
    return pl.pallas_call(
        kernel,
        in_specs=[smem] * len(scalars) + [vmem] * len(arrays),
        out_specs=jax.tree.map(lambda _: vmem, out_shape),
        out_shape=out_shape,
        scratch_shapes=scratch,
        compiler_params=params(),
        cost_estimate=cost_us(time),
        name=name,
    )(*scalars, *arrays)


def route(outer, slot_of, passage_lists, list_counts, n_local):
    smem = pl.BlockSpec(memory_space=pltpu.SMEM)
    n_q, list_len = passage_lists.shape
    return pl.pallas_call(
        functools.partial(route_kernel, n_local),
        in_specs=[smem] * 4,
        out_specs=(smem, smem),
        out_shape=(
            jax.ShapeDtypeStruct((n_q, list_len + GROUP), jnp.int32),
            jax.ShapeDtypeStruct((n_q,), jnp.int32),
        ),
        cost_estimate=cost_us(3),
        name="route",
    )(outer, slot_of, passage_lists, list_counts)


def after(value, *others):
    return lax.optimization_barrier((value,) + others)[0]


def body(
    queries,
    encoded,
    key_weight,
    value_weight,
    out_weight,
    out_grad,
    slot_of,
    passage_lists,
    list_counts,
):
    head_width = key_weight.shape[1]
    rows = queries.shape[0]
    tok_local = encoded.shape[0]
    n_pas = lax.axis_size("pas")
    inner = INNER
    n_outer = n_pas // inner
    width = head_width // inner
    n_pair = width // LANES
    n_local = inner * (tok_local // PLEN)
    n_q = n_pas
    outer = (lax.axis_index("pas") // inner).astype(jnp.int32).reshape(1)
    groups = [[o * inner + i for i in range(inner)] for o in range(n_outer)]
    sds = jax.ShapeDtypeStruct

    def swap(x):
        return lax.all_to_all(
            x, "pas", split_axis=0, concat_axis=0, tiled=True, axis_index_groups=groups
        )

    def swap_all(x):
        return lax.all_to_all(x, "pas", split_axis=0, concat_axis=0, tiled=True)

    def to_outer(x, r):
        return lax.ppermute(
            x,
            "pas",
            [(o * inner + i, ((o + r) % n_outer) * inner + i) for o in range(n_outer) for i in range(inner)],
        )

    def partials(parts):
        return [parts[0]] + [to_outer(parts[r], r) for r in range(1, n_outer)]

    q_spread = vmem_call(spread_kernel, (), (queries,), sds((n_q, rows, width), BF16), [], 1.5, "spread")
    q_all = swap_all(q_spread)
    grad_rows = lax.all_gather(out_grad, "head", axis=1, tiled=True)

    key_part = project(after(encoded, q_spread), key_weight)
    keys = swap(key_part).reshape(n_local, PLEN, width)
    value_part = project(after(encoded, key_part, grad_rows), value_weight)
    g_spread = context_grad_blocks(after(grad_rows, value_part), out_weight, n_outer, width)
    g_spread = g_spread.reshape(n_q, rows, width)
    pick, live = route(after(outer, value_part), slot_of, passage_lists, list_counts, n_local)
    values = swap(after(value_part, g_spread, pick)).reshape(n_local, PLEN, width)

    pair_scratch = pltpu.VMEM((n_pair, 2 * rows, LANES), BF16)
    turned_pair = pltpu.VMEM((n_pair, LANES, 2 * rows), BF16)
    acc_scratch = pltpu.VMEM((n_local, PLEN, width), F32)
    turned = pltpu.VMEM((n_local, width, PLEN), BF16)
    stat_shape = (n_q, n_pair, 2 * rows)
    mix_shape = sds((inner, width, rows), F32)

    stats = vmem_call(
        stats_kernel,
        (pick, live),
        (keys, q_all),
        sds((2,) + stat_shape, F32),
        [turned_pair],
        13,
        "stats",
    )
    norm = vmem_call(
        functools.partial(merge_kernel, n_outer),
        (),
        [stats] + [to_outer(stats, r) for r in range(1, n_outer)],
        sds((3,) + stat_shape, F32),
        [],
        1,
        "merge",
    )
    g_all = swap_all(after(g_spread, values))
    mixes, norm_then = [None] * n_outer, norm
    for r in reversed(range(n_outer)):
        mixes[r] = vmem_call(
            functools.partial(context_kernel, n_outer, r),
            (pick, live, outer),
            (keys, values, q_all, norm_then),
            mix_shape,
            [turned_pair, turned],
            5 if r == 0 else 14,
            "context",
        )
        norm_then = after(norm, mixes[r], g_all)
    value_done = vmem_call(
        value_grad_kernel,
        (pick, live),
        (keys, q_all, g_all, norm_then),
        sds((inner, tok_local + rows, width), BF16),
        [turned_pair, pair_scratch, acc_scratch],
        5,
        "value_grad",
    )
    smem, vmem = pl.BlockSpec(memory_space=pltpu.SMEM), pl.BlockSpec(memory_space=pltpu.VMEM)
    anywhere = pl.BlockSpec(memory_space=pl.ANY)
    packed, grad_dot = pl.pallas_call(
        functools.partial(combine_context_kernel, n_outer),
        in_specs=[smem] + [vmem] * (n_outer + 2) + [anywhere],
        out_specs=(anywhere, vmem),
        out_shape=(
            sds((inner, tok_local + rows, width), BF16),
            sds((inner, n_pair, 2 * rows), F32),
        ),
        scratch_shapes=[pltpu.VMEM((inner, rows, width), BF16), pltpu.SemaphoreType.DMA],
        input_output_aliases={n_outer + 3: 0},
        compiler_params=params(),
        cost_estimate=cost_us(3),
        name="combine_context",
    )(outer, *partials([after(mix, g_all) for mix in mixes]), norm, g_all, value_done)
    dots = [grad_dot] + [to_outer(grad_dot, n_outer - r) for r in range(1, n_outer)]
    packed_back = swap(after(packed, *dots[1:]))
    done = vmem_call(
        functools.partial(score_grad_kernel, n_outer),
        (pick, live, outer),
        [keys, values, q_all, g_all, norm] + dots,
        (sds((n_local, PLEN, width), BF16),) + (mix_shape,) * n_outer,
        [turned_pair, pair_scratch, turned_pair, turned, acc_scratch],
        25,
        "score_grad",
    )
    projected = out_project(after(packed_back, done[0]), rows, out_weight)
    value_grad = collect(after(packed_back, projected), tok_local)
    output = lax.psum_scatter(projected, "head", scatter_dimension=1, tiled=True).astype(BF16)
    key_back = swap(after(done[0], packed_back).reshape(inner, tok_local, width))
    place = (lax.axis_index("pas") % inner).astype(jnp.int32).reshape(1)
    query_blocks = vmem_call(
        functools.partial(combine_query_kernel, n_outer),
        (place,),
        [after(done[1], value_grad)] + partials(done[1:])[1:],
        (sds((rows, width), BF16),) * inner,
        [],
        40,
        "combine_query",
    )
    arrived = [query_blocks[0]] + [
        lax.ppermute(
            query_blocks[r],
            "pas",
            [(o * inner + i, o * inner + (i + r) % inner) for o in range(n_outer) for i in range(inner)],
        )
        for r in range(1, inner)
    ]
    query_grad = vmem_call(
        gather_query_kernel, (place,), arrived, sds((rows, head_width), BF16), [], 30, "gather_query"
    )
    key_grad = collect(key_back, tok_local)
    return (output, query_grad, key_grad, value_grad)


def solution(mesh):
    in_specs = (
        P("pas", "head"),
        P("pas", None),
        P(None, "head"),
        P(None, "head"),
        P("head", None),
        P("pas", "head"),
        P(),
        P(),
        P(),
    )
    out_specs = (P("pas", "head"), P("pas", "head"), P("pas", "head"), P("pas", "head"))
    return jax.shard_map(body, mesh=mesh, in_specs=in_specs, out_specs=out_specs, check_vma=False)
```
